256 devices in a mesh: tm: 32 (over z, y), freq: 8 (over x, core).
Axes of the slice: x: 4, y: 4, z: 8, core: 2. Of those that a mesh axis runs over, the one named last changes fastest.
Arguments:
- spectrum: bfloat16 [256, 1024, 256], P('tm', 'freq'), may hold values from -6 to 6
- conv_weight: bfloat16 [2, 3, 3, 128, 128], replicated, may hold values from -0.125 to 0.125
- qkv_weight: bfloat16 [256, 1536], replicated, may hold values from -0.375 to 0.375
- out_weight: bfloat16 [512, 256], replicated, may hold values from -1.5 to 1.5
- cotangent: bfloat16 [256, 1024, 256], P(('tm', 'freq')), may hold values from -6 to 6
Outputs:
- enhanced: bfloat16 [256, 1024, 256], P(('tm', 'freq'))
- grad_spectrum: bfloat16 [256, 1024, 256], P('tm', 'freq')
- grad_conv: float32 [294912], P(('tm', 'freq'))
- grad_qkv: float32 [393216], P(('tm', 'freq'))
- grad_out: float32 [131072], P(('tm', 'freq'))
The draws below stay inside these ranges and needn't reach their ends.
All inputs are finite; a program needn't handle non-finite values.
Results may differ from the reference program's by a relative error of at most 0.014.
Values may be sent and summed in bfloat16 or wider, within the bound.
No kernel may reach another device: no remote copies, remote signals or barrier semaphores. Data moves between devices by JAX's collectives and lax.ppermute only.
A program may use at most 128 MiB of HBM per device.

```python
import math
import jax
import jax.numpy as jnp
from jax import lax

C = 128
HEADS = 4
HEAD = 128
BINS = 1024
FRAMES = 256


def block_levels(rng, extent, shards, least, high):
    factor_of = 1.0
    for dim, shards_of in shards:
        draws = jax.random.uniform(jax.random.fold_in(jax.random.fold_in(rng, 6), dim), (shards_of,), jnp.float32, least / len(shards), high / len(shards))
        factor_of = factor_of * jnp.repeat(jnp.exp(draws), extent[dim] // shards_of).reshape((-1,) + (1,) * (len(extent) - 1 - dim))
    return factor_of


def normal_values(key, dims, scale, bound, shards=(), held_as=jnp.bfloat16):
    level = block_levels(key, dims, shards, -0.22, 0.18) if shards else 1.0
    result = jax.random.normal(key, dims, jnp.float32) * scale * level
    return jnp.minimum(jnp.maximum(result, -bound), bound).astype(held_as)


def setup_inputs(seed: int = 0) -> dict:
    key_list = jax.random.split(jax.random.key(seed), 6)
    return {
        "spectrum": normal_values(key_list[0], (FRAMES, BINS, 2 * C), 1.0, 6.0, ((0, 32), (1, 8))),
        "conv_weight": normal_values(key_list[1], (2, 3, 3, C, C), (18 * C) ** -0.5, 0.125),
        "qkv_weight": normal_values(key_list[2], (2 * C, 3 * HEADS * HEAD), (2 * C) ** -0.5, 0.375),
        "out_weight": normal_values(key_list[3], (HEADS * HEAD, 2 * C), 0.25, 1.5),
        "cotangent": normal_values(key_list[4], (FRAMES, BINS, 2 * C), 1.0, 6.0, ((0, 256),)),
    }


def block_matrix(conv_weight):
    real_part = conv_weight[0]
    imag_part = conv_weight[1]
    upper_half = jnp.concatenate([real_part, imag_part], axis=-1)
    lower_half = jnp.concatenate([-imag_part, real_part], axis=-1)
    return jnp.concatenate([upper_half, lower_half], axis=-2)

def head_pass(parts):
    queries, key_rows, values, grad_attn = parts
    factor = 1.0 / math.sqrt(queries.shape[-1])
    scores = jnp.dot(queries, key_rows.T, preferred_element_type=jnp.float32) * factor
    raised = jnp.exp(scores)
    probs_f = raised / lax.optimization_barrier(jnp.sum(raised, axis=-1, keepdims=True))
    probs_b = probs_f.astype(jnp.bfloat16)
    attended = jnp.dot(probs_b, values, preferred_element_type=jnp.float32).astype(jnp.bfloat16)
    grad_probs = jnp.dot(grad_attn, values.T, preferred_element_type=jnp.float32)
    grad_values = jnp.dot(probs_b.T, grad_attn, preferred_element_type=jnp.float32).astype(jnp.bfloat16)
    row_inner = lax.optimization_barrier(jnp.sum(grad_probs * probs_f, axis=-1, keepdims=True))
    grad_scores = (probs_f * (grad_probs - row_inner) * factor).astype(jnp.bfloat16)
    grad_queries = jnp.dot(grad_scores, key_rows, preferred_element_type=jnp.float32).astype(jnp.bfloat16)
    grad_keys = jnp.dot(grad_scores.T, queries, preferred_element_type=jnp.float32).astype(jnp.bfloat16)
    return (attended, grad_queries, grad_keys, grad_values)

def frame_pass(hidden, cotangent, qkv_weight, out_weight):
    bin_count = hidden.shape[0]
    hidden_f = hidden.astype(jnp.float32)
    inv_rms = lax.rsqrt(lax.optimization_barrier(jnp.mean(hidden_f * hidden_f, axis=-1, keepdims=True)) + 1e-06)
    normed_f = hidden_f * inv_rms
    normed = normed_f.astype(jnp.bfloat16)
    qkv = jnp.dot(normed, qkv_weight, preferred_element_type=jnp.float32).astype(jnp.bfloat16)
    grad_attn = jnp.dot(cotangent, out_weight.T, preferred_element_type=jnp.float32).astype(jnp.bfloat16)
    split_qkv = qkv.reshape(bin_count, 3, HEADS, -1).transpose(1, 2, 0, 3)
    grad_split = grad_attn.reshape(bin_count, HEADS, -1).transpose(1, 0, 2)
    attended, grad_q, grad_k, grad_v = lax.map(head_pass, (split_qkv[0], split_qkv[1], split_qkv[2], grad_split))
    attended = attended.transpose(1, 0, 2).reshape(bin_count, -1)
    grad_cells = jnp.stack([grad_q, grad_k, grad_v]).transpose(2, 0, 1, 3).reshape(bin_count, -1)
    enhanced = (hidden_f + jnp.dot(attended, out_weight, preferred_element_type=jnp.float32)).astype(jnp.bfloat16)
    grad_normed = jnp.dot(grad_cells, qkv_weight.T, preferred_element_type=jnp.float32)
    mixing = lax.optimization_barrier(jnp.mean(grad_normed * normed_f, axis=-1, keepdims=True))
    grad_hidden = (cotangent.astype(jnp.float32) + inv_rms * (grad_normed - normed_f * mixing)).astype(jnp.bfloat16)
    grad_out = jnp.dot(attended.T, cotangent, preferred_element_type=jnp.float32)
    grad_qkv = jnp.dot(normed.T, grad_cells, preferred_element_type=jnp.float32)
    return (enhanced, grad_hidden, grad_qkv, grad_out)

def attend_frames(hidden, cotangent, qkv_weight, out_weight):
    zero_sums = (jnp.zeros(qkv_weight.shape, jnp.float32), jnp.zeros(out_weight.shape, jnp.float32))

    def frame_step(running, frame_items):
        enhanced, grad_hidden, grad_qkv, grad_out = frame_pass(frame_items[0], frame_items[1], qkv_weight, out_weight)
        return ((running[0] + grad_qkv, running[1] + grad_out), (enhanced, grad_hidden))
    summed, results = lax.scan(frame_step, zero_sums, (hidden, cotangent))
    return (results[0], results[1], summed[0], summed[1])

def reference(spectrum, conv_weight, qkv_weight, out_weight, cotangent):
    block_weight = block_matrix(conv_weight)
    frame_count, bin_count, width = spectrum.shape
    padded = jnp.pad(spectrum, ((1, 1), (1, 1), (0, 0)))
    conv = jnp.zeros((frame_count, bin_count, width), jnp.float32)
    for row_tap in range(3):
        for col_tap in range(3):
            window = padded[row_tap:row_tap + frame_count, col_tap:col_tap + bin_count]
            conv = conv + jnp.dot(window, block_weight[row_tap, col_tap], preferred_element_type=jnp.float32)
    hidden = (spectrum.astype(jnp.float32) + jax.nn.silu(conv)).astype(jnp.bfloat16)
    enhanced, grad_hidden, grad_qkv_sum, grad_out_sum = attend_frames(hidden, cotangent, qkv_weight, out_weight)
    sigma = jax.nn.sigmoid(conv)
    grad_conv_out = (grad_hidden.astype(jnp.float32) * sigma * (1.0 + conv * (1.0 - sigma))).astype(jnp.bfloat16)
    grad_padded = jnp.pad(grad_conv_out, ((1, 1), (1, 1), (0, 0)))
    grad_input = grad_hidden.astype(jnp.float32)
    grad_flat = grad_conv_out.reshape(-1, width)
    tap_grads = []
    for row_tap in range(3):
        for col_tap in range(3):
            back_window = grad_padded[2 - row_tap:2 - row_tap + frame_count, 2 - col_tap:2 - col_tap + bin_count]
            grad_input = grad_input + jnp.dot(back_window, block_weight[row_tap, col_tap].T, preferred_element_type=jnp.float32)
            window = padded[row_tap:row_tap + frame_count, col_tap:col_tap + bin_count]
            tap_grads.append(jnp.dot(window.reshape(-1, width).T, grad_flat, preferred_element_type=jnp.float32))
    grad_block = jnp.stack(tap_grads).reshape(3, 3, width, width)
    chans = width // 2
    grad_real = grad_block[:, :, :chans, :chans] + grad_block[:, :, chans:, chans:]
    grad_imag = grad_block[:, :, :chans, chans:] - grad_block[:, :, chans:, :chans]
    norm_factor = 1.0 / math.sqrt(FRAMES * BINS)
    grad_conv = (jnp.stack([grad_real, grad_imag]) * norm_factor).reshape(-1)
    return (enhanced, grad_input.astype(jnp.bfloat16), grad_conv, (grad_qkv_sum * norm_factor).reshape(-1), (grad_out_sum * norm_factor).reshape(-1))
```

```python
import functools
import math

import jax
import jax.numpy as jnp
from jax import lax
from jax.experimental import pallas as pl
from jax.experimental.pallas import tpu as pltpu
from jax.sharding import PartitionSpec as P

HEADS = 4
HEAD = 128
BF = jnp.bfloat16
F32 = jnp.float32
NN = (((1,), (0,)), ((), ()))
NT = (((1,), (1,)), ((), ()))
TN = (((0,), (0,)), ((), ()))
QUERY_BLOCK = 512


def mm(a, b, dims=NN):
    return lax.dot_general(a, b, dims, preferred_element_type=F32)


def vmem_call(body, out_shape, scratch, name, cost, limit=48):
    def run(*args):
        return pl.pallas_call(
            body,
            out_shape=out_shape,
            in_specs=[pl.BlockSpec(memory_space=pltpu.VMEM)] * len(args),
            out_specs=jax.tree.map(lambda _: pl.BlockSpec(memory_space=pltpu.VMEM), out_shape),
            scratch_shapes=scratch,
            compiler_params=pltpu.CompilerParams(vmem_limit_bytes=limit * 2**20),
            cost_estimate=pl.CostEstimate(flops=cost[0], bytes_accessed=cost[1], transcendentals=0),
            name=name,
        )(*args)

    return run


def shape(dims, kind=BF):
    return jax.ShapeDtypeStruct(dims, kind)


def shifted(mid, up, down, left, right):
    rows = jnp.concatenate([up, mid, down], axis=0)
    wide = rows.astype(F32)
    bins = wide.shape[1]
    at = lax.broadcasted_iota(jnp.int32, wide.shape, 1)
    before = jnp.where(at == 0, left.astype(F32), pltpu.roll(wide, 1, 1)).astype(BF)
    after = jnp.where(at == bins - 1, right.astype(F32), pltpu.roll(wide, bins - 1, 1)).astype(BF)
    return before, rows, after


def conv_forward_body(mid, up, down, left, right, weight, hidden, slope, stacked, matrix):
    frames, bins, width = mid.shape
    half = width // 2
    before, rows, after = shifted(mid[...], up[...], down[...], left[...], right[...])
    stacked[:, :, :width] = before
    stacked[:, :, width : 2 * width] = rows
    stacked[:, :, 2 * width :] = after
    conv = None
    for i in range(3):
        for j in range(3):
            real, imag = weight[0, i, j], weight[1, i, j]
            at = j * width
            matrix[i, at : at + half, :half] = real
            matrix[i, at : at + half, half:] = imag
            matrix[i, at + half : at + width, :half] = -imag
            matrix[i, at + half : at + width, half:] = real
        part = mm(stacked[i : i + frames].reshape(frames * bins, 3 * width), matrix[i])
        conv = part if conv is None else conv + part
    sigma = 1.0 / (1.0 + jnp.exp(-conv))
    hidden[...] = (mid[...].reshape(frames * bins, width).astype(F32) + conv * sigma).astype(BF)
    slope[...] = sigma * (1.0 + conv * (1.0 - sigma))


def conv_weight_body(frames, grad_hidden, slope, stacked, grad_conv_out, grad_weight):
    _, bins, triple = stacked.shape
    width = triple // 3
    half = width // 2
    cells = frames * bins
    grad = (grad_hidden[...].reshape(cells, width).astype(F32) * slope[...]).astype(BF)
    grad_conv_out[...] = grad.reshape(frames, bins, width)
    flipped = grad.T
    for i in range(3):
        block = mm(flipped, stacked[i : i + frames].reshape(cells, triple))
        for j in range(3):
            at = j * width
            upper = block[:half, at : at + half] + block[half:, at + half : at + width]
            lower = block[half:, at : at + half] - block[:half, at + half : at + width]
            grad_weight[0, i, j] = upper.T * (1.0 / 512)
            grad_weight[1, i, j] = lower.T * (1.0 / 512)


def conv_data_body(mid, up, down, left, right, weight, grad_hidden, out, stacked, matrix):
    frames, bins, width = mid.shape
    half = width // 2
    before, rows, after = shifted(mid[...], up[...], down[...], left[...], right[...])
    stacked[:, :, :width] = after
    stacked[:, :, width : 2 * width] = rows
    stacked[:, :, 2 * width :] = before
    total = grad_hidden[...].reshape(frames * bins, width).astype(F32)
    for i in range(3):
        for j in range(3):
            real, imag = weight[0, i, j], weight[1, i, j]
            at = j * width
            matrix[i, :half, at : at + half] = real
            matrix[i, :half, at + half : at + width] = imag
            matrix[i, half:, at : at + half] = -imag
            matrix[i, half:, at + half : at + width] = real
        rows_at = 2 - i
        total = total + mm(
            stacked[rows_at : rows_at + frames].reshape(frames * bins, 3 * width), matrix[i], NT
        )
    out[...] = total.astype(BF).reshape(frames, bins, width)


def attend_body(
    hidden, cotangent, qkv_w, out_w, enhanced, grad_hidden, grad_qkv, grad_out,
    qkv, grad_att, attended, grad_cells, sum_keys, sum_values,
):
    cells = hidden.shape[0]
    wide = HEADS * HEAD
    log2e = math.log2(math.e)
    factor = 1.0 / math.sqrt(HEAD)
    hidden_f = hidden[...].astype(F32)
    inv_rms = lax.rsqrt(jnp.mean(hidden_f * hidden_f, axis=-1, keepdims=True) + 1e-6)
    normed = (hidden_f * inv_rms).astype(BF)
    qkv[:, :wide] = (mm(normed, qkv_w[:, :wide]) * (factor * log2e)).astype(BF)
    qkv[:, wide:] = mm(normed, qkv_w[:, wide:]).astype(BF)
    grad_att[...] = mm(cotangent[...], out_w[...], NT).astype(BF)
    ones = jnp.ones((cells, HEAD), BF)

    def columns(part, h):
        return pl.ds(pl.multiple_of(part * wide + h * HEAD, HEAD), HEAD)

    def head(h, carry):
        keys = qkv[:, columns(1, h)]
        values = qkv[:, columns(2, h)]
        values_ones = jnp.concatenate([values, ones], axis=1)
        for block in range(cells // QUERY_BLOCK):
            rows = slice(block * QUERY_BLOCK, (block + 1) * QUERY_BLOCK)
            queries = qkv[rows, columns(0, h)]
            scores = mm(queries, keys, NT)
            raised = jnp.exp2(scores - jnp.max(scores, axis=-1, keepdims=True))
            raised_b = raised.astype(BF)
            sums = mm(raised_b, values_ones)
            inverse = 1.0 / sums[:, HEAD:]
            result = sums[:, :HEAD] * inverse
            attended[rows, columns(0, h)] = result.astype(BF)
            scaled = grad_att[rows, columns(0, h)].astype(F32) * inverse
            inner = jnp.sum(scaled * result, axis=-1, keepdims=True)
            scaled_b = scaled.astype(BF)
            grad_probs = mm(scaled_b, values, NT)
            grad_scores = (raised * (grad_probs - inner)).astype(BF)
            grad_cells[rows, columns(0, h)] = (mm(grad_scores, keys) * factor).astype(BF)
            new_keys = mm(queries.T, grad_scores)
            new_values = mm(scaled_b.T, raised_b)
            if block == 0:
                sum_keys[...] = new_keys
                sum_values[...] = new_values
            else:
                sum_keys[...] += new_keys
                sum_values[...] += new_values
        grad_cells[:, columns(1, h)] = (sum_keys[...] * (1.0 / log2e)).T.astype(BF)
        grad_cells[:, columns(2, h)] = sum_values[...].T.astype(BF)
        return carry

    lax.fori_loop(0, HEADS, head, 0)
    enhanced[...] = (hidden_f + mm(attended[...], out_w[...])).astype(BF)
    grad_normed = mm(grad_cells[...], qkv_w[...], NT)
    normed_f = hidden_f * inv_rms
    mixing = jnp.mean(grad_normed * normed_f, axis=-1, keepdims=True)
    grad_hidden[...] = (
        cotangent[...].astype(F32) + inv_rms * (grad_normed - normed_f * mixing)
    ).astype(BF)
    grad_qkv[...] = (mm(normed, grad_cells[...], TN) * (1.0 / 512)).astype(BF)
    grad_out[...] = (mm(attended[...], cotangent[...], TN) * (1.0 / 512)).astype(BF)


def halos(tile):
    frames, bins, _ = tile.shape
    size = lax.axis_size("tm")
    forward = [(i, i + 1) for i in range(size - 1)]
    back = [(i + 1, i) for i in range(size - 1)]
    up = lax.ppermute(tile[frames - 1 :], "tm", forward)
    down = lax.ppermute(tile[:1], "tm", back)
    size = lax.axis_size("freq")
    forward = [(i, i + 1) for i in range(size - 1)]
    back = [(i + 1, i) for i in range(size - 1)]
    last = jnp.concatenate([up[:, -1:], tile[:, -1:], down[:, -1:]], axis=0)
    first = jnp.concatenate([up[:, :1], tile[:, :1], down[:, :1]], axis=0)
    left = lax.ppermute(last, "freq", forward)
    right = lax.ppermute(first, "freq", back)
    return up, down, left, right


def reduce_share(terms):
    tm, freq = lax.axis_size("tm"), lax.axis_size("freq")
    n = terms.shape[-1]
    grouped = terms.reshape(tm, freq, n).transpose(1, 0, 2)
    came = lax.all_to_all(grouped, "freq", split_axis=0, concat_axis=0, tiled=True)
    part = jnp.sum(came.astype(F32), axis=0).astype(BF)
    part = part.reshape(tm, n // 128, 128)
    came = lax.all_to_all(part, "tm", split_axis=0, concat_axis=0, tiled=True)
    return jnp.sum(came.astype(F32), axis=0).reshape(n)


def shards(spectrum, conv_weight, qkv_weight, out_weight, cotangent):
    frames, bins, width = spectrum.shape
    cells = frames * bins
    conv_cost = (2 * 9 * cells * width * width, 6 * 2**20)
    up, down, left, right = halos(spectrum)
    hidden, slope, stacked = vmem_call(
        conv_forward_body,
        (shape((cells, width)), shape((cells, width), F32), shape((frames + 2, bins, 3 * width))),
        [pltpu.VMEM((3, 3 * width, width), BF)],
        "conv_forward",
        conv_cost,
    )(spectrum, up, down, left, right, conv_weight)
    hidden = hidden.reshape(frames, bins, width)
    frame = lax.all_to_all(hidden, "freq", split_axis=0, concat_axis=0, tiled=True)
    frame = frame.reshape(cells, width)
    wide = HEADS * HEAD
    enhanced, grad_frame, grad_qkv, grad_out = vmem_call(
        attend_body,
        (
            shape((cells, width)),
            shape((cells, width)),
            shape((width, 3 * wide)),
            shape((wide, width)),
        ),
        [
            pltpu.VMEM((cells, 3 * wide), BF),
            pltpu.VMEM((cells, wide), BF),
            pltpu.VMEM((cells, wide), BF),
            pltpu.VMEM((cells, 3 * wide), BF),
            pltpu.VMEM((HEAD, cells), F32),
            pltpu.VMEM((HEAD, cells), F32),
        ],
        "attend",
        (16 * 10**9, 6 * 2**20),
    )(frame, cotangent.reshape(cells, width), qkv_weight, out_weight)
    grad_frame = grad_frame.reshape(frames, bins, width)
    grad_hidden = lax.all_to_all(grad_frame, "freq", split_axis=0, concat_axis=0, tiled=True)
    ranks = lax.axis_size("tm") * lax.axis_size("freq")
    terms = jnp.concatenate([grad_qkv.reshape(ranks, -1), grad_out.reshape(ranks, -1)], axis=1)
    share = reduce_share(terms)
    cut = grad_qkv.size // ranks
    grad_conv_out, grad_weight = vmem_call(
        functools.partial(conv_weight_body, frames),
        (shape((frames, bins, width)), shape(conv_weight.shape, F32)),
        [],
        "conv_weight_grad",
        conv_cost,
    )(grad_hidden, slope, stacked)
    conv_share = reduce_share(grad_weight.astype(BF).reshape(ranks, -1))
    up, down, left, right = halos(grad_conv_out)
    grad_spectrum = vmem_call(
        conv_data_body,
        shape((frames, bins, width)),
        [
            pltpu.VMEM((frames + 2, bins, 3 * width), BF),
            pltpu.VMEM((3, width, 3 * width), BF),
        ],
        "conv_data_grad",
        conv_cost,
    )(grad_conv_out, up, down, left, right, conv_weight, grad_hidden)
    return (
        enhanced.reshape(1, cells, width),
        grad_spectrum,
        conv_share,
        share[:cut],
        share[cut:],
    )


def solution(mesh):
    placed = (P("tm", "freq", None), P(), P(), P(), P(("tm", "freq"), None, None))
    return jax.shard_map(
        shards,
        mesh=mesh,
        in_specs=placed,
        out_specs=(
            P(("tm", "freq"), None, None),
            P("tm", "freq", None),
            P(("tm", "freq")),
            P(("tm", "freq")),
            P(("tm", "freq")),
        ),
        check_vma=False,
    )
```

```python
import math

import jax
import jax.numpy as jnp
from jax import lax
from jax.experimental import pallas as pl
from jax.experimental.pallas import tpu as pltpu
from jax.sharding import PartitionSpec as P

HEADS = 4
HEAD = 128
EARLY = 3
EXTRA = 16
SCALE = 1.0 / 512
LOG2E = math.log2(math.e)
FACTOR = 1.0 / math.sqrt(HEAD)
BF = jnp.bfloat16
F32 = jnp.float32
NN = (((1,), (0,)), ((), ()))
NT = (((1,), (1,)), ((), ()))
QUERY_BLOCK = 512


def mm(a, b, dims=NN):
    return lax.dot_general(a, b, dims, preferred_element_type=F32)


def kernel_call(body, name, outs, *args, scratch=(), mflops=0, limit=48):
    outs = [jax.ShapeDtypeStruct(dims, kind) for dims, kind in outs]
    size = sum(a.size * a.dtype.itemsize for a in (*args, *outs))
    return pl.pallas_call(
        body,
        out_shape=outs,
        in_specs=[pl.BlockSpec(memory_space=pltpu.VMEM)] * len(args),
        out_specs=[pl.BlockSpec(memory_space=pltpu.VMEM)] * len(outs),
        scratch_shapes=list(scratch),
        compiler_params=pltpu.CompilerParams(vmem_limit_bytes=limit * 2**20),
        cost_estimate=pl.CostEstimate(
            flops=mflops * 10**6, bytes_accessed=size, transcendentals=0
        ),
        name=name,
    )(*args)


def sigmoid(v):
    return 1.0 / (1.0 + jnp.exp(-v))


def slope_of(v, sigma):
    return sigma * (1.0 + v * (1.0 - sigma))


def moved_down(rows):
    at = lax.broadcasted_iota(jnp.int32, rows.shape, 0)
    return jnp.where(at == 0, 0.0, pltpu.roll(rows, 1, 0))


def moved_up(rows):
    last = rows.shape[0] - 1
    at = lax.broadcasted_iota(jnp.int32, rows.shape, 0)
    return jnp.where(at == last, 0.0, pltpu.roll(rows, last, 0))


def with_borders(inner, first, last):
    at = lax.broadcasted_iota(jnp.int32, inner.shape, 1)
    inner = jnp.where(at == 0, first[:, None, :], inner)
    return jnp.where(at == inner.shape[1] - 1, last[:, None, :], inner)


def bins_before(rows, left):
    at = lax.broadcasted_iota(jnp.int32, rows.shape, 1)
    return jnp.where(at == 0, left, pltpu.roll(rows, 1, 1))


def bins_after(rows, right):
    last = rows.shape[1] - 1
    at = lax.broadcasted_iota(jnp.int32, rows.shape, 1)
    return jnp.where(at == last, right, pltpu.roll(rows, last, 1))


def conv_own_body(mid, weight, conv, borders, matrix, matrix_back, stacked):
    frames, bins, width = mid.shape
    half = width // 2
    wide = mid[...].astype(F32)
    stacked[:, :, :width] = bins_before(wide, 0.0).astype(BF)
    stacked[:, :, width : 2 * width] = mid[...]
    stacked[:, :, 2 * width :] = bins_after(wide, 0.0).astype(BF)
    for i in range(3):
        for j in range(3):
            real, imag = weight[0, i, j], weight[1, i, j]
            at = j * width
            matrix[i, at : at + half, :half] = real
            matrix[i, at : at + half, half:] = imag
            matrix[i, at + half : at + width, :half] = -imag
            matrix[i, at + half : at + width, half:] = real
            matrix_back[i, :half, at : at + half] = real
            matrix_back[i, :half, at + half : at + width] = imag
            matrix_back[i, half:, at : at + half] = -imag
            matrix_back[i, half:, at + half : at + width] = real
    inner = (frames - 1) * bins
    everything = stacked[...].reshape(frames * bins, 3 * width)
    conv[...] = mm(everything, matrix[1])
    conv[bins:] += mm(everything[:inner], matrix[0])
    conv[:inner] += mm(everything[bins:], matrix[2])
    borders[0] = mid[:, 0, :].astype(F32)
    borders[1] = mid[:, bins - 1, :].astype(F32)


def conv_finish_body(mid, up, down, own, borders, matrix, payload, slope, conv, pieces):
    frames, bins, width = mid.shape
    cells = frames * bins

    def stack(row):
        wide = row[...].astype(F32)
        before = bins_before(wide, 0.0).astype(BF)
        after = bins_after(wide, 0.0).astype(BF)
        return jnp.concatenate([before[0], row[0], after[0]], axis=1)

    conv[...] = own[...].reshape(frames, bins, width)
    conv[0] += mm(stack(up), matrix[0])
    conv[frames - 1] += mm(stack(down), matrix[2])

    def beyond(bin_at, side, tap):
        rows = jnp.concatenate(
            [up[:, bin_at, :].astype(F32), borders[side], down[:, bin_at, :].astype(F32)], axis=0
        )
        total = None
        for i in range(3):
            term = mm(
                rows[i : i + frames].astype(BF), matrix[i, tap * width : (tap + 1) * width, :]
            )
            total = term if total is None else total + term
        return total

    parts = (
        beyond(0, 0, 2),
        conv[:, 0, :],
        conv[:, bins - 1, :],
        beyond(bins - 1, 1, 0),
    )
    pieces[...] = jnp.zeros(pieces.shape, F32)
    for at, part in enumerate(parts):
        high = part.astype(BF).astype(F32)
        pieces[:, 2 * at, :] = high
        pieces[:, 2 * at + 1, :] = part - high
    values = conv[...]
    sigma = sigmoid(values)
    slope[...] = slope_of(values, sigma)
    hidden = mid[...].astype(F32) + values * sigma
    payload[:, :bins, :] = with_borders(hidden, borders[0], borders[1]).astype(BF)
    payload[:, bins:, :] = pieces[...].astype(BF)


def prepare_body(mid, up, down, cotangent, out_w, turned, grad_att):
    frames, bins, width = mid.shape
    turned[:, :bins] = up[0].T
    turned[:, bins : (frames + 1) * bins] = mid[...].reshape(frames * bins, width).T
    turned[:, (frames + 1) * bins :] = down[0].T
    grad_att[...] = mm(cotangent[...], out_w[...], NT).astype(BF)


def columns(part, h):
    at = part * HEADS * HEAD + h * HEAD
    if not isinstance(h, int):
        at = pl.multiple_of(at, HEAD)
    return pl.ds(at, HEAD)


def one_head(h, qkv, grad_att, attended, grad_cells, sum_keys, sum_values):
    cells = qkv.shape[0]
    keys = qkv[:, columns(1, h)]
    values = qkv[:, columns(2, h)]
    values_ones = jnp.concatenate([values, jnp.ones((cells, HEAD), BF)], axis=1)
    for block in range(cells // QUERY_BLOCK):
        rows = slice(block * QUERY_BLOCK, (block + 1) * QUERY_BLOCK)
        queries = qkv[rows, columns(0, h)]
        scores = mm(queries, keys, NT)
        raised = jnp.exp2(scores - jnp.max(scores, axis=-1, keepdims=True))
        raised_b = raised.astype(BF)
        sums = mm(raised_b, values_ones)
        inverse = 1.0 / sums[:, HEAD:]
        result = sums[:, :HEAD] * inverse
        attended[rows, columns(0, h)] = result.astype(BF)
        scaled = grad_att[rows, columns(0, h)].astype(F32) * inverse
        inner = jnp.sum(scaled * result, axis=-1, keepdims=True)
        scaled_b = scaled.astype(BF)
        grad_probs = mm(scaled_b, values, NT)
        grad_scores = (raised * (grad_probs - inner)).astype(BF)
        grad_cells[rows, columns(0, h)] = (mm(grad_scores, keys) * FACTOR).astype(BF)
        new_keys = mm(queries.T, grad_scores)
        new_values = mm(scaled_b.T, raised_b)
        if block == 0:
            sum_keys[...] = new_keys
            sum_values[...] = new_values
        else:
            sum_keys[...] += new_keys
            sum_values[...] += new_values
    grad_cells[:, columns(1, h)] = (sum_keys[...] * (1.0 / LOG2E)).T.astype(BF)
    grad_cells[:, columns(2, h)] = sum_values[...].T.astype(BF)


def normed_parts(hidden_f):
    inv_rms = lax.rsqrt(jnp.mean(hidden_f * hidden_f, axis=-1, keepdims=True) + 1e-6)
    normed_f = hidden_f * inv_rms
    return inv_rms, normed_f, normed_f.astype(BF)


def split_columns(target, at, values):
    for n in range(values.shape[1] // 128):
        target[at + n] = values[:, n * 128 : (n + 1) * 128]


def spread_rows(message, at, source, group, first, step, count):
    for f in range(message.shape[0]):
        rows = source[group, pl.ds(first(f), count, stride=step), :]
        message[f, at : at + count, :] = rows.astype(BF)


def attend_first_body(
    came, qkv_w, grad_att, cotangent, hidden, border_slope, qkv, attended, grad_cells, message,
    sum_keys, sum_values, grads, grads_out, pieces,
):
    chunks, long, width = came.shape
    bins = long - EXTRA
    wide = HEADS * HEAD
    pieces[...] = came[:, bins:, :].astype(F32)
    here_first = pieces[:, 2, :] + pieces[:, 3, :]
    here_last = pieces[:, 4, :] + pieces[:, 5, :]
    first = here_first + moved_down(pieces[:, 6, :] + pieces[:, 7, :])
    last = here_last + moved_up(pieces[:, 0, :] + pieces[:, 1, :])
    sigma_first, sigma_last = sigmoid(first), sigmoid(last)
    border_slope[0] = slope_of(first, sigma_first)
    border_slope[1] = slope_of(last, sigma_last)
    fixed_first = came[:, 0, :].astype(F32) + first * sigma_first
    fixed_last = came[:, bins - 1, :].astype(F32) + last * sigma_last
    cells = with_borders(came[:, :bins, :].astype(F32), fixed_first, fixed_last)
    hidden[...] = cells.astype(BF).reshape(chunks * bins, width)
    _, _, normed = normed_parts(hidden[...].astype(F32))
    qkv[:, :wide] = (mm(normed, qkv_w[:, :wide]) * (FACTOR * LOG2E)).astype(BF)
    qkv[:, wide:] = mm(normed, qkv_w[:, wide:]).astype(BF)

    def head(h, carry):
        one_head(h, qkv, grad_att, attended, grad_cells, sum_keys, sum_values)
        return carry

    lax.fori_loop(0, EARLY, head, 0)
    turned = normed.T
    narrow = EARLY * HEAD
    for part in range(3):
        values = mm(turned, grad_cells[:, part * wide : part * wide + narrow])
        split_columns(grads, part * EARLY, SCALE * values)
    split_columns(grads_out, 0, SCALE * mm(attended[:, :narrow].T, cotangent[...]))
    tm = width // 8
    for group in range(3 * EARLY):
        spread_rows(message, group * tm, grads, group, lambda f: f, 8, tm)
    for group in range(4):
        b, c = divmod(group, 2)
        few = tm * EARLY // HEADS
        spread_rows(
            message, 3 * EARLY * tm + group * few, grads_out, c,
            lambda f: 2 * f + b, 16, few,
        )


def attend_last_body(
    hidden, border_slope, qkv, attended_in, grad_cells_in, grad_att, cotangent, qkv_w, out_w,
    payload, enhanced, message,
    attended, grad_cells, sum_keys, sum_values, grads, grads_out, rows_f, pieces,
):
    chunks, long, width = payload.shape
    bins = long - EXTRA
    wide = HEADS * HEAD
    narrow = EARLY * HEAD
    attended[:, :narrow] = attended_in[:, :narrow]
    for part in range(3):
        cut = slice(part * wide, part * wide + narrow)
        grad_cells[:, cut] = grad_cells_in[:, cut]
    for h in range(EARLY, HEADS):
        one_head(h, qkv, grad_att, attended, grad_cells, sum_keys, sum_values)
    hidden_f = hidden[...].astype(F32)
    inv_rms, normed_f, normed = normed_parts(hidden_f)
    grad_normed = mm(grad_cells[...], qkv_w[...], NT)
    mixing = jnp.mean(grad_normed * normed_f, axis=-1, keepdims=True)
    grad = cotangent[...].astype(F32) + inv_rms * (grad_normed - normed_f * mixing)
    grad_b = grad.astype(BF).reshape(chunks, bins, width)
    payload[:, :bins, :] = grad_b
    rows_f[...] = grad_b.astype(F32)
    first = rows_f[:, 0, :] * border_slope[0]
    last = rows_f[:, bins - 1, :] * border_slope[1]
    pieces[...] = jnp.zeros(pieces.shape, F32)
    pieces[:, 0, :] = moved_down(last)
    pieces[:, 1, :] = first
    pieces[:, 2, :] = last
    pieces[:, 3, :] = moved_up(first)
    payload[:, bins:, :] = pieces[...].astype(BF)
    enhanced[...] = (hidden_f + mm(attended[...], out_w[...])).astype(BF)
    turned = normed.T
    tm = width // 8
    for part in range(3):
        split_columns(grads, part, SCALE * mm(turned, grad_cells[:, columns(part, EARLY)]))
        spread_rows(message, part * tm, grads, part, lambda f: f, 8, tm)
    split_columns(grads_out, 0, SCALE * mm(attended[:, narrow:].T, cotangent[...]))
    few = tm // HEADS
    for group in range(4):
        b, c = divmod(group, 2)
        spread_rows(
            message, 3 * tm + group * few, grads_out, c, lambda f: 2 * f + b, 16, few
        )


def stack_back(rows, left, right):
    after = bins_after(rows, right).astype(BF)
    before = bins_before(rows, left).astype(BF)
    return jnp.concatenate([after, rows.astype(BF), before], axis=-1)


def conv_weight_body(came, slope, turned, head_message, stacked, edges, message, grads, pieces):
    frames, long, width = came.shape
    bins = long - EXTRA
    half = width // 2
    cells = frames * bins
    pieces[...] = came[:, bins:, :].astype(F32)
    grad = came[:, :bins, :].astype(F32) * slope[...]
    grad = with_borders(grad, pieces[:, 1, :], pieces[:, 2, :])
    grad_b = grad.astype(BF)
    for side, frame in enumerate((0, frames - 1)):
        edges[side, :, :bins, :] = grad_b[frame : frame + 1]
        edges[side, :, bins:, :] = came[frame : frame + 1, bins:, :]
    stacked[...] = stack_back(
        grad_b.astype(F32), pieces[:, 0, :][:, None, :], pieces[:, 3, :][:, None, :]
    )
    flat = stacked[...].reshape(cells, 3 * width)
    for i in range(3):
        block = mm(turned[:, i * bins : i * bins + cells], flat)
        for j in range(3):
            at = j * width
            upper = block[:half, at : at + half] + block[half:, at + half : at + width]
            lower = block[:half, at + half : at + width] - block[half:, at : at + half]
            tap = (3 * i + j) * half
            grads[tap : tap + half] = upper * SCALE
            grads[9 * half + tap : 9 * half + tap + half] = lower * SCALE
    early = head_message.shape[1]
    message[:, :early, :] = head_message[...]
    tm = width // 8
    for f in range(8):
        for e in range(9):
            rows = grads[pl.ds(9 * f + e, tm, stride=72), :]
            message[f, early + e * tm : early + (e + 1) * tm, :] = rows.astype(BF)


def conv_data_body(came, stacked, matrix, total):
    frames, bins, triple = stacked.shape
    width = triple // 3
    inner = (frames - 1) * bins
    flat = stacked[...].reshape(frames * bins, triple)
    total[...] = came[:, :bins, :].reshape(frames * bins, width).astype(F32) + mm(
        flat, matrix[1], NT
    )
    total[:inner] += mm(flat[bins:], matrix[0], NT)
    total[bins:] += mm(flat[:inner], matrix[2], NT)


def conv_data_finish_body(total, up, down, matrix, out):
    frames, bins, width = out.shape

    def stack(edge):
        extra = edge[0, :, bins:, :].astype(F32)
        rows = edge[0, :, :bins, :].astype(F32)
        return stack_back(rows, extra[:, 0:1, :], extra[:, 3:4, :])[0]

    out[...] = total[...].reshape(frames, bins, width).astype(BF)
    out[0] = (total[:bins] + mm(stack(up), matrix[2], NT)).astype(BF)
    out[frames - 1] = (total[(frames - 1) * bins :] + mm(stack(down), matrix[0], NT)).astype(BF)


def sum_body(came, out):
    total = came[0].astype(F32)
    for source in range(1, came.shape[0]):
        total = total + came[source].astype(F32)
    out[...] = total


def regroup_body(early, came, chunk, late, rows):
    tm = chunk.shape[0]
    sum_body(came, late)
    few, more = tm // HEADS, tm * EARLY // HEADS
    base = 3 * tm + 4 * few
    rows[...] = jnp.zeros(rows.shape, F32)
    for t in range(tm):
        rows[t, 0:9, :] = late[pl.ds(base + t, 9, stride=tm), :]
        rows[t, 9:18, :] = early[pl.ds(t, 3 * EARLY, stride=tm), :]
        rows[t, 18:21, :] = late[pl.ds(t, 3, stride=tm), :]
        if t < more:
            rows[t, 21:25, :] = early[pl.ds(3 * EARLY * tm + t, 4, stride=more), :]
        else:
            rows[t, 21:25, :] = late[pl.ds(3 * tm + t - more, 4, stride=few), :]
    chunk[...] = rows[...].astype(BF)


def share_body(came, conv, qkv, out, total):
    sum_body(came, total)
    conv[...] = total[0:9]
    for part in range(3):
        qkv[4 * part : 4 * part + 3, :] = total[9 + 3 * part : 12 + 3 * part]
        qkv[4 * part + 3 : 4 * part + 4, :] = total[18 + part : 19 + part]
    out[...] = total[21:25]


def along_tm(last, first):
    size = lax.axis_size("tm")
    up = lax.ppermute(last, "tm", [(i, i + 1) for i in range(size - 1)])
    down = lax.ppermute(first, "tm", [(i + 1, i) for i in range(size - 1)])
    return up, down


def exchange(array, axis):
    return lax.all_to_all(array, axis, split_axis=0, concat_axis=0, tiled=True)


def shards(spectrum, conv_weight, qkv_weight, out_weight, cotangent):
    frames, bins, width = spectrum.shape
    cells = frames * bins
    wide = HEADS * HEAD
    long = bins + EXTRA
    tm = lax.axis_size("tm")
    vmem = pltpu.VMEM
    cotangent = cotangent.reshape(cells, width)
    up, down = along_tm(spectrum[frames - 1 :], spectrum[:1])
    own, borders, matrix, matrix_back = kernel_call(
        conv_own_body, "conv_own",
        [
            ((cells, width), F32), ((2, frames, width), F32),
            ((3, 3 * width, width), BF), ((3, width, 3 * width), BF),
        ],
        spectrum, conv_weight,
        scratch=[vmem((frames, bins, 3 * width), BF)], mflops=1200,
    )
    payload, slope = kernel_call(
        conv_finish_body, "conv_finish",
        [((frames, long, width), BF), ((frames, bins, width), F32)],
        spectrum, up, down, own, borders, matrix,
        scratch=[vmem((frames, bins, width), F32), vmem((frames, EXTRA, width), F32)], mflops=200,
    )
    frame = exchange(payload, "freq")
    turned, grad_att = kernel_call(
        prepare_body, "prepare",
        [((width, cells + 2 * bins), BF), ((cells, wide), BF)],
        spectrum, up, down, cotangent, out_weight, mflops=300,
    )
    sums = [vmem((HEAD, cells), F32), vmem((HEAD, cells), F32)]
    more = tm * EARLY // HEADS
    hidden, border_slope, qkv, attended, grad_cells, message = kernel_call(
        attend_first_body, "attend_first",
        [
            ((cells, width), BF), ((2, frames, width), F32), ((cells, 3 * wide), BF),
            ((cells, wide), BF), ((cells, 3 * wide), BF),
            ((8, 3 * EARLY * tm + 4 * more, 128), BF),
        ],
        frame, qkv_weight, grad_att, cotangent,
        scratch=sums + [
            vmem((3 * EARLY, width, HEAD), F32), vmem((2, EARLY * HEAD, HEAD), F32),
            vmem((frames, EXTRA, width), F32),
        ],
        mflops=10000,
    )
    early = exchange(message, "freq")
    back, enhanced, head_message = kernel_call(
        attend_last_body, "attend_last",
        [
            ((frames, long, width), BF), ((cells, width), BF),
            ((8, 3 * tm + 4 * (tm - more), 128), BF),
        ],
        hidden, border_slope, qkv, attended, grad_cells, grad_att, cotangent, qkv_weight,
        out_weight,
        scratch=[vmem((cells, wide), BF), vmem((cells, 3 * wide), BF)] + sums + [
            vmem((3, width, HEAD), F32), vmem((2, HEAD, HEAD), F32),
            vmem((frames, bins, width), F32), vmem((frames, EXTRA, width), F32),
        ],
        mflops=5000,
    )
    (early,) = kernel_call(sum_body, "sum_early", [(early.shape[1:], F32)], early)
    grads = exchange(back, "freq")
    stacked, edges, message = kernel_call(
        conv_weight_body, "conv_weight_grad",
        [
            ((frames, bins, 3 * width), BF), ((2, 1, long, width), BF),
            ((8, head_message.shape[1] + 9 * tm, 128), BF),
        ],
        grads, slope, turned, head_message,
        scratch=[vmem((18 * (width // 2), width // 2), F32), vmem((frames, EXTRA, width), F32)],
        mflops=1200,
    )
    late = exchange(message, "freq")
    edge_up, edge_down = along_tm(edges[1:], edges[:1])
    (total,) = kernel_call(
        conv_data_body, "conv_data", [((cells, width), F32)],
        grads, stacked, matrix_back, mflops=1200,
    )
    (grad_spectrum,) = kernel_call(
        conv_data_finish_body, "conv_data_finish", [((frames, bins, width), BF)],
        total, edge_up, edge_down, matrix_back, mflops=100,
    )
    (chunk,) = kernel_call(
        regroup_body, "regroup", [((tm, 32, 128), BF)],
        early, late,
        scratch=[vmem(late.shape[1:], F32), vmem((tm, 32, 128), F32)],
    )
    shares = kernel_call(
        share_body, "share", [((9, 128), F32), ((12, 128), F32), ((4, 128), F32)],
        exchange(chunk, "tm"),
        scratch=[vmem((32, 128), F32)],
    )
    return (enhanced.reshape(1, cells, width), grad_spectrum, *[s.reshape(-1) for s in shares])


def solution(mesh):
    placed = (P("tm", "freq", None), P(), P(), P(), P(("tm", "freq"), None, None))
    return jax.shard_map(
        shards,
        mesh=mesh,
        in_specs=placed,
        out_specs=(
            P(("tm", "freq"), None, None),
            P("tm", "freq", None),
            P(("tm", "freq")),
            P(("tm", "freq")),
            P(("tm", "freq")),
        ),
        check_vma=False,
    )
```

```python
import math

import jax
import jax.numpy as jnp
from jax import lax
from jax.experimental import pallas as pl
from jax.experimental.pallas import tpu as pltpu
from jax.sharding import PartitionSpec as P

HEADS = 4
HEAD = 128
EARLY = 3
EXTRA = 16
SCALE = 1.0 / 512
LOG2E = math.log2(math.e)
FACTOR = 1.0 / math.sqrt(HEAD)
BF = jnp.bfloat16
F32 = jnp.float32
NN = (((1,), (0,)), ((), ()))
NT = (((1,), (1,)), ((), ()))
QUERY_BLOCK = 512


def mm(a, b, dims=NN):
    return lax.dot_general(a, b, dims, preferred_element_type=F32)


def kernel_call(body, name, outs, *args, far=(), scratch=(), copies=0, mflops=0, limit=48):
    shapes = [
        (pltpu.HBM if away else jax.ShapeDtypeStruct)(dims, kind) for dims, kind, away in outs
    ]
    args = [
        pltpu.with_memory_space_constraint(a, pltpu.HBM) if n in far else a
        for n, a in enumerate(args)
    ]
    size = sum(math.prod(a.shape) * a.dtype.itemsize for a in (*args, *shapes))
    near, hbm = pl.BlockSpec(memory_space=pltpu.VMEM), pl.BlockSpec(memory_space=pltpu.HBM)
    scratch = list(scratch) + ([pltpu.SemaphoreType.DMA((copies,))] if copies else [])
    return pl.pallas_call(
        body,
        out_shape=shapes,
        in_specs=[hbm if n in far else near for n in range(len(args))],
        out_specs=[hbm if away else near for _, _, away in outs],
        scratch_shapes=scratch,
        compiler_params=pltpu.CompilerParams(vmem_limit_bytes=limit * 2**20),
        cost_estimate=pl.CostEstimate(
            flops=mflops * 10**6, bytes_accessed=size, transcendentals=0
        ),
        name=name,
    )(*args)


def copier(semaphores):
    started = []

    def start(source, target):
        copy = pltpu.make_async_copy(source, target, semaphores.at[len(started)])
        copy.start()
        started.append(copy)
        return copy

    return start


def sigmoid(v):
    return 1.0 / (1.0 + jnp.exp(-v))


def slope_of(v, sigma):
    return sigma * (1.0 + v * (1.0 - sigma))


def moved_down(rows):
    at = lax.broadcasted_iota(jnp.int32, rows.shape, 0)
    return jnp.where(at == 0, 0.0, pltpu.roll(rows, 1, 0))


def moved_up(rows):
    last = rows.shape[0] - 1
    at = lax.broadcasted_iota(jnp.int32, rows.shape, 0)
    return jnp.where(at == last, 0.0, pltpu.roll(rows, last, 0))


def with_borders(inner, first, last):
    at = lax.broadcasted_iota(jnp.int32, inner.shape, 1)
    inner = jnp.where(at == 0, first[:, None, :], inner)
    return jnp.where(at == inner.shape[1] - 1, last[:, None, :], inner)


def bins_before(rows, left):
    at = lax.broadcasted_iota(jnp.int32, rows.shape, 1)
    return jnp.where(at == 0, left, pltpu.roll(rows, 1, 1))


def bins_after(rows, right):
    last = rows.shape[1] - 1
    at = lax.broadcasted_iota(jnp.int32, rows.shape, 1)
    return jnp.where(at == last, right, pltpu.roll(rows, last, 1))


def conv_own_body(mid_far, weight_far, conv, borders, matrix, mid, weight, stacked, semaphores):
    start = copier(semaphores)
    load_weight, load_mid = start(weight_far, weight), start(mid_far, mid)
    frames, bins, width = mid.shape
    half = width // 2
    load_weight.wait()
    for i in range(3):
        for j in range(3):
            real, imag = weight[0, i, j], weight[1, i, j]
            at = j * width
            matrix[i, at : at + half, :half] = real
            matrix[i, at : at + half, half:] = imag
            matrix[i, at + half : at + width, :half] = -imag
            matrix[i, at + half : at + width, half:] = real
    load_mid.wait()
    wide = mid[...].astype(F32)
    stacked[:, :, :width] = bins_before(wide, 0.0).astype(BF)
    stacked[:, :, width : 2 * width] = mid[...]
    stacked[:, :, 2 * width :] = bins_after(wide, 0.0).astype(BF)
    inner = (frames - 1) * bins
    everything = stacked[...].reshape(frames * bins, 3 * width)
    conv[...] = mm(everything, matrix[1])
    conv[bins:] += mm(everything[:inner], matrix[0])
    conv[:inner] += mm(everything[bins:], matrix[2])
    borders[0] = mid[:, 0, :].astype(F32)
    borders[1] = mid[:, bins - 1, :].astype(F32)


def conv_finish_body(
    mid_far, up, down, own, borders, matrix, payload, slope_far, mid, slope, conv, pieces, semaphores
):
    start = copier(semaphores)
    load_mid = start(mid_far, mid)
    frames, bins, width = mid.shape
    cells = frames * bins

    def stack(row):
        wide = row[...].astype(F32)
        before = bins_before(wide, 0.0).astype(BF)
        after = bins_after(wide, 0.0).astype(BF)
        return jnp.concatenate([before[0], row[0], after[0]], axis=1)

    conv[...] = own[...].reshape(frames, bins, width)
    conv[0] += mm(stack(up), matrix[0])
    conv[frames - 1] += mm(stack(down), matrix[2])

    def beyond(bin_at, side, tap):
        rows = jnp.concatenate(
            [up[:, bin_at, :].astype(F32), borders[side], down[:, bin_at, :].astype(F32)], axis=0
        )
        total = None
        for i in range(3):
            term = mm(
                rows[i : i + frames].astype(BF), matrix[i, tap * width : (tap + 1) * width, :]
            )
            total = term if total is None else total + term
        return total

    parts = (
        beyond(0, 0, 2),
        conv[:, 0, :],
        conv[:, bins - 1, :],
        beyond(bins - 1, 1, 0),
    )
    pieces[...] = jnp.zeros(pieces.shape, F32)
    for at, part in enumerate(parts):
        high = part.astype(BF).astype(F32)
        pieces[:, 2 * at, :] = high
        pieces[:, 2 * at + 1, :] = part - high
    values = conv[...]
    sigma = sigmoid(values)
    slope[...] = slope_of(values, sigma)
    store = start(slope, slope_far)
    load_mid.wait()
    hidden = mid[...].astype(F32) + values * sigma
    payload[:, :bins, :] = with_borders(hidden, borders[0], borders[1]).astype(BF)
    payload[:, bins:, :] = pieces[...].astype(BF)
    store.wait()


def prepare_body(
    mid_far, up, down, cotangent_far, out_w_far, turned_far, grad_att_far,
    mid, cotangent, out_w, turned, grad_att, semaphores,
):
    start = copier(semaphores)
    loads = start(mid_far, mid), start(cotangent_far, cotangent), start(out_w_far, out_w)
    for load in loads:
        load.wait()
    frames, bins, width = mid.shape
    turned[:, :bins] = up[0].T
    turned[:, bins : (frames + 1) * bins] = mid[...].reshape(frames * bins, width).T
    turned[:, (frames + 1) * bins :] = down[0].T
    grad_att[...] = mm(cotangent[...], out_w[...], NT).astype(BF)
    stores = start(turned, turned_far), start(grad_att, grad_att_far)
    for store in stores:
        store.wait()


def columns(part, h, heads=HEADS):
    at = (part * heads + h) * HEAD
    if not isinstance(h, int):
        at = pl.multiple_of(at, HEAD)
    return pl.ds(at, HEAD)


def one_head(h, heads, qkv, grad_att, attended, grad_cells, sum_keys, sum_values):
    def columns_of(part):
        return columns(part, h, heads)

    cells = qkv.shape[0]
    keys = qkv[:, columns_of(1)]
    values = qkv[:, columns_of(2)]
    values_ones = jnp.concatenate([values, jnp.ones((cells, HEAD), BF)], axis=1)
    for block in range(cells // QUERY_BLOCK):
        rows = slice(block * QUERY_BLOCK, (block + 1) * QUERY_BLOCK)
        queries = qkv[rows, columns_of(0)]
        scores = mm(queries, keys, NT)
        raised = jnp.exp2(scores - jnp.max(scores, axis=-1, keepdims=True))
        raised_b = raised.astype(BF)
        sums = mm(raised_b, values_ones)
        inverse = 1.0 / sums[:, HEAD:]
        result = sums[:, :HEAD] * inverse
        attended[rows, columns_of(0)] = result.astype(BF)
        scaled = grad_att[rows, columns_of(0)].astype(F32) * inverse
        inner = jnp.sum(scaled * result, axis=-1, keepdims=True)
        scaled_b = scaled.astype(BF)
        grad_probs = mm(scaled_b, values, NT)
        grad_scores = (raised * (grad_probs - inner)).astype(BF)
        grad_cells[rows, columns_of(0)] = (mm(grad_scores, keys) * FACTOR).astype(BF)
        new_keys = mm(queries.T, grad_scores)
        new_values = mm(scaled_b.T, raised_b)
        if block == 0:
            sum_keys[...] = new_keys
            sum_values[...] = new_values
        else:
            sum_keys[...] += new_keys
            sum_values[...] += new_values
    grad_cells[:, columns_of(1)] = (sum_keys[...] * (1.0 / LOG2E)).T.astype(BF)
    grad_cells[:, columns_of(2)] = sum_values[...].T.astype(BF)


def normed_parts(hidden_f):
    inv_rms = lax.rsqrt(jnp.mean(hidden_f * hidden_f, axis=-1, keepdims=True) + 1e-6)
    normed_f = hidden_f * inv_rms
    return inv_rms, normed_f, normed_f.astype(BF)


def split_columns(target, at, values):
    for n in range(values.shape[1] // 128):
        target[at + n] = values[:, n * 128 : (n + 1) * 128]


def spread_rows(message, at, source, group, first, step, count):
    for f in range(message.shape[0]):
        rows = source[group, pl.ds(first(f), count, stride=step), :]
        message[f, at : at + count, :] = rows.astype(BF)


def attend_first_body(
    came, qkv_w_far, grad_att_far, cotangent_far,
    border_slope, message, hidden_far, qkv_far, attended_far, grad_cells_far,
    qkv_w, grad_att, cotangent, hidden, qkv, late, attended, grad_cells,
    sum_keys, sum_values, grads, grads_out, pieces, semaphores,
):
    start = copier(semaphores)
    narrow = EARLY * HEAD
    load_qkv_w = start(qkv_w_far, qkv_w)
    load_grad_att = start(grad_att_far.at[:, :narrow], grad_att)
    load_cotangent = start(cotangent_far, cotangent)
    chunks, long, width = came.shape
    bins = long - EXTRA
    wide = HEADS * HEAD
    pieces[...] = came[:, bins:, :].astype(F32)
    here_first = pieces[:, 2, :] + pieces[:, 3, :]
    here_last = pieces[:, 4, :] + pieces[:, 5, :]
    first = here_first + moved_down(pieces[:, 6, :] + pieces[:, 7, :])
    last = here_last + moved_up(pieces[:, 0, :] + pieces[:, 1, :])
    sigma_first, sigma_last = sigmoid(first), sigmoid(last)
    border_slope[0] = slope_of(first, sigma_first)
    border_slope[1] = slope_of(last, sigma_last)
    fixed_first = came[:, 0, :].astype(F32) + first * sigma_first
    fixed_last = came[:, bins - 1, :].astype(F32) + last * sigma_last
    cells = with_borders(came[:, :bins, :].astype(F32), fixed_first, fixed_last)
    hidden[...] = cells.astype(BF).reshape(chunks * bins, width)
    stores = [start(hidden, hidden_far)]
    _, _, normed = normed_parts(hidden[...].astype(F32))
    load_qkv_w.wait()
    for part in range(3):
        values = mm(normed, qkv_w[:, part * wide : (part + 1) * wide])
        if part == 0:
            values = values * (FACTOR * LOG2E)
        values = values.astype(BF)
        qkv[:, part * narrow : (part + 1) * narrow] = values[:, :narrow]
        late[:, part * HEAD : (part + 1) * HEAD] = values[:, narrow:]
    stores.append(start(late, qkv_far))
    load_grad_att.wait()

    def head(h, carry):
        one_head(h, EARLY, qkv, grad_att, attended, grad_cells, sum_keys, sum_values)
        return carry

    lax.fori_loop(0, EARLY, head, 0)
    stores += [start(attended, attended_far), start(grad_cells, grad_cells_far)]
    load_cotangent.wait()
    turned = normed.T
    for part in range(3):
        values = mm(turned, grad_cells[:, part * narrow : (part + 1) * narrow])
        split_columns(grads, part * EARLY, SCALE * values)
    split_columns(grads_out, 0, SCALE * mm(attended[...].T, cotangent[...]))
    tm = width // 8
    for group in range(3 * EARLY):
        spread_rows(message, group * tm, grads, group, lambda f: f, 8, tm)
    for group in range(4):
        b, c = divmod(group, 2)
        few = tm * EARLY // HEADS
        spread_rows(
            message, 3 * EARLY * tm + group * few, grads_out, c,
            lambda f: 2 * f + b, 16, few,
        )
    for store in stores:
        store.wait()


def attend_last_body(
    border_slope, hidden_far, qkv_far, grad_cells_far, grad_att_far, cotangent_far, qkv_w_far,
    payload, attended_far, late_cells_far,
    hidden, qkv, grad_att, cotangent, qkv_w, attended, late_cells, grad_cells,
    sum_keys, sum_values, rows_f, pieces, semaphores,
):
    start = copier(semaphores)
    chunks, long, width = payload.shape
    bins = long - EXTRA
    wide = HEADS * HEAD
    narrow = EARLY * HEAD
    loads = [start(qkv_far, qkv), start(grad_att_far.at[:, narrow:], grad_att)]
    later = [
        start(hidden_far, hidden), start(cotangent_far, cotangent), start(qkv_w_far, qkv_w)
    ]
    for part in range(3):
        source = grad_cells_far.at[:, part * narrow : (part + 1) * narrow]
        target = grad_cells.at[:, part * wide : part * wide + narrow]
        later.append(start(source, target))
    for load in loads:
        load.wait()
    one_head(0, 1, qkv, grad_att, attended, late_cells, sum_keys, sum_values)
    stores = [start(attended, attended_far), start(late_cells, late_cells_far)]
    for load in later:
        load.wait()
    for part in range(3):
        grad_cells[:, columns(part, EARLY)] = late_cells[:, columns(part, 0, 1)]
    inv_rms, normed_f, _ = normed_parts(hidden[...].astype(F32))
    grad_normed = mm(grad_cells[...], qkv_w[...], NT)
    mixing = jnp.mean(grad_normed * normed_f, axis=-1, keepdims=True)
    grad = cotangent[...].astype(F32) + inv_rms * (grad_normed - normed_f * mixing)
    grad_b = grad.astype(BF).reshape(chunks, bins, width)
    payload[:, :bins, :] = grad_b
    rows_f[...] = grad_b.astype(F32)
    first = rows_f[:, 0, :] * border_slope[0]
    last = rows_f[:, bins - 1, :] * border_slope[1]
    pieces[...] = jnp.zeros(pieces.shape, F32)
    pieces[:, 0, :] = moved_down(last)
    pieces[:, 1, :] = first
    pieces[:, 2, :] = last
    pieces[:, 3, :] = moved_up(first)
    payload[:, bins:, :] = pieces[...].astype(BF)
    for store in stores:
        store.wait()


def attend_rest_body(
    hidden_far, attended_far, attended_late_far, late_cells_far, cotangent_far, out_w_far,
    enhanced, message_far,
    hidden, attended, late_cells, cotangent, out_w, message, grads, grads_out, semaphores,
):
    start = copier(semaphores)
    narrow = EARLY * HEAD
    loads = [
        start(hidden_far, hidden), start(late_cells_far, late_cells),
        start(attended_far, attended.at[:, :narrow]),
        start(attended_late_far, attended.at[:, narrow:]),
        start(cotangent_far, cotangent), start(out_w_far, out_w),
    ]
    for load in loads:
        load.wait()
    width = hidden.shape[1]
    hidden_f = hidden[...].astype(F32)
    _, _, normed = normed_parts(hidden_f)
    enhanced[...] = (hidden_f + mm(attended[...], out_w[...])).astype(BF)
    tm = width // 8
    split_columns(grads, 0, SCALE * mm(normed.T, late_cells[...]))
    for part in range(3):
        spread_rows(message, part * tm, grads, part, lambda f: f, 8, tm)
    split_columns(grads_out, 0, SCALE * mm(attended[:, narrow:].T, cotangent[...]))
    few = tm // HEADS
    for group in range(4):
        b, c = divmod(group, 2)
        spread_rows(
            message, 3 * tm + group * few, grads_out, c, lambda f: 2 * f + b, 16, few
        )
    start(message, message_far).wait()


def stack_back(rows, left, right):
    after = bins_after(rows, right).astype(BF)
    before = bins_before(rows, left).astype(BF)
    return jnp.concatenate([after, rows.astype(BF), before], axis=-1)


def conv_weight_body(
    came, slope_far, turned_far, head_far, edges, message, stacked_far, grad_far,
    slope, turned, head_message, stacked, own, grads, pieces, semaphores,
):
    start = copier(semaphores)
    load_slope, load_turned = start(slope_far, slope), start(turned_far, turned)
    load_head = start(head_far, head_message)
    frames, long, width = came.shape
    bins = long - EXTRA
    half = width // 2
    cells = frames * bins
    pieces[...] = came[:, bins:, :].astype(F32)
    own[...] = came[:, :bins, :]
    stores = [start(own, grad_far)]
    load_slope.wait()
    grad = own[...].astype(F32) * slope[...]
    grad = with_borders(grad, pieces[:, 1, :], pieces[:, 2, :])
    grad_b = grad.astype(BF)
    for side, frame in enumerate((0, frames - 1)):
        edges[side, :, :bins, :] = grad_b[frame : frame + 1]
        edges[side, :, bins:, :] = came[frame : frame + 1, bins:, :]
    stacked[...] = stack_back(
        grad_b.astype(F32), pieces[:, 0, :][:, None, :], pieces[:, 3, :][:, None, :]
    )
    stores.append(start(stacked, stacked_far))
    flat = stacked[...].reshape(cells, 3 * width)
    load_turned.wait()
    for i in range(3):
        block = mm(turned[:, i * bins : i * bins + cells], flat)
        for j in range(3):
            at = j * width
            upper = block[:half, at : at + half] + block[half:, at + half : at + width]
            lower = block[:half, at + half : at + width] - block[half:, at : at + half]
            tap = (3 * i + j) * half
            grads[tap : tap + half] = upper * SCALE
            grads[9 * half + tap : 9 * half + tap + half] = lower * SCALE
    load_head.wait()
    early = head_message.shape[1]
    message[:, :early, :] = head_message[...]
    tm = width // 8
    for f in range(8):
        for e in range(9):
            rows = grads[pl.ds(9 * f + e, tm, stride=72), :]
            message[f, early + e * tm : early + (e + 1) * tm, :] = rows.astype(BF)
    for store in stores:
        store.wait()


def conv_data_body(
    grad_far, stacked_far, weight_far, total, matrix, grad, stacked, weight, semaphores
):
    start = copier(semaphores)
    load_weight, load_stacked = start(weight_far, weight), start(stacked_far, stacked)
    load_grad = start(grad_far, grad)
    frames, bins, triple = stacked.shape
    width = triple // 3
    half = width // 2
    load_weight.wait()
    for i in range(3):
        for j in range(3):
            real, imag = weight[0, i, j], weight[1, i, j]
            at = j * width
            matrix[i, :half, at : at + half] = real
            matrix[i, :half, at + half : at + width] = imag
            matrix[i, half:, at : at + half] = -imag
            matrix[i, half:, at + half : at + width] = real
    load_stacked.wait()
    load_grad.wait()
    inner = (frames - 1) * bins
    flat = stacked[...].reshape(frames * bins, triple)
    total[...] = grad[...].reshape(frames * bins, width).astype(F32) + mm(flat, matrix[1], NT)
    total[:inner] += mm(flat[bins:], matrix[0], NT)
    total[bins:] += mm(flat[:inner], matrix[2], NT)


def conv_data_finish_body(total, up, down, matrix, out):
    frames, bins, width = out.shape

    def stack(edge):
        extra = edge[0, :, bins:, :].astype(F32)
        rows = edge[0, :, :bins, :].astype(F32)
        return stack_back(rows, extra[:, 0:1, :], extra[:, 3:4, :])[0]

    out[...] = total[...].reshape(frames, bins, width).astype(BF)
    out[0] = (total[:bins] + mm(stack(up), matrix[2], NT)).astype(BF)
    out[frames - 1] = (total[(frames - 1) * bins :] + mm(stack(down), matrix[0], NT)).astype(BF)


def sum_body(came, out):
    total = came[0].astype(F32)
    for source in range(1, came.shape[0]):
        total = total + came[source].astype(F32)
    out[...] = total


def regroup_body(early, came, chunk, late, rows):
    tm = chunk.shape[0]
    sum_body(came, late)
    few, more = tm // HEADS, tm * EARLY // HEADS
    base = 3 * tm + 4 * few
    rows[...] = jnp.zeros(rows.shape, F32)
    for t in range(tm):
        rows[t, 0:9, :] = late[pl.ds(base + t, 9, stride=tm), :]
        rows[t, 9:18, :] = early[pl.ds(t, 3 * EARLY, stride=tm), :]
        rows[t, 18:21, :] = late[pl.ds(t, 3, stride=tm), :]
        if t < more:
            rows[t, 21:25, :] = early[pl.ds(3 * EARLY * tm + t, 4, stride=more), :]
        else:
            rows[t, 21:25, :] = late[pl.ds(3 * tm + t - more, 4, stride=few), :]
    chunk[...] = rows[...].astype(BF)


def share_body(came, conv, qkv, out, total):
    sum_body(came, total)
    conv[...] = total[0:9]
    for part in range(3):
        qkv[4 * part : 4 * part + 3, :] = total[9 + 3 * part : 12 + 3 * part]
        qkv[4 * part + 3 : 4 * part + 4, :] = total[18 + part : 19 + part]
    out[...] = total[21:25]


def along_tm(last, first):
    size = lax.axis_size("tm")
    up = lax.ppermute(last, "tm", [(i, i + 1) for i in range(size - 1)])
    down = lax.ppermute(first, "tm", [(i + 1, i) for i in range(size - 1)])
    return up, down


def exchange(array, axis):
    return lax.all_to_all(array, axis, split_axis=0, concat_axis=0, tiled=True)


def shards(spectrum, conv_weight, qkv_weight, out_weight, cotangent):
    frames, bins, width = spectrum.shape
    cells = frames * bins
    wide = HEADS * HEAD
    long = bins + EXTRA
    tm = lax.axis_size("tm")
    vmem = pltpu.VMEM
    cotangent = cotangent.reshape(cells, width)
    up, down = along_tm(spectrum[frames - 1 :], spectrum[:1])
    tile = vmem((frames, bins, width), BF)
    tile_f = vmem((frames, bins, width), F32)
    pieces = vmem((frames, EXTRA, width), F32)
    square = vmem((cells, width), BF)
    kernels = vmem(conv_weight.shape, BF)
    own, borders, matrix = kernel_call(
        conv_own_body, "conv_own",
        [
            ((cells, width), F32, False), ((2, frames, width), F32, False),
            ((3, 3 * width, width), BF, False),
        ],
        spectrum, conv_weight, far=(0, 1),
        scratch=[tile, kernels, vmem((frames, bins, 3 * width), BF)], copies=2, mflops=1200,
    )
    payload, slope = kernel_call(
        conv_finish_body, "conv_finish",
        [((frames, long, width), BF, False), ((frames, bins, width), F32, True)],
        spectrum, up, down, own, borders, matrix, far=(0,),
        scratch=[tile, tile_f, tile_f, pieces], copies=2, mflops=200,
    )
    frame = exchange(payload, "freq")
    turned_shape = (width, cells + 2 * bins)
    turned, grad_att = kernel_call(
        prepare_body, "prepare",
        [(turned_shape, BF, True), ((cells, wide), BF, True)],
        spectrum, up, down, cotangent, out_weight, far=(0, 3, 4),
        scratch=[
            tile, square, vmem((wide, width), BF), vmem(turned_shape, BF), vmem((cells, wide), BF)
        ],
        copies=5, mflops=300,
    )
    sums = [vmem((HEAD, cells), F32), vmem((HEAD, cells), F32)]
    projections = vmem((width, 3 * wide), BF)
    more = tm * EARLY // HEADS
    narrow = EARLY * HEAD
    border_slope, message, hidden, qkv, attended, grad_cells = kernel_call(
        attend_first_body, "attend_first",
        [
            ((2, frames, width), F32, False), ((8, 3 * EARLY * tm + 4 * more, 128), BF, False),
            ((cells, width), BF, True), ((cells, 3 * HEAD), BF, True), ((cells, narrow), BF, True),
            ((cells, 3 * narrow), BF, True),
        ],
        frame, qkv_weight, grad_att, cotangent, far=(1, 2, 3),
        scratch=[
            projections, vmem((cells, narrow), BF), square, square, vmem((cells, 3 * narrow), BF),
            vmem((cells, 3 * HEAD), BF), vmem((cells, narrow), BF), vmem((cells, 3 * narrow), BF),
        ] + sums + [
            vmem((3 * EARLY, width, HEAD), F32), vmem((2, narrow, HEAD), F32), pieces,
        ],
        copies=7, mflops=10000,
    )
    early = exchange(message, "freq")
    back, attended_late, late_cells = kernel_call(
        attend_last_body, "attend_last",
        [
            ((frames, long, width), BF, False), ((cells, HEAD), BF, True),
            ((cells, 3 * HEAD), BF, True),
        ],
        border_slope, hidden, qkv, grad_cells, grad_att, cotangent, qkv_weight,
        far=(1, 2, 3, 4, 5, 6),
        scratch=[
            square, vmem((cells, 3 * HEAD), BF), vmem((cells, HEAD), BF), square, projections,
            vmem((cells, HEAD), BF), vmem((cells, 3 * HEAD), BF), vmem((cells, 3 * wide), BF),
        ] + sums + [tile_f, pieces],
        copies=10, mflops=4000,
    )
    back, early = lax.optimization_barrier((back, early))
    grads = exchange(back, "freq")
    (early,) = kernel_call(sum_body, "sum_early", [(early.shape[1:], F32, False)], early)
    head_shape = (8, 3 * tm + 4 * (tm - more), 128)
    enhanced, head_message = kernel_call(
        attend_rest_body, "attend_rest",
        [((cells, width), BF, False), (head_shape, BF, True)],
        hidden, attended, attended_late, late_cells, cotangent, out_weight,
        far=(0, 1, 2, 3, 4, 5),
        scratch=[
            square, vmem((cells, wide), BF), vmem((cells, 3 * HEAD), BF), square,
            vmem((wide, width), BF), vmem(head_shape, BF), vmem((3, width, HEAD), F32),
            vmem((2, HEAD, HEAD), F32),
        ],
        copies=7, mflops=1000,
    )
    stacked_shape = (frames, bins, 3 * width)
    edges, message, stacked, grad_tile = kernel_call(
        conv_weight_body, "conv_weight_grad",
        [
            ((2, 1, long, width), BF, False), ((8, head_shape[1] + 9 * tm, 128), BF, False),
            (stacked_shape, BF, True), ((frames, bins, width), BF, True),
        ],
        grads, slope, turned, head_message, far=(1, 2, 3),
        scratch=[
            tile_f, vmem(turned_shape, BF), vmem(head_shape, BF), vmem(stacked_shape, BF), tile,
            vmem((18 * (width // 2), width // 2), F32), pieces,
        ],
        copies=5, mflops=1200,
    )
    late = exchange(message, "freq")
    edge_up, edge_down = along_tm(edges[1:], edges[:1])
    total, matrix_back = kernel_call(
        conv_data_body, "conv_data",
        [((cells, width), F32, False), ((3, width, 3 * width), BF, False)],
        grad_tile, stacked, conv_weight, far=(0, 1, 2),
        scratch=[tile, vmem(stacked_shape, BF), kernels], copies=3, mflops=1200,
    )
    (grad_spectrum,) = kernel_call(
        conv_data_finish_body, "conv_data_finish", [((frames, bins, width), BF, False)],
        total, edge_up, edge_down, matrix_back, mflops=100,
    )
    late, grad_spectrum = lax.optimization_barrier((late, grad_spectrum))
    (chunk,) = kernel_call(
        regroup_body, "regroup", [((tm, 32, 128), BF, False)],
        early, late,
        scratch=[vmem(late.shape[1:], F32), vmem((tm, 32, 128), F32)],
    )
    shares = kernel_call(
        share_body, "share", [((9, 128), F32, False), ((12, 128), F32, False), ((4, 128), F32, False)],
        exchange(chunk, "tm"),
        scratch=[vmem((32, 128), F32)],
    )
    return (enhanced.reshape(1, cells, width), grad_spectrum, *[s.reshape(-1) for s in shares])


def solution(mesh):
    placed = (P("tm", "freq", None), P(), P(), P(), P(("tm", "freq"), None, None))
    return jax.shard_map(
        shards,
        mesh=mesh,
        in_specs=placed,
        out_specs=(
            P(("tm", "freq"), None, None),
            P("tm", "freq", None),
            P(("tm", "freq")),
            P(("tm", "freq")),
            P(("tm", "freq")),
        ),
        check_vma=False,
    )
```

```python
import math

import jax
import jax.numpy as jnp
from jax import lax
from jax.experimental import pallas as pl
from jax.experimental.pallas import tpu as pltpu
from jax.sharding import Mesh
from jax.sharding import PartitionSpec as P

HEADS = 4
HEAD = 128
EXTRA = 16
SCALE = 1.0 / 512
LOG2E = math.log2(math.e)
FACTOR = 1.0 / math.sqrt(HEAD)
BF = jnp.bfloat16
F32 = jnp.float32
NN = (((1,), (0,)), ((), ()))
NT = (((1,), (1,)), ((), ()))
QUERY_BLOCK = 1024
GROUPS = 26
EARLY = 16


def mm(a, b, dims=NN):
    return lax.dot_general(a, b, dims, preferred_element_type=F32)


PLACES = {"any": jax.ShapeDtypeStruct, "hbm": pltpu.HBM, "vmem": pltpu.VMEM}


def kernel_call(body, name, outs, *args, far=(), scratch=(), copies=0, mflops=0, limit=48):
    shapes = [
        PLACES[away](dims, kind) for dims, kind, away in outs
    ]
    args = [
        pltpu.with_memory_space_constraint(a, pltpu.HBM) if n in far else a
        for n, a in enumerate(args)
    ]
    size = sum(math.prod(a.shape) * a.dtype.itemsize for a in (*args, *shapes))
    near, hbm = pl.BlockSpec(memory_space=pltpu.VMEM), pl.BlockSpec(memory_space=pltpu.HBM)
    scratch = list(scratch) + ([pltpu.SemaphoreType.DMA((copies,))] if copies else [])
    return pl.pallas_call(
        body,
        out_shape=shapes,
        in_specs=[hbm if n in far else near for n in range(len(args))],
        out_specs=[hbm if away == "hbm" else near for _, _, away in outs],
        scratch_shapes=scratch,
        compiler_params=pltpu.CompilerParams(vmem_limit_bytes=limit * 2**20),
        cost_estimate=pl.CostEstimate(
            flops=mflops * 10**6, bytes_accessed=size, transcendentals=0
        ),
        name=name,
    )(*args)


def copier(semaphores):
    started = []

    def start(source, target):
        copy = pltpu.make_async_copy(source, target, semaphores.at[len(started)])
        copy.start()
        started.append(copy)
        return copy

    return start


def sigmoid(v):
    return 1.0 / (1.0 + jnp.exp(-v))


def slope_of(v, sigma):
    return sigma * (1.0 + v * (1.0 - sigma))


def moved_down(rows):
    at = lax.broadcasted_iota(jnp.int32, rows.shape, 0)
    return jnp.where(at == 0, 0.0, pltpu.roll(rows, 1, 0))


def moved_up(rows):
    last = rows.shape[0] - 1
    at = lax.broadcasted_iota(jnp.int32, rows.shape, 0)
    return jnp.where(at == last, 0.0, pltpu.roll(rows, last, 0))


def with_borders(inner, first, last):
    at = lax.broadcasted_iota(jnp.int32, inner.shape, 1)
    inner = jnp.where(at == 0, first[:, None, :], inner)
    return jnp.where(at == inner.shape[1] - 1, last[:, None, :], inner)


def bins_before(rows, left):
    at = lax.broadcasted_iota(jnp.int32, rows.shape, 1)
    return jnp.where(at == 0, left, pltpu.roll(rows, 1, 1))


def bins_after(rows, right):
    last = rows.shape[1] - 1
    at = lax.broadcasted_iota(jnp.int32, rows.shape, 1)
    return jnp.where(at == last, right, pltpu.roll(rows, last, 1))


def sort_halos(even_down, odd_down, up, down):
    odd = lax.rem(lax.axis_index("y"), 2) == 1
    first, second = even_down[...], odd_down[...]
    up[...] = jnp.where(odd, first, second)
    down[...] = jnp.where(odd, second, first)


def conv_own_body(mid_far, weight_far, conv, borders, matrix, mid, weight, stacked, semaphores):
    start = copier(semaphores)
    load_weight, load_mid = start(weight_far, weight), start(mid_far, mid)
    frames, bins, width = mid.shape
    half = width // 2
    load_weight.wait()
    for i in range(3):
        for j in range(3):
            real, imag = weight[0, i, j], weight[1, i, j]
            at = j * width
            matrix[i, at : at + half, :half] = real
            matrix[i, at : at + half, half:] = imag
            matrix[i, at + half : at + width, :half] = -imag
            matrix[i, at + half : at + width, half:] = real
    load_mid.wait()
    wide = mid[...].astype(F32)
    stacked[:, :, :width] = bins_before(wide, 0.0).astype(BF)
    stacked[:, :, width : 2 * width] = mid[...]
    stacked[:, :, 2 * width :] = bins_after(wide, 0.0).astype(BF)
    inner = (frames - 1) * bins
    everything = stacked[...].reshape(frames * bins, 3 * width)
    conv[...] = mm(everything, matrix[1])
    conv[bins:] += mm(everything[:inner], matrix[0])
    conv[:inner] += mm(everything[bins:], matrix[2])
    borders[0] = mid[:, 0, :].astype(F32)
    borders[1] = mid[:, bins - 1, :].astype(F32)


def conv_finish_body(
    mid_far, even_down, odd_down, own, borders, matrix,
    payload, slope_far, mid, slope, conv, pieces, up, down, semaphores,
):
    start = copier(semaphores)
    load_mid = start(mid_far, mid)
    sort_halos(even_down, odd_down, up, down)
    frames, bins, width = mid.shape

    def stack(row):
        wide = row[...].astype(F32)
        before = bins_before(wide, 0.0).astype(BF)
        after = bins_after(wide, 0.0).astype(BF)
        return jnp.concatenate([before[0], row[0], after[0]], axis=1)

    conv[...] = own[...].reshape(frames, bins, width)
    conv[0] += mm(stack(up), matrix[0])
    conv[frames - 1] += mm(stack(down), matrix[2])

    def beyond(bin_at, side, tap):
        rows = jnp.concatenate(
            [up[:, bin_at, :].astype(F32), borders[side], down[:, bin_at, :].astype(F32)], axis=0
        )
        total = None
        for i in range(3):
            term = mm(
                rows[i : i + frames].astype(BF), matrix[i, tap * width : (tap + 1) * width, :]
            )
            total = term if total is None else total + term
        return total

    parts = (
        beyond(0, 0, 2),
        conv[:, 0, :],
        conv[:, bins - 1, :],
        beyond(bins - 1, 1, 0),
    )
    pieces[...] = jnp.zeros(pieces.shape, F32)
    for at, part in enumerate(parts):
        high = part.astype(BF).astype(F32)
        pieces[:, 2 * at, :] = high
        pieces[:, 2 * at + 1, :] = part - high
    values = conv[...]
    sigma = sigmoid(values)
    slope[...] = slope_of(values, sigma)
    store = start(slope, slope_far)
    load_mid.wait()
    hidden = mid[...].astype(F32) + values * sigma
    payload[:, :bins, :] = with_borders(hidden, borders[0], borders[1]).astype(BF)
    payload[:, bins:, :] = pieces[...].astype(BF)
    store.wait()


def prepare_body(
    mid_far, even_down, odd_down, cotangent_far, out_w_far, turned_far, grad_att_far,
    mid, cotangent, out_w, turned, grad_att, up, down, semaphores,
):
    start = copier(semaphores)
    loads = start(mid_far, mid), start(cotangent_far, cotangent), start(out_w_far, out_w)
    sort_halos(even_down, odd_down, up, down)
    for load in loads:
        load.wait()
    frames, bins, width = mid.shape
    turned[:, :bins] = up[0].T
    turned[:, bins : (frames + 1) * bins] = mid[...].reshape(frames * bins, width).T
    turned[:, (frames + 1) * bins :] = down[0].T
    grad_att[...] = mm(cotangent[...], out_w[...], NT).astype(BF)
    stores = start(turned, turned_far), start(grad_att, grad_att_far)
    for store in stores:
        store.wait()


def columns(part, h, heads=HEADS):
    at = (part * heads + h) * HEAD
    if not isinstance(h, int):
        at = pl.multiple_of(at, HEAD)
    return pl.ds(at, HEAD)


def one_head(h, heads, qkv, grad_att, attended, grad_cells, sum_keys, sum_values):
    def columns_of(part):
        return columns(part, h, heads)

    cells = qkv.shape[0]
    keys = qkv[:, columns_of(1)]
    values = qkv[:, columns_of(2)]
    values_ones = jnp.concatenate([values, jnp.ones((cells, HEAD), BF)], axis=1)
    for block in range(cells // QUERY_BLOCK):
        rows = slice(block * QUERY_BLOCK, (block + 1) * QUERY_BLOCK)
        queries = qkv[rows, columns_of(0)]
        scores = mm(queries, keys, NT)
        raised = jnp.exp2(scores - jnp.max(scores, axis=-1, keepdims=True))
        raised_b = raised.astype(BF)
        sums = mm(raised_b, values_ones)
        inverse = 1.0 / sums[:, HEAD:]
        result = sums[:, :HEAD] * inverse
        attended[rows, columns_of(0)] = result.astype(BF)
        scaled = grad_att[rows, columns_of(0)].astype(F32) * inverse
        inner = jnp.sum(scaled * result, axis=-1, keepdims=True)
        scaled_b = scaled.astype(BF)
        grad_probs = mm(scaled_b, values, NT)
        grad_scores = (raised * (grad_probs - inner)).astype(BF)
        grad_cells[rows, columns_of(0)] = (mm(grad_scores, keys) * FACTOR).astype(BF)
        new_keys = mm(queries.T, grad_scores)
        new_values = mm(scaled_b.T, raised_b)
        if block == 0:
            sum_keys[...] = new_keys
            sum_values[...] = new_values
        else:
            sum_keys[...] += new_keys
            sum_values[...] += new_values
    grad_cells[:, columns_of(1)] = (sum_keys[...] * (1.0 / LOG2E)).T.astype(BF)
    grad_cells[:, columns_of(2)] = sum_values[...].T.astype(BF)


def normed_parts(hidden_f):
    inv_rms = lax.rsqrt(jnp.mean(hidden_f * hidden_f, axis=-1, keepdims=True) + 1e-6)
    normed_f = hidden_f * inv_rms
    return inv_rms, normed_f, normed_f.astype(BF)


def split_columns(target, at, values):
    for n in range(values.shape[1] // 128):
        target[at + n] = values[:, n * 128 : (n + 1) * 128]


def attend_body(
    came, qkv_w_far, grad_att_far, cotangent_far,
    payload, hidden_far, attended_far, grad_cells_far,
    qkv_w, grad_att, cotangent, hidden, qkv, attended, grad_cells,
    sum_keys, sum_values, rows_f, pieces, semaphores,
):
    start = copier(semaphores)
    load_qkv_w = start(qkv_w_far, qkv_w)
    load_grad_att = start(grad_att_far, grad_att)
    load_cotangent = start(cotangent_far, cotangent)
    chunks, long, width = came.shape
    bins = long - EXTRA
    wide = HEADS * HEAD
    pieces[...] = came[:, bins:, :].astype(F32)
    here_first = pieces[:, 2, :] + pieces[:, 3, :]
    here_last = pieces[:, 4, :] + pieces[:, 5, :]
    first = here_first + moved_down(pieces[:, 6, :] + pieces[:, 7, :])
    last = here_last + moved_up(pieces[:, 0, :] + pieces[:, 1, :])
    sigma_first, sigma_last = sigmoid(first), sigmoid(last)
    fixed_first = came[:, 0, :].astype(F32) + first * sigma_first
    fixed_last = came[:, bins - 1, :].astype(F32) + last * sigma_last
    cells = with_borders(came[:, :bins, :].astype(F32), fixed_first, fixed_last)
    hidden[...] = cells.astype(BF).reshape(chunks * bins, width)
    stores = [start(hidden, hidden_far)]
    _, _, normed = normed_parts(hidden[...].astype(F32))
    load_qkv_w.wait()
    qkv[:, :wide] = (mm(normed, qkv_w[:, :wide]) * (FACTOR * LOG2E)).astype(BF)
    qkv[:, wide:] = mm(normed, qkv_w[:, wide:]).astype(BF)
    load_grad_att.wait()

    def head(h, carry):
        one_head(h, HEADS, qkv, grad_att, attended, grad_cells, sum_keys, sum_values)
        return carry

    lax.fori_loop(0, HEADS, head, 0)
    stores += [start(grad_cells, grad_cells_far), start(attended, attended_far)]
    load_cotangent.wait()
    inv_rms, normed_f, _ = normed_parts(hidden[...].astype(F32))
    grad_normed = mm(grad_cells[...], qkv_w[...], NT)
    mixing = jnp.mean(grad_normed * normed_f, axis=-1, keepdims=True)
    grad = cotangent[...].astype(F32) + inv_rms * (grad_normed - normed_f * mixing)
    grad_b = grad.astype(BF).reshape(chunks, bins, width)
    payload[:, :bins, :] = grad_b
    rows_f[...] = grad_b.astype(F32)
    grad_first = rows_f[:, 0, :] * slope_of(first, sigma_first)
    grad_last = rows_f[:, bins - 1, :] * slope_of(last, sigma_last)
    pieces[...] = jnp.zeros(pieces.shape, F32)
    pieces[:, 0, :] = moved_down(grad_last)
    pieces[:, 1, :] = grad_first
    pieces[:, 2, :] = grad_last
    pieces[:, 3, :] = moved_up(grad_first)
    payload[:, bins:, :] = pieces[...].astype(BF)
    for store in stores:
        store.wait()


def deal(rows, core, groups):
    for n in range(rows.shape[0]):
        for e, (source, per, at) in enumerate(groups):
            begin = per * (2 * n + core) + at
            rows[n, 8 * e : 8 * e + 8, :] = source[pl.ds(begin, 8, stride=32 * per), :]


def attend_rest_body(
    hidden_far, attended_far, grad_cells_far, cotangent_far, out_w_far, slope_far, turned_far,
    enhanced, theirs, mine_far, slope, turned,
    hidden, attended, grad_cells, cotangent, out_w, mine, grads, grads_out, rows, semaphores,
):
    start = copier(semaphores)
    load_hidden, load_cells = start(hidden_far, hidden), start(grad_cells_far, grad_cells)
    loads = [
        start(attended_far, attended), start(cotangent_far, cotangent), start(out_w_far, out_w)
    ]
    ahead = [start(slope_far, slope), start(turned_far, turned)]
    load_hidden.wait()
    hidden_f = hidden[...].astype(F32)
    _, _, normed = normed_parts(hidden_f)
    load_cells.wait()
    split_columns(grads, 0, SCALE * mm(normed.T, grad_cells[...]))
    for load in loads:
        load.wait()
    split_columns(grads_out, 0, SCALE * mm(attended[...].T, cotangent[...]))
    groups = [(grads.at[n], 1, 0) for n in range(12)]
    groups += [(grads_out.at[n % 2], 2, n // 2) for n in range(4)]
    core = lax.axis_index("core")
    deal(rows, 1 - core, groups)
    theirs[...] = rows[...].astype(BF)
    deal(rows, core, groups)
    mine[...] = rows[...].astype(BF)
    store = start(mine, mine_far)
    enhanced[...] = (hidden_f + mm(attended[...], out_w[...])).astype(BF)
    for copy in ahead:
        copy.wait()
    store.wait()


def stack_back(rows, left, right):
    after = bins_after(rows, right).astype(BF)
    before = bins_before(rows, left).astype(BF)
    return jnp.concatenate([after, rows.astype(BF), before], axis=-1)


def conv_weight_body(
    came, slope, turned, early_far, edges, theirs, mine, early, stacked_far, grad_far,
    stacked, own, grads, rows, pieces, semaphores,
):
    start = copier(semaphores)
    load_early = start(early_far, early)
    frames, long, width = came.shape
    bins = long - EXTRA
    half = width // 2
    cells = frames * bins
    pieces[...] = came[:, bins:, :].astype(F32)
    own[...] = came[:, :bins, :]
    stores = [start(own, grad_far)]
    grad = own[...].astype(F32) * slope[...]
    grad = with_borders(grad, pieces[:, 1, :], pieces[:, 2, :])
    grad_b = grad.astype(BF)
    odd = lax.rem(lax.axis_index("y"), 2) == 1
    ends = []
    for frame in (0, frames - 1):
        ends.append(
            jnp.concatenate([grad_b[frame : frame + 1], came[frame : frame + 1, bins:, :]], axis=1)
        )
    edges[0] = jnp.where(odd, ends[0], ends[1])
    edges[1] = jnp.where(odd, ends[1], ends[0])
    stacked[...] = stack_back(
        grad_b.astype(F32), pieces[:, 0, :][:, None, :], pieces[:, 3, :][:, None, :]
    )
    stores.append(start(stacked, stacked_far))
    flat = stacked[...].reshape(cells, 3 * width)
    for i in range(3):
        block = mm(turned[:, i * bins : i * bins + cells], flat)
        for j in range(3):
            at = j * width
            upper = block[:half, at : at + half] + block[half:, at + half : at + width]
            lower = block[:half, at + half : at + width] - block[half:, at : at + half]
            tap = (3 * i + j) * half
            grads[tap : tap + half] = upper * SCALE
            grads[9 * half + tap : 9 * half + tap + half] = lower * SCALE
    core = lax.axis_index("core")
    groups = [(grads, 9, e) for e in range(9)]
    rows[:, 72:, :] = jnp.zeros((rows.shape[0], 8, 128), F32)
    deal(rows, 1 - core, groups)
    theirs[...] = rows[...].astype(BF)
    deal(rows, core, groups)
    mine[...] = rows[...].astype(BF)
    load_early.wait()
    for store in stores:
        store.wait()


def conv_data_body(
    grad_far, stacked_far, weight_far, total, matrix, grad, stacked, weight, semaphores
):
    start = copier(semaphores)
    load_weight, load_stacked = start(weight_far, weight), start(stacked_far, stacked)
    load_grad = start(grad_far, grad)
    frames, bins, triple = stacked.shape
    width = triple // 3
    half = width // 2
    load_weight.wait()
    for i in range(3):
        for j in range(3):
            real, imag = weight[0, i, j], weight[1, i, j]
            at = j * width
            matrix[i, :half, at : at + half] = real
            matrix[i, :half, at + half : at + width] = imag
            matrix[i, half:, at : at + half] = -imag
            matrix[i, half:, at + half : at + width] = real
    load_stacked.wait()
    load_grad.wait()
    inner = (frames - 1) * bins
    flat = stacked[...].reshape(frames * bins, triple)
    total[...] = grad[...].reshape(frames * bins, width).astype(F32) + mm(flat, matrix[1], NT)
    total[:inner] += mm(flat[bins:], matrix[0], NT)
    total[bins:] += mm(flat[:inner], matrix[2], NT)


def conv_data_finish_body(total, even_down, odd_down, matrix, out, up, down):
    sort_halos(even_down, odd_down, up, down)
    frames, bins, width = out.shape

    def stack(edge):
        extra = edge[:, bins:, :].astype(F32)
        rows = edge[:, :bins, :].astype(F32)
        return stack_back(rows, extra[:, 0:1, :], extra[:, 3:4, :])[0]

    out[...] = total[...].reshape(frames, bins, width).astype(BF)
    out[0] = (total[:bins] + mm(stack(up), matrix[2], NT)).astype(BF)
    out[frames - 1] = (total[(frames - 1) * bins :] + mm(stack(down), matrix[0], NT)).astype(BF)


def sum_body(came, out):
    total = came[0].astype(F32)
    for source in range(1, came.shape[0]):
        total = total + came[source].astype(F32)
    out[...] = total


def join_body(early, early_got, mine, got, message):
    cut = early.shape[1]
    message[:, :cut, :] = (early[...].astype(F32) + early_got[...].astype(F32)).astype(BF)
    message[:, cut:, :] = (mine[...].astype(F32) + got[...].astype(F32)).astype(BF)


def regroup_body(came, chunk, total, rows):
    sum_body(came, total)
    rows[...] = jnp.zeros(rows.shape, F32)
    for z in range(chunk.shape[0]):
        rows[z, 0:GROUPS, :] = total[pl.ds(z, GROUPS, stride=8), :]
    chunk[...] = rows[...].astype(BF)


def share_body(came, conv, qkv, out, total):
    sum_body(came, total)
    qkv[...] = total[0:12]
    out[...] = total[12:16]
    conv[...] = total[16:25]


def pair_exchanges(first, second):
    size = lax.axis_size("z") * lax.axis_size("y")
    near = [(i, i ^ 1) for i in range(size)]
    apart = [(i, i + 1 if i % 2 else i - 1) for i in range(1, size - 1)]
    return lax.ppermute(first, ("z", "y"), near), lax.ppermute(second, ("z", "y"), apart)


def exchange(array, axis):
    return lax.all_to_all(array, axis, split_axis=0, concat_axis=0, tiled=True)


def swap_cores(array):
    return lax.ppermute(array, "core", [(0, 1), (1, 0)])


def shards(spectrum, conv_weight, qkv_weight, out_weight, cotangent):
    frames, bins, width = spectrum.shape
    cells = frames * bins
    wide = HEADS * HEAD
    long = bins + EXTRA
    vmem = pltpu.VMEM
    cotangent = cotangent.reshape(cells, width)
    odd = lax.rem(lax.axis_index("y"), 2) == 1
    first, last = spectrum[:1], spectrum[frames - 1 :]
    halo_a, halo_b = pair_exchanges(jnp.where(odd, first, last), jnp.where(odd, last, first))
    tile = vmem((frames, bins, width), BF)
    tile_f = vmem((frames, bins, width), F32)
    pieces = vmem((frames, EXTRA, width), F32)
    square = vmem((cells, width), BF)
    kernels = vmem(conv_weight.shape, BF)
    halo = vmem((1, bins, width), BF)
    own, borders, matrix = kernel_call(
        conv_own_body, "conv_own",
        [
            ((cells, width), F32, "any"), ((2, frames, width), F32, "any"),
            ((3, 3 * width, width), BF, "any"),
        ],
        spectrum, conv_weight, far=(0, 1),
        scratch=[tile, kernels, vmem((frames, bins, 3 * width), BF)], copies=2, mflops=1200,
    )
    payload, slope = kernel_call(
        conv_finish_body, "conv_finish",
        [((frames, long, width), BF, "any"), ((frames, bins, width), F32, "hbm")],
        spectrum, halo_a, halo_b, own, borders, matrix, far=(0,),
        scratch=[tile, tile_f, tile_f, pieces, halo, halo], copies=2, mflops=200,
    )
    frame = exchange(payload, ("x", "core"))
    turned_shape = (width, cells + 2 * bins)
    turned, grad_att = kernel_call(
        prepare_body, "prepare",
        [(turned_shape, BF, "hbm"), ((cells, wide), BF, "hbm")],
        spectrum, halo_a, halo_b, cotangent, out_weight, far=(0, 3, 4),
        scratch=[
            tile, square, vmem((wide, width), BF), vmem(turned_shape, BF),
            vmem((cells, wide), BF), halo, halo,
        ],
        copies=5, mflops=300,
    )
    attended_v, cells_v = vmem((cells, wide), BF), vmem((cells, 3 * wide), BF)
    back, hidden, attended, grad_cells = kernel_call(
        attend_body, "attend",
        [
            ((frames, long, width), BF, "any"), ((cells, width), BF, "hbm"),
            ((cells, wide), BF, "hbm"), ((cells, 3 * wide), BF, "hbm"),
        ],
        frame, qkv_weight, grad_att, cotangent, far=(1, 2, 3),
        scratch=[
            vmem((width, 3 * wide), BF), attended_v, square, square, cells_v, attended_v, cells_v,
            vmem((HEAD, cells), F32), vmem((HEAD, cells), F32), tile_f, pieces,
        ],
        copies=6, mflops=15000,
    )
    grads = exchange(back, ("x", "core"))
    ring = lax.axis_size("y") * lax.axis_size("x")
    early_shape = (ring, 8 * EARLY, 128)
    late_shape = (ring, 8 * (GROUPS - EARLY), 128)
    enhanced, theirs, mine, slope, turned = kernel_call(
        attend_rest_body, "attend_rest",
        [
            ((cells, width), BF, "any"), (early_shape, BF, "any"), (early_shape, BF, "hbm"),
            ((frames, bins, width), F32, "vmem"), (turned_shape, BF, "vmem"),
        ],
        hidden, attended, grad_cells, cotangent, out_weight, slope, turned,
        far=(0, 1, 2, 3, 4, 5, 6),
        scratch=[
            square, attended_v, cells_v, square, vmem((wide, width), BF), vmem(early_shape, BF),
            vmem((12, width, HEAD), F32), vmem((2, wide, HEAD), F32), vmem(early_shape, F32),
        ],
        copies=8, mflops=1500, limit=40,
    )
    theirs, grads = lax.optimization_barrier((theirs, grads))
    got = swap_cores(theirs)
    stacked_shape = (frames, bins, 3 * width)
    edges, theirs, late_mine, early, stacked, grad_tile = kernel_call(
        conv_weight_body, "conv_weight_grad",
        [
            ((2, 1, long, width), BF, "any"), (late_shape, BF, "any"), (late_shape, BF, "any"),
            (early_shape, BF, "any"), (stacked_shape, BF, "hbm"),
            ((frames, bins, width), BF, "hbm"),
        ],
        grads, slope, turned, mine, far=(3,),
        scratch=[
            vmem(stacked_shape, BF), tile,
            vmem((18 * (width // 2), width // 2), F32), vmem(late_shape, F32), pieces,
        ],
        copies=3, mflops=1200, limit=40,
    )
    late_got = swap_cores(theirs)
    edges, late_got = lax.optimization_barrier((edges, late_got))
    (message,) = kernel_call(
        join_body, "join", [((ring, 8 * GROUPS, 128), BF, "any")], early, got, late_mine,
        late_got,
    )
    late = exchange(message, ("y", "x"))
    edge_a, edge_b = pair_exchanges(edges[0], edges[1])
    total, matrix_back = kernel_call(
        conv_data_body, "conv_data",
        [((cells, width), F32, "any"), ((3, width, 3 * width), BF, "any")],
        grad_tile, stacked, conv_weight, far=(0, 1, 2),
        scratch=[tile, vmem(stacked_shape, BF), kernels], copies=3, mflops=1200,
    )
    (grad_spectrum,) = kernel_call(
        conv_data_finish_body, "conv_data_finish", [((frames, bins, width), BF, "any")],
        total, edge_a, edge_b, matrix_back,
        scratch=[vmem((1, long, width), BF), vmem((1, long, width), BF)], mflops=100,
    )
    late, grad_spectrum = lax.optimization_barrier((late, grad_spectrum))
    (chunk,) = kernel_call(
        regroup_body, "regroup", [((lax.axis_size("z"), 32, 128), BF, "any")],
        late,
        scratch=[vmem(late.shape[1:], F32), vmem((lax.axis_size("z"), 32, 128), F32)],
    )
    shares = kernel_call(
        share_body, "share", [((9, 128), F32, "any"), ((12, 128), F32, "any"), ((4, 128), F32, "any")],
        exchange(chunk, "z"),
        scratch=[vmem((32, 128), F32)],
    )
    return (enhanced.reshape(1, cells, width), grad_spectrum, *[s.reshape(-1) for s in shares])


def solution(mesh):
    mesh = Mesh(mesh.devices.reshape(8, 4, 4, 2), ("z", "y", "x", "core"))
    every = P(("z", "y", "x", "core"))
    tiles, rows = P(("z", "y"), ("x", "core"), None), P(("z", "y", "x", "core"), None, None)
    return jax.shard_map(
        shards,
        mesh=mesh,
        in_specs=(tiles, P(), P(), P(), rows),
        out_specs=(rows, tiles, every, every, every),
        check_vma=False,
    )
```

```python
import math

import jax
import jax.numpy as jnp
from jax import lax
from jax.experimental import pallas as pl
from jax.experimental.pallas import tpu as pltpu
from jax.sharding import Mesh
from jax.sharding import PartitionSpec as P

HEADS = 4
HEAD = 128
EXTRA = 16
SCALE = 1.0 / 512
LOG2E = math.log2(math.e)
FACTOR = 1.0 / math.sqrt(HEAD)
BF = jnp.bfloat16
F32 = jnp.float32
NN = (((1,), (0,)), ((), ()))
NT = (((1,), (1,)), ((), ()))
QUERY_BLOCK = 1024
GROUPS = 26
EARLY = 16


def mm(a, b, dims=NN):
    return lax.dot_general(a, b, dims, preferred_element_type=F32)


PLACES = {"any": jax.ShapeDtypeStruct, "hbm": pltpu.HBM, "vmem": pltpu.VMEM}


def kernel_call(body, name, outs, *args, far=(), scratch=(), copies=0, mflops=0, limit=48):
    shapes = [
        PLACES[away](dims, kind) for dims, kind, away in outs
    ]
    args = [
        pltpu.with_memory_space_constraint(a, pltpu.HBM) if n in far else a
        for n, a in enumerate(args)
    ]
    size = sum(math.prod(a.shape) * a.dtype.itemsize for a in (*args, *shapes))
    near, hbm = pl.BlockSpec(memory_space=pltpu.VMEM), pl.BlockSpec(memory_space=pltpu.HBM)
    scratch = list(scratch) + ([pltpu.SemaphoreType.DMA((copies,))] if copies else [])
    return pl.pallas_call(
        body,
        out_shape=shapes,
        in_specs=[hbm if n in far else near for n in range(len(args))],
        out_specs=[hbm if away == "hbm" else near for _, _, away in outs],
        scratch_shapes=scratch,
        compiler_params=pltpu.CompilerParams(vmem_limit_bytes=limit * 2**20),
        cost_estimate=pl.CostEstimate(
            flops=mflops * 10**6, bytes_accessed=size, transcendentals=0
        ),
        name=name,
    )(*args)


def copier(semaphores):
    started = []

    def start(source, target):
        copy = pltpu.make_async_copy(source, target, semaphores.at[len(started)])
        copy.start()
        started.append(copy)
        return copy

    return start


def sigmoid(v):
    return 1.0 / (1.0 + jnp.exp(-v))


def slope_of(v, sigma):
    return sigma * (1.0 + v * (1.0 - sigma))


def moved_down(rows):
    at = lax.broadcasted_iota(jnp.int32, rows.shape, 0)
    return jnp.where(at == 0, 0.0, pltpu.roll(rows, 1, 0))


def moved_up(rows):
    last = rows.shape[0] - 1
    at = lax.broadcasted_iota(jnp.int32, rows.shape, 0)
    return jnp.where(at == last, 0.0, pltpu.roll(rows, last, 0))


def with_borders(inner, first, last):
    at = lax.broadcasted_iota(jnp.int32, inner.shape, 1)
    inner = jnp.where(at == 0, first[:, None, :], inner)
    return jnp.where(at == inner.shape[1] - 1, last[:, None, :], inner)


def bins_before(rows, left):
    at = lax.broadcasted_iota(jnp.int32, rows.shape, 1)
    return jnp.where(at == 0, left, pltpu.roll(rows, 1, 1))


def bins_after(rows, right):
    last = rows.shape[1] - 1
    at = lax.broadcasted_iota(jnp.int32, rows.shape, 1)
    return jnp.where(at == last, right, pltpu.roll(rows, last, 1))


def sort_halos(even_down, odd_down, up, down):
    odd = lax.rem(lax.axis_index("y"), 2) == 1
    first, second = even_down[...], odd_down[...]
    up[...] = jnp.where(odd, first, second)
    down[...] = jnp.where(odd, second, first)


def conv_own_body(mid_far, weight_far, conv, borders, matrix, mid, weight, stacked, semaphores):
    start = copier(semaphores)
    load_weight, load_mid = start(weight_far, weight), start(mid_far, mid)
    frames, bins, width = mid.shape
    half = width // 2
    load_weight.wait()
    for i in range(3):
        for j in range(3):
            real, imag = weight[0, i, j], weight[1, i, j]
            at = j * width
            matrix[i, at : at + half, :half] = real
            matrix[i, at : at + half, half:] = imag
            matrix[i, at + half : at + width, :half] = -imag
            matrix[i, at + half : at + width, half:] = real
    load_mid.wait()
    wide = mid[...].astype(F32)
    stacked[:, :, :width] = bins_before(wide, 0.0).astype(BF)
    stacked[:, :, width : 2 * width] = mid[...]
    stacked[:, :, 2 * width :] = bins_after(wide, 0.0).astype(BF)
    inner = (frames - 1) * bins
    everything = stacked[...].reshape(frames * bins, 3 * width)
    conv[...] = mm(everything, matrix[1])
    conv[bins:] += mm(everything[:inner], matrix[0])
    conv[:inner] += mm(everything[bins:], matrix[2])
    borders[0] = mid[:, 0, :].astype(F32)
    borders[1] = mid[:, bins - 1, :].astype(F32)


def conv_finish_body(
    mid_far, even_down, odd_down, own, borders, matrix,
    payload, conv, mid, pieces, up, down, semaphores,
):
    start = copier(semaphores)
    load_mid = start(mid_far, mid)
    sort_halos(even_down, odd_down, up, down)
    frames, bins, width = mid.shape

    def stack(row):
        wide = row[...].astype(F32)
        before = bins_before(wide, 0.0).astype(BF)
        after = bins_after(wide, 0.0).astype(BF)
        return jnp.concatenate([before[0], row[0], after[0]], axis=1)

    conv[...] = own[...].reshape(frames, bins, width)
    conv[0] += mm(stack(up), matrix[0])
    conv[frames - 1] += mm(stack(down), matrix[2])

    def beyond(bin_at, side, tap):
        rows = jnp.concatenate(
            [up[:, bin_at, :].astype(F32), borders[side], down[:, bin_at, :].astype(F32)], axis=0
        )
        total = None
        for i in range(3):
            term = mm(
                rows[i : i + frames].astype(BF), matrix[i, tap * width : (tap + 1) * width, :]
            )
            total = term if total is None else total + term
        return total

    parts = (
        beyond(0, 0, 2),
        conv[:, 0, :],
        conv[:, bins - 1, :],
        beyond(bins - 1, 1, 0),
    )
    pieces[...] = jnp.zeros(pieces.shape, F32)
    for at, part in enumerate(parts):
        high = part.astype(BF).astype(F32)
        pieces[:, 2 * at, :] = high
        pieces[:, 2 * at + 1, :] = part - high
    values = conv[...]
    sigma = sigmoid(values)
    load_mid.wait()
    hidden = mid[...].astype(F32) + values * sigma
    payload[:, :bins, :] = with_borders(hidden, borders[0], borders[1]).astype(BF)
    payload[:, bins:, :] = pieces[...].astype(BF)


def prepare_body(
    conv, mid_far, even_down, odd_down, cotangent_far, out_w_far,
    turned_far, grad_att_far, slope_far,
    slope, mid, cotangent, out_w, turned, grad_att, up, down, semaphores,
):
    start = copier(semaphores)
    loads = start(mid_far, mid), start(cotangent_far, cotangent), start(out_w_far, out_w)
    sort_halos(even_down, odd_down, up, down)
    slope[...] = slope_of(conv[...], sigmoid(conv[...]))
    stores = [start(slope, slope_far)]
    for load in loads:
        load.wait()
    frames, bins, width = mid.shape
    turned[:, :bins] = up[0].T
    turned[:, bins : (frames + 1) * bins] = mid[...].reshape(frames * bins, width).T
    turned[:, (frames + 1) * bins :] = down[0].T
    grad_att[...] = mm(cotangent[...], out_w[...], NT).astype(BF)
    stores += [start(turned, turned_far), start(grad_att, grad_att_far)]
    for store in stores:
        store.wait()


def columns(part, h, heads=HEADS):
    at = (part * heads + h) * HEAD
    if not isinstance(h, int):
        at = pl.multiple_of(at, HEAD)
    return pl.ds(at, HEAD)


def one_head(h, heads, qkv, grad_att, attended, grad_cells, sum_keys, sum_values):
    def columns_of(part):
        return columns(part, h, heads)

    cells = qkv.shape[0]
    keys = qkv[:, columns_of(1)]
    values = qkv[:, columns_of(2)]
    values_ones = jnp.concatenate([values, jnp.ones((cells, HEAD), BF)], axis=1)
    for block in range(cells // QUERY_BLOCK):
        rows = slice(block * QUERY_BLOCK, (block + 1) * QUERY_BLOCK)
        queries = qkv[rows, columns_of(0)]
        scores = mm(queries, keys, NT)
        raised = jnp.exp2(scores - jnp.max(scores, axis=-1, keepdims=True))
        raised_b = raised.astype(BF)
        sums = mm(raised_b, values_ones)
        inverse = 1.0 / sums[:, HEAD:]
        result = sums[:, :HEAD] * inverse
        attended[rows, columns_of(0)] = result.astype(BF)
        scaled = grad_att[rows, columns_of(0)].astype(F32) * inverse
        inner = jnp.sum(scaled * result, axis=-1, keepdims=True)
        scaled_b = scaled.astype(BF)
        grad_probs = mm(scaled_b, values, NT)
        grad_scores = (raised * (grad_probs - inner)).astype(BF)
        grad_cells[rows, columns_of(0)] = (mm(grad_scores, keys) * FACTOR).astype(BF)
        new_keys = mm(queries.T, grad_scores)
        new_values = mm(scaled_b.T, raised_b)
        if block == 0:
            sum_keys[...] = new_keys
            sum_values[...] = new_values
        else:
            sum_keys[...] += new_keys
            sum_values[...] += new_values
    grad_cells[:, columns_of(1)] = (sum_keys[...] * (1.0 / LOG2E)).T.astype(BF)
    grad_cells[:, columns_of(2)] = sum_values[...].T.astype(BF)


def normed_parts(hidden_f):
    inv_rms = lax.rsqrt(jnp.mean(hidden_f * hidden_f, axis=-1, keepdims=True) + 1e-6)
    normed_f = hidden_f * inv_rms
    return inv_rms, normed_f, normed_f.astype(BF)


def split_columns(target, at, values):
    for n in range(values.shape[1] // 128):
        target[at + n] = values[:, n * 128 : (n + 1) * 128]


def attend_body(
    came, qkv_w_far, grad_att_far, cotangent_far,
    payload, hidden_far, attended_far, grad_cells_far,
    qkv_w, grad_att, cotangent, hidden, qkv, attended, grad_cells,
    sum_keys, sum_values, pieces, semaphores,
):
    start = copier(semaphores)
    load_qkv_w = start(qkv_w_far, qkv_w)
    load_grad_att = start(grad_att_far, grad_att)
    load_cotangent = start(cotangent_far, cotangent)
    chunks, long, width = came.shape
    bins = long - EXTRA
    wide = HEADS * HEAD
    pieces[...] = came[:, bins:, :].astype(F32)
    here_first = pieces[:, 2, :] + pieces[:, 3, :]
    here_last = pieces[:, 4, :] + pieces[:, 5, :]
    first = here_first + moved_down(pieces[:, 6, :] + pieces[:, 7, :])
    last = here_last + moved_up(pieces[:, 0, :] + pieces[:, 1, :])
    sigma_first, sigma_last = sigmoid(first), sigmoid(last)
    fixed_first = came[:, 0, :].astype(F32) + first * sigma_first
    fixed_last = came[:, bins - 1, :].astype(F32) + last * sigma_last
    cells = with_borders(came[:, :bins, :].astype(F32), fixed_first, fixed_last)
    hidden[...] = cells.astype(BF).reshape(chunks * bins, width)
    stores = [start(hidden, hidden_far)]
    _, _, normed = normed_parts(hidden[...].astype(F32))
    load_qkv_w.wait()
    qkv[:, :wide] = (mm(normed, qkv_w[:, :wide]) * (FACTOR * LOG2E)).astype(BF)
    qkv[:, wide:] = mm(normed, qkv_w[:, wide:]).astype(BF)
    load_grad_att.wait()

    def head(h, carry):
        one_head(h, HEADS, qkv, grad_att, attended, grad_cells, sum_keys, sum_values)
        return carry

    lax.fori_loop(0, HEADS, head, 0)
    stores += [start(grad_cells, grad_cells_far), start(attended, attended_far)]
    load_cotangent.wait()
    inv_rms, normed_f, _ = normed_parts(hidden[...].astype(F32))
    grad_normed = mm(grad_cells[...], qkv_w[...], NT)
    mixing = jnp.mean(grad_normed * normed_f, axis=-1, keepdims=True)
    grad = cotangent[...].astype(F32) + inv_rms * (grad_normed - normed_f * mixing)
    grad_b = grad.astype(BF).reshape(chunks, bins, width)
    payload[:, :bins, :] = grad_b
    grad_first = payload[:, 0, :].astype(F32) * slope_of(first, sigma_first)
    grad_last = payload[:, bins - 1, :].astype(F32) * slope_of(last, sigma_last)
    pieces[...] = jnp.zeros(pieces.shape, F32)
    pieces[:, 0, :] = moved_down(grad_last)
    pieces[:, 1, :] = grad_first
    pieces[:, 2, :] = grad_last
    pieces[:, 3, :] = moved_up(grad_first)
    payload[:, bins:, :] = pieces[...].astype(BF)
    for store in stores:
        store.wait()


def deal(rows, core, groups):
    for n in range(rows.shape[0]):
        for e, (source, per, at) in enumerate(groups):
            begin = per * (2 * n + core) + at
            rows[n, 8 * e : 8 * e + 8, :] = source[pl.ds(begin, 8, stride=32 * per), :]


def attend_rest_body(
    hidden_far, attended_far, grad_cells_far, cotangent_far, out_w_far, slope_far, turned_far,
    enhanced, theirs, mine_far, slope, turned,
    hidden, attended, grad_cells, cotangent, out_w, mine, grads, grads_out, rows, semaphores,
):
    start = copier(semaphores)
    load_hidden, load_cells = start(hidden_far, hidden), start(grad_cells_far, grad_cells)
    loads = [
        start(attended_far, attended), start(cotangent_far, cotangent), start(out_w_far, out_w)
    ]
    ahead = [start(slope_far, slope), start(turned_far, turned)]
    load_hidden.wait()
    hidden_f = hidden[...].astype(F32)
    _, _, normed = normed_parts(hidden_f)
    load_cells.wait()
    split_columns(grads, 0, SCALE * mm(normed.T, grad_cells[...]))
    for load in loads:
        load.wait()
    split_columns(grads_out, 0, SCALE * mm(attended[...].T, cotangent[...]))
    groups = [(grads.at[n], 1, 0) for n in range(12)]
    groups += [(grads_out.at[n % 2], 2, n // 2) for n in range(4)]
    core = lax.axis_index("core")
    deal(rows, 1 - core, groups)
    theirs[...] = rows[...].astype(BF)
    deal(rows, core, groups)
    mine[...] = rows[...].astype(BF)
    store = start(mine, mine_far)
    enhanced[...] = (hidden_f + mm(attended[...], out_w[...])).astype(BF)
    for copy in ahead:
        copy.wait()
    store.wait()


def stack_back(rows, left, right):
    after = bins_after(rows, right).astype(BF)
    before = bins_before(rows, left).astype(BF)
    return jnp.concatenate([after, rows.astype(BF), before], axis=-1)


def conv_weight_body(
    came, slope, turned, early_far, edges, theirs, mine, early, stacked_far, grad_far,
    stacked, own, grads, rows, pieces, semaphores,
):
    start = copier(semaphores)
    load_early = start(early_far, early)
    frames, long, width = came.shape
    bins = long - EXTRA
    half = width // 2
    cells = frames * bins
    pieces[...] = came[:, bins:, :].astype(F32)
    own[...] = came[:, :bins, :]
    stores = [start(own, grad_far)]
    grad = own[...].astype(F32) * slope[...]
    grad = with_borders(grad, pieces[:, 1, :], pieces[:, 2, :])
    grad_b = grad.astype(BF)
    odd = lax.rem(lax.axis_index("y"), 2) == 1
    ends = []
    for frame in (0, frames - 1):
        ends.append(
            jnp.concatenate([grad_b[frame : frame + 1], came[frame : frame + 1, bins:, :]], axis=1)
        )
    edges[0] = jnp.where(odd, ends[0], ends[1])
    edges[1] = jnp.where(odd, ends[1], ends[0])
    stacked[...] = stack_back(
        grad_b.astype(F32), pieces[:, 0, :][:, None, :], pieces[:, 3, :][:, None, :]
    )
    stores.append(start(stacked, stacked_far))
    flat = stacked[...].reshape(cells, 3 * width)
    for i in range(3):
        block = mm(turned[:, i * bins : i * bins + cells], flat)
        for j in range(3):
            at = j * width
            upper = block[:half, at : at + half] + block[half:, at + half : at + width]
            lower = block[:half, at + half : at + width] - block[half:, at : at + half]
            tap = (3 * i + j) * half
            grads[tap : tap + half] = upper * SCALE
            grads[9 * half + tap : 9 * half + tap + half] = lower * SCALE
    core = lax.axis_index("core")
    groups = [(grads, 9, e) for e in range(9)]
    rows[:, 72:, :] = jnp.zeros((rows.shape[0], 8, 128), F32)
    deal(rows, 1 - core, groups)
    theirs[...] = rows[...].astype(BF)
    deal(rows, core, groups)
    mine[...] = rows[...].astype(BF)
    load_early.wait()
    for store in stores:
        store.wait()


def conv_data_body(
    grad_far, stacked_far, weight_far, total, matrix, grad, stacked, weight, semaphores
):
    start = copier(semaphores)
    load_weight, load_stacked = start(weight_far, weight), start(stacked_far, stacked)
    load_grad = start(grad_far, grad)
    frames, bins, triple = stacked.shape
    width = triple // 3
    half = width // 2
    load_weight.wait()
    for i in range(3):
        for j in range(3):
            real, imag = weight[0, i, j], weight[1, i, j]
            at = j * width
            matrix[i, :half, at : at + half] = real
            matrix[i, :half, at + half : at + width] = imag
            matrix[i, half:, at : at + half] = -imag
            matrix[i, half:, at + half : at + width] = real
    load_stacked.wait()
    load_grad.wait()
    inner = (frames - 1) * bins
    flat = stacked[...].reshape(frames * bins, triple)
    total[...] = grad[...].reshape(frames * bins, width).astype(F32) + mm(flat, matrix[1], NT)
    total[:inner] += mm(flat[bins:], matrix[0], NT)
    total[bins:] += mm(flat[:inner], matrix[2], NT)


def conv_data_finish_body(total, even_down, odd_down, matrix, out, up, down):
    sort_halos(even_down, odd_down, up, down)
    frames, bins, width = out.shape

    def stack(edge):
        extra = edge[:, bins:, :].astype(F32)
        rows = edge[:, :bins, :].astype(F32)
        return stack_back(rows, extra[:, 0:1, :], extra[:, 3:4, :])[0]

    out[...] = total[...].reshape(frames, bins, width).astype(BF)
    out[0] = (total[:bins] + mm(stack(up), matrix[2], NT)).astype(BF)
    out[frames - 1] = (total[(frames - 1) * bins :] + mm(stack(down), matrix[0], NT)).astype(BF)


def sum_body(came, out):
    total = came[0].astype(F32)
    for source in range(1, came.shape[0]):
        total = total + came[source].astype(F32)
    out[...] = total


def join_body(early, early_got, mine, got, message):
    cut = early.shape[1]
    message[:, :cut, :] = (early[...].astype(F32) + early_got[...].astype(F32)).astype(BF)
    message[:, cut:, :] = (mine[...].astype(F32) + got[...].astype(F32)).astype(BF)


def regroup_body(came, chunk, total, rows):
    sum_body(came, total)
    rows[...] = jnp.zeros(rows.shape, F32)
    for z in range(chunk.shape[0]):
        rows[z, 0:GROUPS, :] = total[pl.ds(z, GROUPS, stride=8), :]
    chunk[...] = rows[...].astype(BF)


def share_body(came, conv, qkv, out, total):
    sum_body(came, total)
    qkv[...] = total[0:12]
    out[...] = total[12:16]
    conv[...] = total[16:25]


def pair_exchanges(first, second):
    size = lax.axis_size("z") * lax.axis_size("y")
    near = [(i, i ^ 1) for i in range(size)]
    apart = [(i, i + 1 if i % 2 else i - 1) for i in range(1, size - 1)]
    return lax.ppermute(first, ("z", "y"), near), lax.ppermute(second, ("z", "y"), apart)


def exchange(array, axis):
    return lax.all_to_all(array, axis, split_axis=0, concat_axis=0, tiled=True)


def swap_cores(array):
    return lax.ppermute(array, "core", [(0, 1), (1, 0)])


def shards(spectrum, conv_weight, qkv_weight, out_weight, cotangent):
    frames, bins, width = spectrum.shape
    cells = frames * bins
    wide = HEADS * HEAD
    long = bins + EXTRA
    vmem = pltpu.VMEM
    cotangent = cotangent.reshape(cells, width)
    odd = lax.rem(lax.axis_index("y"), 2) == 1
    first, last = spectrum[:1], spectrum[frames - 1 :]
    halo_a, halo_b = pair_exchanges(jnp.where(odd, first, last), jnp.where(odd, last, first))
    tile = vmem((frames, bins, width), BF)
    tile_f = vmem((frames, bins, width), F32)
    pieces = vmem((frames, EXTRA, width), F32)
    square = vmem((cells, width), BF)
    kernels = vmem(conv_weight.shape, BF)
    halo = vmem((1, bins, width), BF)
    own, borders, matrix = kernel_call(
        conv_own_body, "conv_own",
        [
            ((cells, width), F32, "any"), ((2, frames, width), F32, "any"),
            ((3, 3 * width, width), BF, "any"),
        ],
        spectrum, conv_weight, far=(0, 1),
        scratch=[tile, kernels, vmem((frames, bins, 3 * width), BF)], copies=2, mflops=1200,
    )
    payload, conv = kernel_call(
        conv_finish_body, "conv_finish",
        [((frames, long, width), BF, "any"), ((frames, bins, width), F32, "vmem")],
        spectrum, halo_a, halo_b, own, borders, matrix, far=(0,),
        scratch=[tile, pieces, halo, halo], copies=1, mflops=200,
    )
    frame = exchange(payload, ("x", "core"))
    turned_shape = (width, cells + 2 * bins)
    turned, grad_att, slope = kernel_call(
        prepare_body, "prepare",
        [
            (turned_shape, BF, "hbm"), ((cells, wide), BF, "hbm"),
            ((frames, bins, width), F32, "hbm"),
        ],
        conv, spectrum, halo_a, halo_b, cotangent, out_weight, far=(1, 4, 5),
        scratch=[
            tile_f, tile, square, vmem((wide, width), BF), vmem(turned_shape, BF),
            vmem((cells, wide), BF), halo, halo,
        ],
        copies=6, mflops=300,
    )
    attended_v, cells_v = vmem((cells, wide), BF), vmem((cells, 3 * wide), BF)
    back, hidden, attended, grad_cells = kernel_call(
        attend_body, "attend",
        [
            ((frames, long, width), BF, "any"), ((cells, width), BF, "hbm"),
            ((cells, wide), BF, "hbm"), ((cells, 3 * wide), BF, "hbm"),
        ],
        frame, qkv_weight, grad_att, cotangent, far=(1, 2, 3),
        scratch=[
            vmem((width, 3 * wide), BF), attended_v, square, square, cells_v, attended_v, cells_v,
            vmem((HEAD, cells), F32), vmem((HEAD, cells), F32), pieces,
        ],
        copies=6, mflops=15000,
    )
    grads = exchange(back, ("x", "core"))
    ring = lax.axis_size("y") * lax.axis_size("x")
    early_shape = (ring, 8 * EARLY, 128)
    late_shape = (ring, 8 * (GROUPS - EARLY), 128)
    enhanced, theirs, mine, slope, turned = kernel_call(
        attend_rest_body, "attend_rest",
        [
            ((cells, width), BF, "any"), (early_shape, BF, "any"), (early_shape, BF, "hbm"),
            ((frames, bins, width), F32, "vmem"), (turned_shape, BF, "vmem"),
        ],
        hidden, attended, grad_cells, cotangent, out_weight, slope, turned,
        far=(0, 1, 2, 3, 4, 5, 6),
        scratch=[
            square, attended_v, cells_v, square, vmem((wide, width), BF), vmem(early_shape, BF),
            vmem((12, width, HEAD), F32), vmem((2, wide, HEAD), F32), vmem(early_shape, F32),
        ],
        copies=8, mflops=1500, limit=40,
    )
    theirs, grads = lax.optimization_barrier((theirs, grads))
    got = swap_cores(theirs)
    stacked_shape = (frames, bins, 3 * width)
    edges, theirs, late_mine, early, stacked, grad_tile = kernel_call(
        conv_weight_body, "conv_weight_grad",
        [
            ((2, 1, long, width), BF, "any"), (late_shape, BF, "any"), (late_shape, BF, "any"),
            (early_shape, BF, "any"), (stacked_shape, BF, "hbm"),
            ((frames, bins, width), BF, "hbm"),
        ],
        grads, slope, turned, mine, far=(3,),
        scratch=[
            vmem(stacked_shape, BF), tile,
            vmem((18 * (width // 2), width // 2), F32), vmem(late_shape, F32), pieces,
        ],
        copies=3, mflops=1200, limit=40,
    )
    late_got = swap_cores(theirs)
    (message,) = kernel_call(
        join_body, "join", [((ring, 8 * GROUPS, 128), BF, "any")], early, got, late_mine,
        late_got,
    )
    late = exchange(message, ("y", "x"))
    total, matrix_back = kernel_call(
        conv_data_body, "conv_data",
        [((cells, width), F32, "vmem"), ((3, width, 3 * width), BF, "vmem")],
        grad_tile, stacked, conv_weight, far=(0, 1, 2),
        scratch=[tile, vmem(stacked_shape, BF), kernels], copies=3, mflops=1200,
    )
    late, total = lax.optimization_barrier((late, total))
    (chunk,) = kernel_call(
        regroup_body, "regroup", [((lax.axis_size("z"), 32, 128), BF, "any")],
        late,
        scratch=[vmem(late.shape[1:], F32), vmem((lax.axis_size("z"), 32, 128), F32)],
    )
    chunk, edges = lax.optimization_barrier((chunk, edges))
    edge_a, edge_b = pair_exchanges(edges[0], edges[1])
    (grad_spectrum,) = kernel_call(
        conv_data_finish_body, "conv_data_finish", [((frames, bins, width), BF, "any")],
        total, edge_a, edge_b, matrix_back,
        scratch=[vmem((1, long, width), BF), vmem((1, long, width), BF)], mflops=100,
    )
    shares = kernel_call(
        share_body, "share", [((9, 128), F32, "any"), ((12, 128), F32, "any"), ((4, 128), F32, "any")],
        exchange(chunk, "z"),
        scratch=[vmem((32, 128), F32)],
    )
    return (enhanced.reshape(1, cells, width), grad_spectrum, *[s.reshape(-1) for s in shares])


def solution(mesh):
    mesh = Mesh(mesh.devices.reshape(8, 4, 4, 2), ("z", "y", "x", "core"))
    every = P(("z", "y", "x", "core"))
    tiles, rows = P(("z", "y"), ("x", "core"), None), P(("z", "y", "x", "core"), None, None)
    return jax.shard_map(
        shards,
        mesh=mesh,
        in_specs=(tiles, P(), P(), P(), rows),
        out_specs=(rows, tiles, every, every, every),
        check_vma=False,
    )
```

```python
import math

import jax
import jax.numpy as jnp
from jax import lax
from jax.experimental import pallas as pl
from jax.experimental.pallas import tpu as pltpu
from jax.sharding import Mesh
from jax.sharding import PartitionSpec as P

HEADS = 4
HEAD = 128
EXTRA = 16
SCALE = 1.0 / 512
LOG2E = math.log2(math.e)
FACTOR = 1.0 / math.sqrt(HEAD)
BF = jnp.bfloat16
F32 = jnp.float32
NN = (((1,), (0,)), ((), ()))
NT = (((1,), (1,)), ((), ()))
QUERY_BLOCK = 1024
GROUPS = 26
EARLY = 16


def mm(a, b, dims=NN):
    return lax.dot_general(a, b, dims, preferred_element_type=F32)


PLACES = {"any": jax.ShapeDtypeStruct, "hbm": pltpu.HBM, "vmem": pltpu.VMEM}


def kernel_call(body, name, outs, *args, far=(), scratch=(), copies=0, mflops=0, limit=48):
    shapes = [
        PLACES[away](dims, kind) for dims, kind, away in outs
    ]
    args = [
        pltpu.with_memory_space_constraint(a, pltpu.HBM) if n in far else a
        for n, a in enumerate(args)
    ]
    size = sum(math.prod(a.shape) * a.dtype.itemsize for a in (*args, *shapes))
    near, hbm = pl.BlockSpec(memory_space=pltpu.VMEM), pl.BlockSpec(memory_space=pltpu.HBM)
    scratch = list(scratch) + ([pltpu.SemaphoreType.DMA((copies,))] if copies else [])
    return pl.pallas_call(
        body,
        out_shape=shapes,
        in_specs=[hbm if n in far else near for n in range(len(args))],
        out_specs=[hbm if away == "hbm" else near for _, _, away in outs],
        scratch_shapes=scratch,
        compiler_params=pltpu.CompilerParams(vmem_limit_bytes=limit * 2**20),
        cost_estimate=pl.CostEstimate(
            flops=mflops * 10**6, bytes_accessed=size, transcendentals=0
        ),
        name=name,
    )(*args)


def copier(semaphores):
    started = []

    def start(source, target):
        copy = pltpu.make_async_copy(source, target, semaphores.at[len(started)])
        copy.start()
        started.append(copy)
        return copy

    return start


def sigmoid(v):
    return 1.0 / (1.0 + jnp.exp(-v))


def slope_of(v, sigma):
    return sigma * (1.0 + v * (1.0 - sigma))


def moved_down(rows):
    at = lax.broadcasted_iota(jnp.int32, rows.shape, 0)
    return jnp.where(at == 0, 0.0, pltpu.roll(rows, 1, 0))


def moved_up(rows):
    last = rows.shape[0] - 1
    at = lax.broadcasted_iota(jnp.int32, rows.shape, 0)
    return jnp.where(at == last, 0.0, pltpu.roll(rows, last, 0))


def with_borders(inner, first, last):
    at = lax.broadcasted_iota(jnp.int32, inner.shape, 1)
    inner = jnp.where(at == 0, first[:, None, :], inner)
    return jnp.where(at == inner.shape[1] - 1, last[:, None, :], inner)


def bins_before(rows, left):
    at = lax.broadcasted_iota(jnp.int32, rows.shape, 1)
    return jnp.where(at == 0, left, pltpu.roll(rows, 1, 1))


def bins_after(rows, right):
    last = rows.shape[1] - 1
    at = lax.broadcasted_iota(jnp.int32, rows.shape, 1)
    return jnp.where(at == last, right, pltpu.roll(rows, last, 1))


def sort_halos(even_down, odd_down, up, down):
    odd = lax.rem(lax.axis_index("y"), 2) == 1
    first, second = even_down[...], odd_down[...]
    up[...] = jnp.where(odd, first, second)
    down[...] = jnp.where(odd, second, first)


def conv_own_body(mid_far, weight_far, conv, borders, matrix, mid, weight, stacked, semaphores):
    start = copier(semaphores)
    load_weight, load_mid = start(weight_far, weight), start(mid_far, mid)
    frames, bins, width = mid.shape
    half = width // 2
    load_weight.wait()
    for i in range(3):
        for j in range(3):
            real, imag = weight[0, i, j], weight[1, i, j]
            at = j * width
            matrix[i, at : at + half, :half] = real
            matrix[i, at : at + half, half:] = imag
            matrix[i, at + half : at + width, :half] = -imag
            matrix[i, at + half : at + width, half:] = real
    load_mid.wait()
    wide = mid[...].astype(F32)
    stacked[:, :, :width] = bins_before(wide, 0.0).astype(BF)
    stacked[:, :, width : 2 * width] = mid[...]
    stacked[:, :, 2 * width :] = bins_after(wide, 0.0).astype(BF)
    inner = (frames - 1) * bins
    everything = stacked[...].reshape(frames * bins, 3 * width)
    conv[...] = mm(everything, matrix[1])
    conv[bins:] += mm(everything[:inner], matrix[0])
    conv[:inner] += mm(everything[bins:], matrix[2])
    borders[0] = mid[:, 0, :].astype(F32)
    borders[1] = mid[:, bins - 1, :].astype(F32)


def conv_finish_body(
    mid_far, even_down, odd_down, own, borders, matrix,
    payload, conv, mid, pieces, up, down, semaphores,
):
    start = copier(semaphores)
    load_mid = start(mid_far, mid)
    sort_halos(even_down, odd_down, up, down)
    frames, bins, width = mid.shape

    def stack(row):
        wide = row[...].astype(F32)
        before = bins_before(wide, 0.0).astype(BF)
        after = bins_after(wide, 0.0).astype(BF)
        return jnp.concatenate([before[0], row[0], after[0]], axis=1)

    conv[...] = own[...].reshape(frames, bins, width)
    conv[0] += mm(stack(up), matrix[0])
    conv[frames - 1] += mm(stack(down), matrix[2])

    def beyond(bin_at, side, tap):
        rows = jnp.concatenate(
            [up[:, bin_at, :].astype(F32), borders[side], down[:, bin_at, :].astype(F32)], axis=0
        )
        total = None
        for i in range(3):
            term = mm(
                rows[i : i + frames].astype(BF), matrix[i, tap * width : (tap + 1) * width, :]
            )
            total = term if total is None else total + term
        return total

    parts = (
        beyond(0, 0, 2),
        conv[:, 0, :],
        conv[:, bins - 1, :],
        beyond(bins - 1, 1, 0),
    )
    pieces[...] = jnp.zeros(pieces.shape, F32)
    for at, part in enumerate(parts):
        high = part.astype(BF).astype(F32)
        pieces[:, 2 * at, :] = high
        pieces[:, 2 * at + 1, :] = part - high
    values = conv[...]
    sigma = sigmoid(values)
    load_mid.wait()
    hidden = mid[...].astype(F32) + values * sigma
    payload[:, :bins, :] = with_borders(hidden, borders[0], borders[1]).astype(BF)
    payload[:, bins:, :] = pieces[...].astype(BF)


def prepare_body(
    conv, mid_far, even_down, odd_down, cotangent_far, out_w_far,
    turned_far, grad_att_far, slope_far,
    slope, mid, cotangent, out_w, turned, grad_att, up, down, semaphores,
):
    start = copier(semaphores)
    loads = start(mid_far, mid), start(cotangent_far, cotangent), start(out_w_far, out_w)
    sort_halos(even_down, odd_down, up, down)
    slope[...] = slope_of(conv[...], sigmoid(conv[...]))
    stores = [start(slope, slope_far)]
    for load in loads:
        load.wait()
    frames, bins, width = mid.shape
    turned[:, :bins] = up[0].T
    turned[:, bins : (frames + 1) * bins] = mid[...].reshape(frames * bins, width).T
    turned[:, (frames + 1) * bins :] = down[0].T
    grad_att[...] = mm(cotangent[...], out_w[...], NT).astype(BF)
    stores += [start(turned, turned_far), start(grad_att, grad_att_far)]
    for store in stores:
        store.wait()


def columns(part, h, heads=HEADS):
    at = (part * heads + h) * HEAD
    if not isinstance(h, int):
        at = pl.multiple_of(at, HEAD)
    return pl.ds(at, HEAD)


def one_head(h, heads, qkv, grad_att, attended, grad_cells, sum_keys, sum_values):
    def columns_of(part):
        return columns(part, h, heads)

    cells = qkv.shape[0]
    keys = qkv[:, columns_of(1)]
    values = qkv[:, columns_of(2)]
    values_ones = jnp.concatenate([values, jnp.ones((cells, HEAD), BF)], axis=1)
    for block in range(cells // QUERY_BLOCK):
        rows = slice(block * QUERY_BLOCK, (block + 1) * QUERY_BLOCK)
        queries = qkv[rows, columns_of(0)]
        scores = mm(queries, keys, NT)
        raised = jnp.exp2(scores - jnp.max(scores, axis=-1, keepdims=True))
        raised_b = raised.astype(BF)
        sums = mm(raised_b, values_ones)
        inverse = 1.0 / sums[:, HEAD:]
        result = sums[:, :HEAD] * inverse
        attended[rows, columns_of(0)] = result.astype(BF)
        scaled = grad_att[rows, columns_of(0)].astype(F32) * inverse
        inner = jnp.sum(scaled * result, axis=-1, keepdims=True)
        scaled_b = scaled.astype(BF)
        grad_probs = mm(scaled_b, values, NT)
        grad_scores = (raised * (grad_probs - inner)).astype(BF)
        grad_cells[rows, columns_of(0)] = (mm(grad_scores, keys) * FACTOR).astype(BF)
        new_keys = mm(queries.T, grad_scores)
        new_values = mm(scaled_b.T, raised_b)
        if block == 0:
            sum_keys[...] = new_keys
            sum_values[...] = new_values
        else:
            sum_keys[...] += new_keys
            sum_values[...] += new_values
    grad_cells[:, columns_of(1)] = (sum_keys[...] * (1.0 / LOG2E)).T.astype(BF)
    grad_cells[:, columns_of(2)] = sum_values[...].T.astype(BF)


def normed_parts(hidden_f):
    inv_rms = lax.rsqrt(jnp.mean(hidden_f * hidden_f, axis=-1, keepdims=True) + 1e-6)
    normed_f = hidden_f * inv_rms
    return inv_rms, normed_f, normed_f.astype(BF)


def split_columns(target, at, values):
    for n in range(values.shape[1] // 128):
        target[at + n] = values[:, n * 128 : (n + 1) * 128]


def attend_body(
    came, qkv_w_far, grad_att_far, cotangent_far,
    payload, hidden_far, attended_far, grad_cells_far,
    qkv_w, grad_att, cotangent, hidden, qkv, attended, grad_cells,
    sum_keys, sum_values, pieces, semaphores,
):
    start = copier(semaphores)
    load_qkv_w = start(qkv_w_far, qkv_w)
    load_grad_att = start(grad_att_far, grad_att)
    load_cotangent = start(cotangent_far, cotangent)
    chunks, long, width = came.shape
    bins = long - EXTRA
    wide = HEADS * HEAD
    pieces[...] = came[:, bins:, :].astype(F32)
    here_first = pieces[:, 2, :] + pieces[:, 3, :]
    here_last = pieces[:, 4, :] + pieces[:, 5, :]
    first = here_first + moved_down(pieces[:, 6, :] + pieces[:, 7, :])
    last = here_last + moved_up(pieces[:, 0, :] + pieces[:, 1, :])
    sigma_first, sigma_last = sigmoid(first), sigmoid(last)
    fixed_first = came[:, 0, :].astype(F32) + first * sigma_first
    fixed_last = came[:, bins - 1, :].astype(F32) + last * sigma_last
    cells = with_borders(came[:, :bins, :].astype(F32), fixed_first, fixed_last)
    hidden[...] = cells.astype(BF).reshape(chunks * bins, width)
    stores = [start(hidden, hidden_far)]
    _, _, normed = normed_parts(hidden[...].astype(F32))
    load_qkv_w.wait()
    qkv[:, :wide] = (mm(normed, qkv_w[:, :wide]) * (FACTOR * LOG2E)).astype(BF)
    qkv[:, wide:] = mm(normed, qkv_w[:, wide:]).astype(BF)
    load_grad_att.wait()

    for h in range(HEADS):
        one_head(h, HEADS, qkv, grad_att, attended, grad_cells, sum_keys, sum_values)
    stores += [start(grad_cells, grad_cells_far), start(attended, attended_far)]
    load_cotangent.wait()
    inv_rms, normed_f, _ = normed_parts(hidden[...].astype(F32))
    grad_normed = mm(grad_cells[...], qkv_w[...], NT)
    mixing = jnp.mean(grad_normed * normed_f, axis=-1, keepdims=True)
    grad = cotangent[...].astype(F32) + inv_rms * (grad_normed - normed_f * mixing)
    grad_b = grad.astype(BF).reshape(chunks, bins, width)
    payload[:, :bins, :] = grad_b
    grad_first = payload[:, 0, :].astype(F32) * slope_of(first, sigma_first)
    grad_last = payload[:, bins - 1, :].astype(F32) * slope_of(last, sigma_last)
    pieces[...] = jnp.zeros(pieces.shape, F32)
    pieces[:, 0, :] = moved_down(grad_last)
    pieces[:, 1, :] = grad_first
    pieces[:, 2, :] = grad_last
    pieces[:, 3, :] = moved_up(grad_first)
    payload[:, bins:, :] = pieces[...].astype(BF)
    for store in stores:
        store.wait()


def deal(rows, core, groups):
    for n in range(rows.shape[0]):
        for e, (source, per, at) in enumerate(groups):
            begin = per * (2 * n + core) + at
            rows[n, 8 * e : 8 * e + 8, :] = source[pl.ds(begin, 8, stride=32 * per), :]


def attend_rest_body(
    hidden_far, attended_far, grad_cells_far, cotangent_far, out_w_far, slope_far, turned_far,
    enhanced, theirs, mine_far, slope, turned,
    hidden, attended, grad_cells, cotangent, out_w, mine, grads, grads_out, rows, semaphores,
):
    start = copier(semaphores)
    load_hidden, load_cells = start(hidden_far, hidden), start(grad_cells_far, grad_cells)
    loads = [
        start(attended_far, attended), start(cotangent_far, cotangent), start(out_w_far, out_w)
    ]
    ahead = [start(slope_far, slope), start(turned_far, turned)]
    load_hidden.wait()
    hidden_f = hidden[...].astype(F32)
    _, _, normed = normed_parts(hidden_f)
    load_cells.wait()
    split_columns(grads, 0, SCALE * mm(normed.T, grad_cells[...]))
    for load in loads:
        load.wait()
    split_columns(grads_out, 0, SCALE * mm(attended[...].T, cotangent[...]))
    groups = [(grads.at[n], 1, 0) for n in range(12)]
    groups += [(grads_out.at[n % 2], 2, n // 2) for n in range(4)]
    core = lax.axis_index("core")
    deal(rows, 1 - core, groups)
    theirs[...] = rows[...].astype(BF)
    deal(rows, core, groups)
    mine[...] = rows[...].astype(BF)
    store = start(mine, mine_far)
    enhanced[...] = (hidden_f + mm(attended[...], out_w[...])).astype(BF)
    for copy in ahead:
        copy.wait()
    store.wait()


def stack_back(rows, left, right):
    after = bins_after(rows, right).astype(BF)
    before = bins_before(rows, left).astype(BF)
    return jnp.concatenate([after, rows.astype(BF), before], axis=-1)


def conv_weight_body(
    came, slope, turned, early_far, edges, theirs, mine, early, stacked_far, grad_far,
    stacked, own, grads, rows, pieces, semaphores,
):
    start = copier(semaphores)
    load_early = start(early_far, early)
    frames, long, width = came.shape
    bins = long - EXTRA
    half = width // 2
    cells = frames * bins
    pieces[...] = came[:, bins:, :].astype(F32)
    own[...] = came[:, :bins, :]
    stores = [start(own, grad_far)]
    grad = own[...].astype(F32) * slope[...]
    grad = with_borders(grad, pieces[:, 1, :], pieces[:, 2, :])
    grad_b = grad.astype(BF)
    odd = lax.rem(lax.axis_index("y"), 2) == 1
    ends = []
    for frame in (0, frames - 1):
        ends.append(
            jnp.concatenate([grad_b[frame : frame + 1], came[frame : frame + 1, bins:, :]], axis=1)
        )
    edges[0] = jnp.where(odd, ends[0], ends[1])
    edges[1] = jnp.where(odd, ends[1], ends[0])
    stacked[...] = stack_back(
        grad_b.astype(F32), pieces[:, 0, :][:, None, :], pieces[:, 3, :][:, None, :]
    )
    stores.append(start(stacked, stacked_far))
    flat = stacked[...].reshape(cells, 3 * width)
    for i in range(3):
        block = mm(turned[:, i * bins : i * bins + cells], flat)
        for j in range(3):
            at = j * width
            upper = block[:half, at : at + half] + block[half:, at + half : at + width]
            lower = block[:half, at + half : at + width] - block[half:, at : at + half]
            tap = (3 * i + j) * half
            grads[tap : tap + half] = upper * SCALE
            grads[9 * half + tap : 9 * half + tap + half] = lower * SCALE
    core = lax.axis_index("core")
    groups = [(grads, 9, e) for e in range(9)]
    rows[:, 72:, :] = jnp.zeros((rows.shape[0], 8, 128), F32)
    deal(rows, 1 - core, groups)
    theirs[...] = rows[...].astype(BF)
    deal(rows, core, groups)
    mine[...] = rows[...].astype(BF)
    load_early.wait()
    for store in stores:
        store.wait()


def conv_data_body(
    grad_far, stacked_far, weight_far, total, matrix, grad, stacked, weight, semaphores
):
    start = copier(semaphores)
    load_weight, load_stacked = start(weight_far, weight), start(stacked_far, stacked)
    load_grad = start(grad_far, grad)
    frames, bins, triple = stacked.shape
    width = triple // 3
    half = width // 2
    load_weight.wait()
    for i in range(3):
        for j in range(3):
            real, imag = weight[0, i, j], weight[1, i, j]
            at = j * width
            matrix[i, :half, at : at + half] = real
            matrix[i, :half, at + half : at + width] = imag
            matrix[i, half:, at : at + half] = -imag
            matrix[i, half:, at + half : at + width] = real
    load_stacked.wait()
    load_grad.wait()
    inner = (frames - 1) * bins
    flat = stacked[...].reshape(frames * bins, triple)
    total[...] = grad[...].reshape(frames * bins, width).astype(F32) + mm(flat, matrix[1], NT)
    total[:inner] += mm(flat[bins:], matrix[0], NT)
    total[bins:] += mm(flat[:inner], matrix[2], NT)


def conv_data_finish_body(total, even_down, odd_down, matrix, out, up, down):
    sort_halos(even_down, odd_down, up, down)
    frames, bins, width = out.shape

    def stack(edge):
        extra = edge[:, bins:, :].astype(F32)
        rows = edge[:, :bins, :].astype(F32)
        return stack_back(rows, extra[:, 0:1, :], extra[:, 3:4, :])[0]

    out[...] = total[...].reshape(frames, bins, width).astype(BF)
    out[0] = (total[:bins] + mm(stack(up), matrix[2], NT)).astype(BF)
    out[frames - 1] = (total[(frames - 1) * bins :] + mm(stack(down), matrix[0], NT)).astype(BF)


def sum_body(came, out):
    total = came[0].astype(F32)
    for source in range(1, came.shape[0]):
        total = total + came[source].astype(F32)
    out[...] = total


def join_body(early, early_got, mine, got, message):
    cut = early.shape[1]
    message[:, :cut, :] = (early[...].astype(F32) + early_got[...].astype(F32)).astype(BF)
    message[:, cut:, :] = (mine[...].astype(F32) + got[...].astype(F32)).astype(BF)


def regroup_body(came, chunk, total, rows):
    sum_body(came, total)
    rows[...] = jnp.zeros(rows.shape, F32)
    for z in range(chunk.shape[0]):
        rows[z, 0:GROUPS, :] = total[pl.ds(z, GROUPS, stride=8), :]
    chunk[...] = rows[...].astype(BF)


def share_body(came, conv, qkv, out, total):
    sum_body(came, total)
    qkv[...] = total[0:12]
    out[...] = total[12:16]
    conv[...] = total[16:25]


def pair_exchanges(first, second):
    size = lax.axis_size("z") * lax.axis_size("y")
    near = [(i, i ^ 1) for i in range(size)]
    apart = [(i, i + 1 if i % 2 else i - 1) for i in range(1, size - 1)]
    return lax.ppermute(first, ("z", "y"), near), lax.ppermute(second, ("z", "y"), apart)


def exchange(array, axis):
    return lax.all_to_all(array, axis, split_axis=0, concat_axis=0, tiled=True)


def swap_cores(array):
    return lax.ppermute(array, "core", [(0, 1), (1, 0)])


def shards(spectrum, conv_weight, qkv_weight, out_weight, cotangent):
    frames, bins, width = spectrum.shape
    cells = frames * bins
    wide = HEADS * HEAD
    long = bins + EXTRA
    vmem = pltpu.VMEM
    cotangent = cotangent.reshape(cells, width)
    odd = lax.rem(lax.axis_index("y"), 2) == 1
    first, last = spectrum[:1], spectrum[frames - 1 :]
    halo_a, halo_b = pair_exchanges(jnp.where(odd, first, last), jnp.where(odd, last, first))
    tile = vmem((frames, bins, width), BF)
    tile_f = vmem((frames, bins, width), F32)
    pieces = vmem((frames, EXTRA, width), F32)
    square = vmem((cells, width), BF)
    kernels = vmem(conv_weight.shape, BF)
    halo = vmem((1, bins, width), BF)
    own, borders, matrix = kernel_call(
        conv_own_body, "conv_own",
        [
            ((cells, width), F32, "any"), ((2, frames, width), F32, "any"),
            ((3, 3 * width, width), BF, "any"),
        ],
        spectrum, conv_weight, far=(0, 1),
        scratch=[tile, kernels, vmem((frames, bins, 3 * width), BF)], copies=2, mflops=1200,
    )
    payload, conv = kernel_call(
        conv_finish_body, "conv_finish",
        [((frames, long, width), BF, "any"), ((frames, bins, width), F32, "vmem")],
        spectrum, halo_a, halo_b, own, borders, matrix, far=(0,),
        scratch=[tile, pieces, halo, halo], copies=1, mflops=200,
    )
    frame = exchange(payload, ("x", "core"))
    turned_shape = (width, cells + 2 * bins)
    turned, grad_att, slope = kernel_call(
        prepare_body, "prepare",
        [
            (turned_shape, BF, "hbm"), ((cells, wide), BF, "hbm"),
            ((frames, bins, width), F32, "hbm"),
        ],
        conv, spectrum, halo_a, halo_b, cotangent, out_weight, far=(1, 4, 5),
        scratch=[
            tile_f, tile, square, vmem((wide, width), BF), vmem(turned_shape, BF),
            vmem((cells, wide), BF), halo, halo,
        ],
        copies=6, mflops=300,
    )
    attended_v, cells_v = vmem((cells, wide), BF), vmem((cells, 3 * wide), BF)
    back, hidden, attended, grad_cells = kernel_call(
        attend_body, "attend",
        [
            ((frames, long, width), BF, "any"), ((cells, width), BF, "hbm"),
            ((cells, wide), BF, "hbm"), ((cells, 3 * wide), BF, "hbm"),
        ],
        frame, qkv_weight, grad_att, cotangent, far=(1, 2, 3),
        scratch=[
            vmem((width, 3 * wide), BF), attended_v, square, square, cells_v, attended_v, cells_v,
            vmem((HEAD, cells), F32), vmem((HEAD, cells), F32), pieces,
        ],
        copies=6, mflops=15000,
    )
    grads = exchange(back, ("x", "core"))
    ring = lax.axis_size("y") * lax.axis_size("x")
    early_shape = (ring, 8 * EARLY, 128)
    late_shape = (ring, 8 * (GROUPS - EARLY), 128)
    enhanced, theirs, mine, slope, turned = kernel_call(
        attend_rest_body, "attend_rest",
        [
            ((cells, width), BF, "any"), (early_shape, BF, "any"), (early_shape, BF, "hbm"),
            ((frames, bins, width), F32, "vmem"), (turned_shape, BF, "vmem"),
        ],
        hidden, attended, grad_cells, cotangent, out_weight, slope, turned,
        far=(0, 1, 2, 3, 4, 5, 6),
        scratch=[
            square, attended_v, cells_v, square, vmem((wide, width), BF), vmem(early_shape, BF),
            vmem((12, width, HEAD), F32), vmem((2, wide, HEAD), F32), vmem(early_shape, F32),
        ],
        copies=8, mflops=1500, limit=40,
    )
    theirs, grads = lax.optimization_barrier((theirs, grads))
    got = swap_cores(theirs)
    stacked_shape = (frames, bins, 3 * width)
    edges, theirs, late_mine, early, stacked, grad_tile = kernel_call(
        conv_weight_body, "conv_weight_grad",
        [
            ((2, 1, long, width), BF, "any"), (late_shape, BF, "any"), (late_shape, BF, "any"),
            (early_shape, BF, "any"), (stacked_shape, BF, "hbm"),
            ((frames, bins, width), BF, "hbm"),
        ],
        grads, slope, turned, mine, far=(3,),
        scratch=[
            vmem(stacked_shape, BF), tile,
            vmem((18 * (width // 2), width // 2), F32), vmem(late_shape, F32), pieces,
        ],
        copies=3, mflops=1200, limit=40,
    )
    late_got = swap_cores(theirs)
    edges, late_got = lax.optimization_barrier((edges, late_got))
    (message,) = kernel_call(
        join_body, "join", [((ring, 8 * GROUPS, 128), BF, "any")], early, got, late_mine,
        late_got,
    )
    late = exchange(message, ("y", "x"))
    total, matrix_back = kernel_call(
        conv_data_body, "conv_data",
        [((cells, width), F32, "vmem"), ((3, width, 3 * width), BF, "vmem")],
        grad_tile, stacked, conv_weight, far=(0, 1, 2),
        scratch=[tile, vmem(stacked_shape, BF), kernels], copies=3, mflops=1200,
    )
    edge_a, edge_b = pair_exchanges(edges[0], edges[1])
    late, total, edge_a, edge_b = lax.optimization_barrier((late, total, edge_a, edge_b))
    (chunk,) = kernel_call(
        regroup_body, "regroup", [((lax.axis_size("z"), 32, 128), BF, "any")],
        late,
        scratch=[vmem(late.shape[1:], F32), vmem((lax.axis_size("z"), 32, 128), F32)],
    )
    (grad_spectrum,) = kernel_call(
        conv_data_finish_body, "conv_data_finish", [((frames, bins, width), BF, "any")],
        total, edge_a, edge_b, matrix_back,
        scratch=[vmem((1, long, width), BF), vmem((1, long, width), BF)], mflops=100,
    )
    shares = kernel_call(
        share_body, "share", [((9, 128), F32, "any"), ((12, 128), F32, "any"), ((4, 128), F32, "any")],
        exchange(chunk, "z"),
        scratch=[vmem((32, 128), F32)],
    )
    return (enhanced.reshape(1, cells, width), grad_spectrum, *[s.reshape(-1) for s in shares])


def solution(mesh):
    mesh = Mesh(mesh.devices.reshape(8, 4, 4, 2), ("z", "y", "x", "core"))
    every = P(("z", "y", "x", "core"))
    tiles, rows = P(("z", "y"), ("x", "core"), None), P(("z", "y", "x", "core"), None, None)
    return jax.shard_map(
        shards,
        mesh=mesh,
        in_specs=(tiles, P(), P(), P(), rows),
        out_specs=(rows, tiles, every, every, every),
        check_vma=False,
    )
```

```python
import math

import jax
import jax.numpy as jnp
from jax import lax
from jax.experimental import pallas as pl
from jax.experimental.pallas import tpu as pltpu
from jax.sharding import Mesh
from jax.sharding import PartitionSpec as P

HEADS = 4
HEAD = 128
EXTRA = 16
SCALE = 1.0 / 512
LOG2E = math.log2(math.e)
FACTOR = 1.0 / math.sqrt(HEAD)
BF = jnp.bfloat16
F32 = jnp.float32
NN = (((1,), (0,)), ((), ()))
NT = (((1,), (1,)), ((), ()))
QUERY_BLOCK = 1024
GROUPS = 26
EARLY = 16


def mm(a, b, dims=NN):
    return lax.dot_general(a, b, dims, preferred_element_type=F32)


PLACES = {"any": jax.ShapeDtypeStruct, "hbm": pltpu.HBM, "vmem": pltpu.VMEM}


def kernel_call(body, name, outs, *args, far=(), scratch=(), copies=0, mflops=0, limit=48):
    shapes = [
        PLACES[away](dims, kind) for dims, kind, away in outs
    ]
    args = [
        pltpu.with_memory_space_constraint(a, pltpu.HBM) if n in far else a
        for n, a in enumerate(args)
    ]
    size = sum(math.prod(a.shape) * a.dtype.itemsize for a in (*args, *shapes))
    near, hbm = pl.BlockSpec(memory_space=pltpu.VMEM), pl.BlockSpec(memory_space=pltpu.HBM)
    scratch = list(scratch) + ([pltpu.SemaphoreType.DMA((copies,))] if copies else [])
    return pl.pallas_call(
        body,
        out_shape=shapes,
        in_specs=[hbm if n in far else near for n in range(len(args))],
        out_specs=[hbm if away == "hbm" else near for _, _, away in outs],
        scratch_shapes=scratch,
        compiler_params=pltpu.CompilerParams(vmem_limit_bytes=limit * 2**20),
        cost_estimate=pl.CostEstimate(
            flops=mflops * 10**6, bytes_accessed=size, transcendentals=0
        ),
        name=name,
    )(*args)


def copier(semaphores):
    started = []

    def start(source, target):
        copy = pltpu.make_async_copy(source, target, semaphores.at[len(started)])
        copy.start()
        started.append(copy)
        return copy

    return start


def sigmoid(v):
    return 1.0 / (1.0 + jnp.exp(-v))


def slope_of(v, sigma):
    return sigma * (1.0 + v * (1.0 - sigma))


def moved_down(rows):
    at = lax.broadcasted_iota(jnp.int32, rows.shape, 0)
    return jnp.where(at == 0, 0.0, pltpu.roll(rows, 1, 0))


def moved_up(rows):
    last = rows.shape[0] - 1
    at = lax.broadcasted_iota(jnp.int32, rows.shape, 0)
    return jnp.where(at == last, 0.0, pltpu.roll(rows, last, 0))


def with_borders(inner, first, last):
    at = lax.broadcasted_iota(jnp.int32, inner.shape, 1)
    inner = jnp.where(at == 0, first[:, None, :], inner)
    return jnp.where(at == inner.shape[1] - 1, last[:, None, :], inner)


def bins_before(rows, left):
    at = lax.broadcasted_iota(jnp.int32, rows.shape, 1)
    return jnp.where(at == 0, left, pltpu.roll(rows, 1, 1))


def bins_after(rows, right):
    last = rows.shape[1] - 1
    at = lax.broadcasted_iota(jnp.int32, rows.shape, 1)
    return jnp.where(at == last, right, pltpu.roll(rows, last, 1))


def sort_halos(even_down, odd_down, up, down):
    odd = lax.rem(lax.axis_index("y"), 2) == 1
    first, second = even_down[...], odd_down[...]
    up[...] = jnp.where(odd, first, second)
    down[...] = jnp.where(odd, second, first)


def begin_body(mid_far, weight_far, send_a, send_b, borders, matrix, stacked, mid, weight, semaphores):
    start = copier(semaphores)
    load_mid, load_weight = start(mid_far, mid), start(weight_far, weight)
    frames, bins, width = mid.shape
    half = width // 2
    load_mid.wait()
    odd = lax.rem(lax.axis_index("y"), 2) == 1
    first, last = mid[0:1], mid[frames - 1 : frames]
    send_a[...] = jnp.where(odd, first, last)
    send_b[...] = jnp.where(odd, last, first)
    wide = mid[...].astype(F32)
    stacked[:, :, :width] = bins_before(wide, 0.0).astype(BF)
    stacked[:, :, width : 2 * width] = mid[...]
    stacked[:, :, 2 * width :] = bins_after(wide, 0.0).astype(BF)
    borders[0] = mid[:, 0, :].astype(F32)
    borders[1] = mid[:, bins - 1, :].astype(F32)
    load_weight.wait()
    for i in range(3):
        for j in range(3):
            real, imag = weight[0, i, j], weight[1, i, j]
            at = j * width
            matrix[i, at : at + half, :half] = real
            matrix[i, at : at + half, half:] = imag
            matrix[i, at + half : at + width, :half] = -imag
            matrix[i, at + half : at + width, half:] = real


def conv_own_body(stacked, matrix, conv):
    frames, bins, triple = stacked.shape
    inner = (frames - 1) * bins
    everything = stacked[...].reshape(frames * bins, triple)
    conv[...] = mm(everything, matrix[1])
    conv[bins:] += mm(everything[:inner], matrix[0])
    conv[:inner] += mm(everything[bins:], matrix[2])


def conv_finish_body(
    mid_far, even_down, odd_down, own, borders, matrix,
    payload, conv, mid, pieces, up, down, semaphores,
):
    start = copier(semaphores)
    load_mid = start(mid_far, mid)
    sort_halos(even_down, odd_down, up, down)
    frames, bins, width = mid.shape

    def stack(row):
        wide = row[...].astype(F32)
        before = bins_before(wide, 0.0).astype(BF)
        after = bins_after(wide, 0.0).astype(BF)
        return jnp.concatenate([before[0], row[0], after[0]], axis=1)

    conv[...] = own[...].reshape(frames, bins, width)
    conv[0] += mm(stack(up), matrix[0])
    conv[frames - 1] += mm(stack(down), matrix[2])

    def beyond(bin_at, side, tap):
        rows = jnp.concatenate(
            [up[:, bin_at, :].astype(F32), borders[side], down[:, bin_at, :].astype(F32)], axis=0
        )
        total = None
        for i in range(3):
            term = mm(
                rows[i : i + frames].astype(BF), matrix[i, tap * width : (tap + 1) * width, :]
            )
            total = term if total is None else total + term
        return total

    parts = (
        beyond(0, 0, 2),
        conv[:, 0, :],
        conv[:, bins - 1, :],
        beyond(bins - 1, 1, 0),
    )
    pieces[...] = jnp.zeros(pieces.shape, F32)
    for at, part in enumerate(parts):
        high = part.astype(BF).astype(F32)
        pieces[:, 2 * at, :] = high
        pieces[:, 2 * at + 1, :] = part - high
    values = conv[...]
    sigma = sigmoid(values)
    load_mid.wait()
    hidden = mid[...].astype(F32) + values * sigma
    payload[:, :bins, :] = with_borders(hidden, borders[0], borders[1]).astype(BF)
    payload[:, bins:, :] = pieces[...].astype(BF)


def prepare_body(
    conv, mid_far, even_down, odd_down, cotangent_far, out_w_far,
    turned_far, grad_att_far, slope_far,
    slope, mid, cotangent, out_w, turned, grad_att, up, down, semaphores,
):
    start = copier(semaphores)
    loads = start(mid_far, mid), start(cotangent_far, cotangent), start(out_w_far, out_w)
    sort_halos(even_down, odd_down, up, down)
    slope[...] = slope_of(conv[...], sigmoid(conv[...]))
    stores = [start(slope, slope_far)]
    for load in loads:
        load.wait()
    frames, bins, width = mid.shape
    turned[:, :bins] = up[0].T
    turned[:, bins : (frames + 1) * bins] = mid[...].reshape(frames * bins, width).T
    turned[:, (frames + 1) * bins :] = down[0].T
    grad_att[...] = mm(cotangent[...], out_w[...], NT).astype(BF)
    stores += [start(turned, turned_far), start(grad_att, grad_att_far)]
    for store in stores:
        store.wait()


def columns(part, h, heads=HEADS):
    at = (part * heads + h) * HEAD
    if not isinstance(h, int):
        at = pl.multiple_of(at, HEAD)
    return pl.ds(at, HEAD)


def one_head(h, heads, qkv, grad_att, attended, grad_cells, sum_keys, sum_values):
    def columns_of(part):
        return columns(part, h, heads)

    cells = qkv.shape[0]
    keys = qkv[:, columns_of(1)]
    values = qkv[:, columns_of(2)]
    values_ones = jnp.concatenate([values, jnp.ones((cells, HEAD), BF)], axis=1)
    for block in range(cells // QUERY_BLOCK):
        rows = slice(block * QUERY_BLOCK, (block + 1) * QUERY_BLOCK)
        queries = qkv[rows, columns_of(0)]
        scores = mm(queries, keys, NT)
        raised = jnp.exp2(scores - jnp.max(scores, axis=-1, keepdims=True))
        raised_b = raised.astype(BF)
        sums = mm(raised_b, values_ones)
        inverse = 1.0 / sums[:, HEAD:]
        result = sums[:, :HEAD] * inverse
        attended[rows, columns_of(0)] = result.astype(BF)
        scaled = grad_att[rows, columns_of(0)].astype(F32) * inverse
        inner = jnp.sum(scaled * result, axis=-1, keepdims=True)
        scaled_b = scaled.astype(BF)
        grad_probs = mm(scaled_b, values, NT)
        grad_scores = (raised * (grad_probs - inner)).astype(BF)
        grad_cells[rows, columns_of(0)] = (mm(grad_scores, keys) * FACTOR).astype(BF)
        new_keys = mm(queries.T, grad_scores)
        new_values = mm(scaled_b.T, raised_b)
        if block == 0:
            sum_keys[...] = new_keys
            sum_values[...] = new_values
        else:
            sum_keys[...] += new_keys
            sum_values[...] += new_values
    grad_cells[:, columns_of(1)] = (sum_keys[...] * (1.0 / LOG2E)).T.astype(BF)
    grad_cells[:, columns_of(2)] = sum_values[...].T.astype(BF)


def normed_parts(hidden_f):
    inv_rms = lax.rsqrt(jnp.mean(hidden_f * hidden_f, axis=-1, keepdims=True) + 1e-6)
    normed_f = hidden_f * inv_rms
    return inv_rms, normed_f, normed_f.astype(BF)


def split_columns(target, at, values):
    for n in range(values.shape[1] // 128):
        target[at + n] = values[:, n * 128 : (n + 1) * 128]


def attend_body(
    came, qkv_w_far, grad_att_far, cotangent_far,
    payload, hidden_far, attended_far, grad_cells_far,
    qkv_w, grad_att, cotangent, hidden, qkv, attended, grad_cells,
    sum_keys, sum_values, pieces, semaphores,
):
    start = copier(semaphores)
    load_qkv_w = start(qkv_w_far, qkv_w)
    load_grad_att = start(grad_att_far, grad_att)
    load_cotangent = start(cotangent_far, cotangent)
    chunks, long, width = came.shape
    bins = long - EXTRA
    wide = HEADS * HEAD
    pieces[...] = came[:, bins:, :].astype(F32)
    here_first = pieces[:, 2, :] + pieces[:, 3, :]
    here_last = pieces[:, 4, :] + pieces[:, 5, :]
    first = here_first + moved_down(pieces[:, 6, :] + pieces[:, 7, :])
    last = here_last + moved_up(pieces[:, 0, :] + pieces[:, 1, :])
    sigma_first, sigma_last = sigmoid(first), sigmoid(last)
    fixed_first = came[:, 0, :].astype(F32) + first * sigma_first
    fixed_last = came[:, bins - 1, :].astype(F32) + last * sigma_last
    cells = with_borders(came[:, :bins, :].astype(F32), fixed_first, fixed_last)
    hidden[...] = cells.astype(BF).reshape(chunks * bins, width)
    stores = [start(hidden, hidden_far)]
    _, _, normed = normed_parts(hidden[...].astype(F32))
    load_qkv_w.wait()
    qkv[:, :wide] = (mm(normed, qkv_w[:, :wide]) * (FACTOR * LOG2E)).astype(BF)
    qkv[:, wide:] = mm(normed, qkv_w[:, wide:]).astype(BF)
    load_grad_att.wait()

    for h in range(HEADS):
        one_head(h, HEADS, qkv, grad_att, attended, grad_cells, sum_keys, sum_values)
        part = columns(0, h)
        stores.append(start(attended.at[:, part], attended_far.at[:, part]))
        for n in range(3):
            part = columns(n, h)
            stores.append(start(grad_cells.at[:, part], grad_cells_far.at[:, part]))
    load_cotangent.wait()
    inv_rms, normed_f, _ = normed_parts(hidden[...].astype(F32))
    grad_normed = mm(grad_cells[...], qkv_w[...], NT)
    mixing = jnp.mean(grad_normed * normed_f, axis=-1, keepdims=True)
    grad = cotangent[...].astype(F32) + inv_rms * (grad_normed - normed_f * mixing)
    grad_b = grad.astype(BF).reshape(chunks, bins, width)
    payload[:, :bins, :] = grad_b
    grad_first = payload[:, 0, :].astype(F32) * slope_of(first, sigma_first)
    grad_last = payload[:, bins - 1, :].astype(F32) * slope_of(last, sigma_last)
    pieces[...] = jnp.zeros(pieces.shape, F32)
    pieces[:, 0, :] = moved_down(grad_last)
    pieces[:, 1, :] = grad_first
    pieces[:, 2, :] = grad_last
    pieces[:, 3, :] = moved_up(grad_first)
    payload[:, bins:, :] = pieces[...].astype(BF)
    for store in stores:
        store.wait()


def deal(rows, core, groups):
    for n in range(rows.shape[0]):
        for e, (source, per, at) in enumerate(groups):
            begin = per * (2 * n + core) + at
            rows[n, 8 * e : 8 * e + 8, :] = source[pl.ds(begin, 8, stride=32 * per), :]


def attend_rest_body(
    hidden_far, attended_far, grad_cells_far, cotangent_far, out_w_far, slope_far, turned_far,
    enhanced, theirs, mine_far, slope, turned,
    hidden, attended, grad_cells, cotangent, out_w, mine, grads, grads_out, rows, semaphores,
):
    start = copier(semaphores)
    load_hidden, load_cells = start(hidden_far, hidden), start(grad_cells_far, grad_cells)
    loads = [
        start(attended_far, attended), start(cotangent_far, cotangent), start(out_w_far, out_w)
    ]
    ahead = [start(slope_far, slope), start(turned_far, turned)]
    load_hidden.wait()
    hidden_f = hidden[...].astype(F32)
    _, _, normed = normed_parts(hidden_f)
    load_cells.wait()
    split_columns(grads, 0, SCALE * mm(normed.T, grad_cells[...]))
    for load in loads:
        load.wait()
    split_columns(grads_out, 0, SCALE * mm(attended[...].T, cotangent[...]))
    groups = [(grads.at[n], 1, 0) for n in range(12)]
    groups += [(grads_out.at[n % 2], 2, n // 2) for n in range(4)]
    core = lax.axis_index("core")
    deal(rows, 1 - core, groups)
    theirs[...] = rows[...].astype(BF)
    deal(rows, core, groups)
    mine[...] = rows[...].astype(BF)
    store = start(mine, mine_far)
    enhanced[...] = (hidden_f + mm(attended[...], out_w[...])).astype(BF)
    for copy in ahead:
        copy.wait()
    store.wait()


def stack_back(rows, left, right):
    after = bins_after(rows, right).astype(BF)
    before = bins_before(rows, left).astype(BF)
    return jnp.concatenate([after, rows.astype(BF), before], axis=-1)


def conv_weight_body(
    came, slope, turned, early_far, edges, theirs, mine, early, stacked_far, grad_far,
    stacked, own, grads, rows, pieces, semaphores,
):
    start = copier(semaphores)
    load_early = start(early_far, early)
    frames, long, width = came.shape
    bins = long - EXTRA
    half = width // 2
    cells = frames * bins
    pieces[...] = came[:, bins:, :].astype(F32)
    own[...] = came[:, :bins, :]
    stores = [start(own, grad_far)]
    grad = own[...].astype(F32) * slope[...]
    grad = with_borders(grad, pieces[:, 1, :], pieces[:, 2, :])
    grad_b = grad.astype(BF)
    odd = lax.rem(lax.axis_index("y"), 2) == 1
    ends = []
    for frame in (0, frames - 1):
        ends.append(
            jnp.concatenate([grad_b[frame : frame + 1], came[frame : frame + 1, bins:, :]], axis=1)
        )
    edges[0] = jnp.where(odd, ends[0], ends[1])
    edges[1] = jnp.where(odd, ends[1], ends[0])
    stacked[...] = stack_back(
        grad_b.astype(F32), pieces[:, 0, :][:, None, :], pieces[:, 3, :][:, None, :]
    )
    stores.append(start(stacked, stacked_far))
    flat = stacked[...].reshape(cells, 3 * width)
    for i in range(3):
        block = mm(turned[:, i * bins : i * bins + cells], flat)
        for j in range(3):
            at = j * width
            upper = block[:half, at : at + half] + block[half:, at + half : at + width]
            lower = block[:half, at + half : at + width] - block[half:, at : at + half]
            tap = (3 * i + j) * half
            grads[tap : tap + half] = upper * SCALE
            grads[9 * half + tap : 9 * half + tap + half] = lower * SCALE
    core = lax.axis_index("core")
    groups = [(grads, 9, e) for e in range(9)]
    rows[:, 72:, :] = jnp.zeros((rows.shape[0], 8, 128), F32)
    deal(rows, 1 - core, groups)
    theirs[...] = rows[...].astype(BF)
    deal(rows, core, groups)
    mine[...] = rows[...].astype(BF)
    load_early.wait()
    for store in stores:
        store.wait()


def conv_data_body(
    grad_far, stacked_far, weight_far, total, matrix, grad, stacked, weight, semaphores
):
    start = copier(semaphores)
    load_weight, load_stacked = start(weight_far, weight), start(stacked_far, stacked)
    load_grad = start(grad_far, grad)
    frames, bins, triple = stacked.shape
    width = triple // 3
    half = width // 2
    load_weight.wait()
    for i in range(3):
        for j in range(3):
            real, imag = weight[0, i, j], weight[1, i, j]
            at = j * width
            matrix[i, :half, at : at + half] = real
            matrix[i, :half, at + half : at + width] = imag
            matrix[i, half:, at : at + half] = -imag
            matrix[i, half:, at + half : at + width] = real
    load_stacked.wait()
    load_grad.wait()
    inner = (frames - 1) * bins
    flat = stacked[...].reshape(frames * bins, triple)
    total[...] = grad[...].reshape(frames * bins, width).astype(F32) + mm(flat, matrix[1], NT)
    total[:inner] += mm(flat[bins:], matrix[0], NT)
    total[bins:] += mm(flat[:inner], matrix[2], NT)


def conv_data_finish_body(total, even_down, odd_down, matrix, out, up, down):
    sort_halos(even_down, odd_down, up, down)
    frames, bins, width = out.shape

    def stack(edge):
        extra = edge[:, bins:, :].astype(F32)
        rows = edge[:, :bins, :].astype(F32)
        return stack_back(rows, extra[:, 0:1, :], extra[:, 3:4, :])[0]

    out[...] = total[...].reshape(frames, bins, width).astype(BF)
    out[0] = (total[:bins] + mm(stack(up), matrix[2], NT)).astype(BF)
    out[frames - 1] = (total[(frames - 1) * bins :] + mm(stack(down), matrix[0], NT)).astype(BF)


def sum_body(came, out):
    total = came[0].astype(F32)
    for source in range(1, came.shape[0]):
        total = total + came[source].astype(F32)
    out[...] = total


def join_body(early, early_got, mine, got, message):
    cut = early.shape[1]
    message[:, :cut, :] = (early[...].astype(F32) + early_got[...].astype(F32)).astype(BF)
    message[:, cut:, :] = (mine[...].astype(F32) + got[...].astype(F32)).astype(BF)


def regroup_body(came, chunk, total, rows):
    sum_body(came, total)
    rows[...] = jnp.zeros(rows.shape, F32)
    for z in range(chunk.shape[0]):
        rows[z, 0:GROUPS, :] = total[pl.ds(z, GROUPS, stride=8), :]
    chunk[...] = rows[...].astype(BF)


def share_body(came, conv, qkv, out, total):
    sum_body(came, total)
    qkv[...] = total[0:12]
    out[...] = total[12:16]
    conv[...] = total[16:25]


def pair_exchanges(first, second):
    size = lax.axis_size("z") * lax.axis_size("y")
    near = [(i, i ^ 1) for i in range(size)]
    apart = [(i, i + 1 if i % 2 else i - 1) for i in range(1, size - 1)]
    return lax.ppermute(first, ("z", "y"), near), lax.ppermute(second, ("z", "y"), apart)


def exchange(array, axis):
    return lax.all_to_all(array, axis, split_axis=0, concat_axis=0, tiled=True)


def swap_cores(array):
    return lax.ppermute(array, "core", [(0, 1), (1, 0)])


def shards(spectrum, conv_weight, qkv_weight, out_weight, cotangent):
    frames, bins, width = spectrum.shape
    cells = frames * bins
    wide = HEADS * HEAD
    long = bins + EXTRA
    vmem = pltpu.VMEM
    cotangent = cotangent.reshape(cells, width)
    tile = vmem((frames, bins, width), BF)
    tile_f = vmem((frames, bins, width), F32)
    pieces = vmem((frames, EXTRA, width), F32)
    square = vmem((cells, width), BF)
    kernels = vmem(conv_weight.shape, BF)
    halo = vmem((1, bins, width), BF)
    send_a, send_b, borders, matrix, stacked = kernel_call(
        begin_body, "begin",
        [
            ((1, bins, width), BF, "any"), ((1, bins, width), BF, "any"),
            ((2, frames, width), F32, "any"), ((3, 3 * width, width), BF, "vmem"),
            ((frames, bins, 3 * width), BF, "vmem"),
        ],
        spectrum, conv_weight, far=(0, 1),
        scratch=[tile, kernels], copies=2,
    )
    halo_a, halo_b = pair_exchanges(send_a, send_b)
    (own,) = kernel_call(
        conv_own_body, "conv_own", [((cells, width), F32, "any")], stacked, matrix, mflops=1200
    )
    payload, conv = kernel_call(
        conv_finish_body, "conv_finish",
        [((frames, long, width), BF, "any"), ((frames, bins, width), F32, "vmem")],
        spectrum, halo_a, halo_b, own, borders, matrix, far=(0,),
        scratch=[tile, pieces, halo, halo], copies=1, mflops=200,
    )
    frame = exchange(payload, ("x", "core"))
    turned_shape = (width, cells + 2 * bins)
    turned, grad_att, slope = kernel_call(
        prepare_body, "prepare",
        [
            (turned_shape, BF, "hbm"), ((cells, wide), BF, "hbm"),
            ((frames, bins, width), F32, "hbm"),
        ],
        conv, spectrum, halo_a, halo_b, cotangent, out_weight, far=(1, 4, 5),
        scratch=[
            tile_f, tile, square, vmem((wide, width), BF), vmem(turned_shape, BF),
            vmem((cells, wide), BF), halo, halo,
        ],
        copies=6, mflops=300,
    )
    attended_v, cells_v = vmem((cells, wide), BF), vmem((cells, 3 * wide), BF)
    back, hidden, attended, grad_cells = kernel_call(
        attend_body, "attend",
        [
            ((frames, long, width), BF, "any"), ((cells, width), BF, "hbm"),
            ((cells, wide), BF, "hbm"), ((cells, 3 * wide), BF, "hbm"),
        ],
        frame, qkv_weight, grad_att, cotangent, far=(1, 2, 3),
        scratch=[
            vmem((width, 3 * wide), BF), attended_v, square, square, cells_v, attended_v, cells_v,
            vmem((HEAD, cells), F32), vmem((HEAD, cells), F32), pieces,
        ],
        copies=4 + 4 * HEADS, mflops=15000,
    )
    grads = exchange(back, ("x", "core"))
    ring = lax.axis_size("y") * lax.axis_size("x")
    early_shape = (ring, 8 * EARLY, 128)
    late_shape = (ring, 8 * (GROUPS - EARLY), 128)
    enhanced, theirs, mine, slope, turned = kernel_call(
        attend_rest_body, "attend_rest",
        [
            ((cells, width), BF, "any"), (early_shape, BF, "any"), (early_shape, BF, "hbm"),
            ((frames, bins, width), F32, "vmem"), (turned_shape, BF, "vmem"),
        ],
        hidden, attended, grad_cells, cotangent, out_weight, slope, turned,
        far=(0, 1, 2, 3, 4, 5, 6),
        scratch=[
            square, attended_v, cells_v, square, vmem((wide, width), BF), vmem(early_shape, BF),
            vmem((12, width, HEAD), F32), vmem((2, wide, HEAD), F32), vmem(early_shape, F32),
        ],
        copies=8, mflops=1500, limit=40,
    )
    theirs, grads = lax.optimization_barrier((theirs, grads))
    got = swap_cores(theirs)
    stacked_shape = (frames, bins, 3 * width)
    edges, theirs, late_mine, early, stacked, grad_tile = kernel_call(
        conv_weight_body, "conv_weight_grad",
        [
            ((2, 1, long, width), BF, "any"), (late_shape, BF, "any"), (late_shape, BF, "any"),
            (early_shape, BF, "any"), (stacked_shape, BF, "hbm"),
            ((frames, bins, width), BF, "hbm"),
        ],
        grads, slope, turned, mine, far=(3,),
        scratch=[
            vmem(stacked_shape, BF), tile,
            vmem((18 * (width // 2), width // 2), F32), vmem(late_shape, F32), pieces,
        ],
        copies=3, mflops=1200, limit=40,
    )
    late_got = swap_cores(theirs)
    edges, late_got = lax.optimization_barrier((edges, late_got))
    (message,) = kernel_call(
        join_body, "join", [((ring, 8 * GROUPS, 128), BF, "any")], early, got, late_mine,
        late_got,
    )
    late = exchange(message, ("y", "x"))
    total, matrix_back = kernel_call(
        conv_data_body, "conv_data",
        [((cells, width), F32, "vmem"), ((3, width, 3 * width), BF, "vmem")],
        grad_tile, stacked, conv_weight, far=(0, 1, 2),
        scratch=[tile, vmem(stacked_shape, BF), kernels], copies=3, mflops=1200,
    )
    edge_a, edge_b = pair_exchanges(edges[0], edges[1])
    late, total, edge_a, edge_b = lax.optimization_barrier((late, total, edge_a, edge_b))
    (chunk,) = kernel_call(
        regroup_body, "regroup", [((lax.axis_size("z"), 32, 128), BF, "any")],
        late,
        scratch=[vmem(late.shape[1:], F32), vmem((lax.axis_size("z"), 32, 128), F32)],
    )
    (grad_spectrum,) = kernel_call(
        conv_data_finish_body, "conv_data_finish", [((frames, bins, width), BF, "any")],
        total, edge_a, edge_b, matrix_back,
        scratch=[vmem((1, long, width), BF), vmem((1, long, width), BF)], mflops=100,
    )
    shares = kernel_call(
        share_body, "share", [((9, 128), F32, "any"), ((12, 128), F32, "any"), ((4, 128), F32, "any")],
        exchange(chunk, "z"),
        scratch=[vmem((32, 128), F32)],
    )
    return (enhanced.reshape(1, cells, width), grad_spectrum, *[s.reshape(-1) for s in shares])


def solution(mesh):
    mesh = Mesh(mesh.devices.reshape(8, 4, 4, 2), ("z", "y", "x", "core"))
    every = P(("z", "y", "x", "core"))
    tiles, rows = P(("z", "y"), ("x", "core"), None), P(("z", "y", "x", "core"), None, None)
    return jax.shard_map(
        shards,
        mesh=mesh,
        in_specs=(tiles, P(), P(), P(), rows),
        out_specs=(rows, tiles, every, every, every),
        check_vma=False,
    )
```

```python
import math

import jax
import jax.numpy as jnp
from jax import lax
from jax.experimental import pallas as pl
from jax.experimental.pallas import tpu as pltpu
from jax.sharding import Mesh
from jax.sharding import PartitionSpec as P

HEADS = 4
HEAD = 128
EXTRA = 16
SCALE = 1.0 / 512
LOG2E = math.log2(math.e)
FACTOR = 1.0 / math.sqrt(HEAD)
BF = jnp.bfloat16
F32 = jnp.float32
NN = (((1,), (0,)), ((), ()))
NT = (((1,), (1,)), ((), ()))
QUERY_BLOCK = 1024
GROUPS = 26
EARLY = 16


def mm(a, b, dims=NN):
    return lax.dot_general(a, b, dims, preferred_element_type=F32)


PLACES = {"any": jax.ShapeDtypeStruct, "hbm": pltpu.HBM, "vmem": pltpu.VMEM}


def kernel_call(body, name, outs, *args, far=(), scratch=(), copies=0, mflops=0, limit=48):
    shapes = [
        PLACES[away](dims, kind) for dims, kind, away in outs
    ]
    args = [
        pltpu.with_memory_space_constraint(a, pltpu.HBM) if n in far else a
        for n, a in enumerate(args)
    ]
    size = sum(math.prod(a.shape) * a.dtype.itemsize for a in (*args, *shapes))
    near, hbm = pl.BlockSpec(memory_space=pltpu.VMEM), pl.BlockSpec(memory_space=pltpu.HBM)
    scratch = list(scratch) + ([pltpu.SemaphoreType.DMA((copies,))] if copies else [])
    return pl.pallas_call(
        body,
        out_shape=shapes,
        in_specs=[hbm if n in far else near for n in range(len(args))],
        out_specs=[hbm if away == "hbm" else near for _, _, away in outs],
        scratch_shapes=scratch,
        compiler_params=pltpu.CompilerParams(vmem_limit_bytes=limit * 2**20),
        cost_estimate=pl.CostEstimate(
            flops=mflops * 10**6, bytes_accessed=size, transcendentals=0
        ),
        name=name,
    )(*args)


def copier(semaphores):
    started = []

    def start(source, target):
        copy = pltpu.make_async_copy(source, target, semaphores.at[len(started)])
        copy.start()
        started.append(copy)
        return copy

    return start


def sigmoid(v):
    return 1.0 / (1.0 + jnp.exp(-v))


def slope_of(v, sigma):
    return sigma * (1.0 + v * (1.0 - sigma))


def moved_down(rows):
    at = lax.broadcasted_iota(jnp.int32, rows.shape, 0)
    return jnp.where(at == 0, 0.0, pltpu.roll(rows, 1, 0))


def moved_up(rows):
    last = rows.shape[0] - 1
    at = lax.broadcasted_iota(jnp.int32, rows.shape, 0)
    return jnp.where(at == last, 0.0, pltpu.roll(rows, last, 0))


def with_borders(inner, first, last):
    at = lax.broadcasted_iota(jnp.int32, inner.shape, 1)
    inner = jnp.where(at == 0, first[:, None, :], inner)
    return jnp.where(at == inner.shape[1] - 1, last[:, None, :], inner)


def bins_before(rows, left):
    at = lax.broadcasted_iota(jnp.int32, rows.shape, 1)
    return jnp.where(at == 0, left, pltpu.roll(rows, 1, 1))


def bins_after(rows, right):
    last = rows.shape[1] - 1
    at = lax.broadcasted_iota(jnp.int32, rows.shape, 1)
    return jnp.where(at == last, right, pltpu.roll(rows, last, 1))


def sort_halos(even_down, odd_down, up, down):
    odd = lax.rem(lax.axis_index("y"), 2) == 1
    first, second = even_down[...], odd_down[...]
    up[...] = jnp.where(odd, first, second)
    down[...] = jnp.where(odd, second, first)


def conv_own_body(mid_far, weight_far, conv, borders, matrix, mid, weight, stacked, semaphores):
    start = copier(semaphores)
    load_weight, load_mid = start(weight_far, weight), start(mid_far, mid)
    frames, bins, width = mid.shape
    half = width // 2
    load_weight.wait()
    for i in range(3):
        for j in range(3):
            real, imag = weight[0, i, j], weight[1, i, j]
            at = j * width
            matrix[i, at : at + half, :half] = real
            matrix[i, at : at + half, half:] = imag
            matrix[i, at + half : at + width, :half] = -imag
            matrix[i, at + half : at + width, half:] = real
    load_mid.wait()
    wide = mid[...].astype(F32)
    stacked[:, :, :width] = bins_before(wide, 0.0).astype(BF)
    stacked[:, :, width : 2 * width] = mid[...]
    stacked[:, :, 2 * width :] = bins_after(wide, 0.0).astype(BF)
    inner = (frames - 1) * bins
    everything = stacked[...].reshape(frames * bins, 3 * width)
    conv[...] = mm(everything, matrix[1])
    conv[bins:] += mm(everything[:inner], matrix[0])
    conv[:inner] += mm(everything[bins:], matrix[2])
    borders[0] = mid[:, 0, :].astype(F32)
    borders[1] = mid[:, bins - 1, :].astype(F32)


def conv_finish_body(
    mid_far, even_down, odd_down, own, borders, matrix,
    payload, conv, mid, pieces, up, down, semaphores,
):
    start = copier(semaphores)
    load_mid = start(mid_far, mid)
    sort_halos(even_down, odd_down, up, down)
    frames, bins, width = mid.shape

    def stack(row):
        wide = row[...].astype(F32)
        before = bins_before(wide, 0.0).astype(BF)
        after = bins_after(wide, 0.0).astype(BF)
        return jnp.concatenate([before[0], row[0], after[0]], axis=1)

    conv[...] = own[...].reshape(frames, bins, width)
    conv[0] += mm(stack(up), matrix[0])
    conv[frames - 1] += mm(stack(down), matrix[2])

    def beyond(bin_at, side, tap):
        rows = jnp.concatenate(
            [up[:, bin_at, :].astype(F32), borders[side], down[:, bin_at, :].astype(F32)], axis=0
        )
        total = None
        for i in range(3):
            term = mm(
                rows[i : i + frames].astype(BF), matrix[i, tap * width : (tap + 1) * width, :]
            )
            total = term if total is None else total + term
        return total

    parts = (
        beyond(0, 0, 2),
        conv[:, 0, :],
        conv[:, bins - 1, :],
        beyond(bins - 1, 1, 0),
    )
    pieces[...] = jnp.zeros(pieces.shape, F32)
    for at, part in enumerate(parts):
        high = part.astype(BF).astype(F32)
        pieces[:, 2 * at, :] = high
        pieces[:, 2 * at + 1, :] = part - high
    values = conv[...]
    sigma = sigmoid(values)
    load_mid.wait()
    hidden = mid[...].astype(F32) + values * sigma
    payload[:, :bins, :] = with_borders(hidden, borders[0], borders[1]).astype(BF)
    payload[:, bins:, :] = pieces[...].astype(BF)


def prepare_body(
    conv, mid_far, even_down, odd_down, cotangent_far, out_w_far,
    turned_far, grad_att_far, slope_far,
    slope, mid, cotangent, out_w, turned, grad_att, up, down, semaphores,
):
    start = copier(semaphores)
    loads = start(mid_far, mid), start(cotangent_far, cotangent), start(out_w_far, out_w)
    sort_halos(even_down, odd_down, up, down)
    slope[...] = slope_of(conv[...], sigmoid(conv[...]))
    stores = [start(slope, slope_far)]
    for load in loads:
        load.wait()
    frames, bins, width = mid.shape
    turned[:, :bins] = up[0].T
    turned[:, bins : (frames + 1) * bins] = mid[...].reshape(frames * bins, width).T
    turned[:, (frames + 1) * bins :] = down[0].T
    grad_att[...] = mm(cotangent[...], out_w[...], NT).astype(BF)
    stores += [start(turned, turned_far), start(grad_att, grad_att_far)]
    for store in stores:
        store.wait()


def columns(part, h, heads=HEADS):
    at = (part * heads + h) * HEAD
    if not isinstance(h, int):
        at = pl.multiple_of(at, HEAD)
    return pl.ds(at, HEAD)


def one_head(h, heads, qkv, grad_att, attended, grad_cells, sum_keys, sum_values):
    def columns_of(part):
        return columns(part, h, heads)

    cells = qkv.shape[0]
    keys = qkv[:, columns_of(1)]
    values = qkv[:, columns_of(2)]
    values_ones = jnp.concatenate([values, jnp.ones((cells, HEAD), BF)], axis=1)
    for block in range(cells // QUERY_BLOCK):
        rows = slice(block * QUERY_BLOCK, (block + 1) * QUERY_BLOCK)
        queries = qkv[rows, columns_of(0)]
        scores = mm(queries, keys, NT)
        raised = jnp.exp2(scores - jnp.max(scores, axis=-1, keepdims=True))
        raised_b = raised.astype(BF)
        sums = mm(raised_b, values_ones)
        inverse = 1.0 / sums[:, HEAD:]
        result = sums[:, :HEAD] * inverse
        attended[rows, columns_of(0)] = result.astype(BF)
        scaled = grad_att[rows, columns_of(0)].astype(F32) * inverse
        inner = jnp.sum(scaled * result, axis=-1, keepdims=True)
        scaled_b = scaled.astype(BF)
        grad_probs = mm(scaled_b, values, NT)
        grad_scores = (raised * (grad_probs - inner)).astype(BF)
        grad_cells[rows, columns_of(0)] = (mm(grad_scores, keys) * FACTOR).astype(BF)
        new_keys = mm(queries.T, grad_scores)
        new_values = mm(scaled_b.T, raised_b)
        if block == 0:
            sum_keys[...] = new_keys
            sum_values[...] = new_values
        else:
            sum_keys[...] += new_keys
            sum_values[...] += new_values
    grad_cells[:, columns_of(1)] = (sum_keys[...] * (1.0 / LOG2E)).T.astype(BF)
    grad_cells[:, columns_of(2)] = sum_values[...].T.astype(BF)


def normed_parts(hidden_f):
    inv_rms = lax.rsqrt(jnp.mean(hidden_f * hidden_f, axis=-1, keepdims=True) + 1e-6)
    normed_f = hidden_f * inv_rms
    return inv_rms, normed_f, normed_f.astype(BF)


def split_columns(target, at, values):
    for n in range(values.shape[1] // 128):
        target[at + n] = values[:, n * 128 : (n + 1) * 128]


def attend_body(
    came, qkv_w_far, grad_att_far, cotangent_far,
    payload, hidden_far, attended_far, grad_cells_far,
    qkv_w, grad_att, cotangent, hidden, qkv, attended, grad_cells,
    sum_keys, sum_values, pieces, semaphores,
):
    start = copier(semaphores)
    load_qkv_w = start(qkv_w_far, qkv_w)
    load_grad_att = start(grad_att_far, grad_att)
    load_cotangent = start(cotangent_far, cotangent)
    chunks, long, width = came.shape
    bins = long - EXTRA
    wide = HEADS * HEAD
    pieces[...] = came[:, bins:, :].astype(F32)
    here_first = pieces[:, 2, :] + pieces[:, 3, :]
    here_last = pieces[:, 4, :] + pieces[:, 5, :]
    first = here_first + moved_down(pieces[:, 6, :] + pieces[:, 7, :])
    last = here_last + moved_up(pieces[:, 0, :] + pieces[:, 1, :])
    sigma_first, sigma_last = sigmoid(first), sigmoid(last)
    fixed_first = came[:, 0, :].astype(F32) + first * sigma_first
    fixed_last = came[:, bins - 1, :].astype(F32) + last * sigma_last
    cells = with_borders(came[:, :bins, :].astype(F32), fixed_first, fixed_last)
    hidden[...] = cells.astype(BF).reshape(chunks * bins, width)
    stores = [start(hidden, hidden_far)]
    _, _, normed = normed_parts(hidden[...].astype(F32))
    load_qkv_w.wait()
    qkv[:, :wide] = (mm(normed, qkv_w[:, :wide]) * (FACTOR * LOG2E)).astype(BF)
    qkv[:, wide:] = mm(normed, qkv_w[:, wide:]).astype(BF)
    load_grad_att.wait()

    def head(h, carry):
        one_head(h, HEADS, qkv, grad_att, attended, grad_cells, sum_keys, sum_values)
        return carry

    lax.fori_loop(0, HEADS, head, 0)
    stores += [start(grad_cells, grad_cells_far), start(attended, attended_far)]
    load_cotangent.wait()
    inv_rms, normed_f, _ = normed_parts(hidden[...].astype(F32))
    grad_normed = mm(grad_cells[...], qkv_w[...], NT)
    mixing = jnp.mean(grad_normed * normed_f, axis=-1, keepdims=True)
    grad = cotangent[...].astype(F32) + inv_rms * (grad_normed - normed_f * mixing)
    grad_b = grad.astype(BF).reshape(chunks, bins, width)
    payload[:, :bins, :] = grad_b
    grad_first = payload[:, 0, :].astype(F32) * slope_of(first, sigma_first)
    grad_last = payload[:, bins - 1, :].astype(F32) * slope_of(last, sigma_last)
    pieces[...] = jnp.zeros(pieces.shape, F32)
    pieces[:, 0, :] = moved_down(grad_last)
    pieces[:, 1, :] = grad_first
    pieces[:, 2, :] = grad_last
    pieces[:, 3, :] = moved_up(grad_first)
    payload[:, bins:, :] = pieces[...].astype(BF)
    for store in stores:
        store.wait()


def deal(rows, core, groups):
    for n in range(rows.shape[0]):
        for e, (source, per, at) in enumerate(groups):
            begin = per * (2 * n + core) + at
            rows[n, 8 * e : 8 * e + 8, :] = source[pl.ds(begin, 8, stride=32 * per), :]


def attend_rest_body(
    hidden_far, attended_far, grad_cells_far, cotangent_far, out_w_far, slope_far, turned_far,
    enhanced, theirs, mine_far, slope, turned,
    hidden, attended, grad_cells, cotangent, out_w, mine, grads, grads_out, rows, semaphores,
):
    start = copier(semaphores)
    load_hidden, load_cells = start(hidden_far, hidden), start(grad_cells_far, grad_cells)
    loads = [
        start(attended_far, attended), start(cotangent_far, cotangent), start(out_w_far, out_w)
    ]
    ahead = [start(slope_far, slope), start(turned_far, turned)]
    load_hidden.wait()
    hidden_f = hidden[...].astype(F32)
    _, _, normed = normed_parts(hidden_f)
    load_cells.wait()
    split_columns(grads, 0, SCALE * mm(normed.T, grad_cells[...]))
    for load in loads:
        load.wait()
    split_columns(grads_out, 0, SCALE * mm(attended[...].T, cotangent[...]))
    groups = [(grads.at[n], 1, 0) for n in range(12)]
    groups += [(grads_out.at[n % 2], 2, n // 2) for n in range(4)]
    core = lax.axis_index("core")
    deal(rows, 1 - core, groups)
    theirs[...] = rows[...].astype(BF)
    deal(rows, core, groups)
    mine[...] = rows[...].astype(BF)
    store = start(mine, mine_far)
    enhanced[...] = (hidden_f + mm(attended[...], out_w[...])).astype(BF)
    for copy in ahead:
        copy.wait()
    store.wait()


def stack_back(rows, left, right):
    after = bins_after(rows, right).astype(BF)
    before = bins_before(rows, left).astype(BF)
    return jnp.concatenate([after, rows.astype(BF), before], axis=-1)


def conv_weight_body(
    came, slope, turned, early_far, edges, theirs, mine, early, stacked_far, grad_far,
    stacked, own, grads, rows, pieces, semaphores,
):
    start = copier(semaphores)
    load_early = start(early_far, early)
    frames, long, width = came.shape
    bins = long - EXTRA
    half = width // 2
    cells = frames * bins
    pieces[...] = came[:, bins:, :].astype(F32)
    own[...] = came[:, :bins, :]
    stores = [start(own, grad_far)]
    grad = own[...].astype(F32) * slope[...]
    grad = with_borders(grad, pieces[:, 1, :], pieces[:, 2, :])
    grad_b = grad.astype(BF)
    odd = lax.rem(lax.axis_index("y"), 2) == 1
    ends = []
    for frame in (0, frames - 1):
        ends.append(
            jnp.concatenate([grad_b[frame : frame + 1], came[frame : frame + 1, bins:, :]], axis=1)
        )
    edges[0] = jnp.where(odd, ends[0], ends[1])
    edges[1] = jnp.where(odd, ends[1], ends[0])
    stacked[...] = stack_back(
        grad_b.astype(F32), pieces[:, 0, :][:, None, :], pieces[:, 3, :][:, None, :]
    )
    stores.append(start(stacked, stacked_far))
    flat = stacked[...].reshape(cells, 3 * width)
    for i in range(3):
        block = mm(turned[:, i * bins : i * bins + cells], flat)
        for j in range(3):
            at = j * width
            upper = block[:half, at : at + half] + block[half:, at + half : at + width]
            lower = block[:half, at + half : at + width] - block[half:, at : at + half]
            tap = (3 * i + j) * half
            grads[tap : tap + half] = upper * SCALE
            grads[9 * half + tap : 9 * half + tap + half] = lower * SCALE
    core = lax.axis_index("core")
    groups = [(grads, 9, e) for e in range(9)]
    rows[:, 72:, :] = jnp.zeros((rows.shape[0], 8, 128), F32)
    deal(rows, 1 - core, groups)
    theirs[...] = rows[...].astype(BF)
    deal(rows, core, groups)
    mine[...] = rows[...].astype(BF)
    load_early.wait()
    for store in stores:
        store.wait()


def conv_data_body(
    grad_far, stacked_far, weight_far, total, matrix, grad, stacked, weight, semaphores
):
    start = copier(semaphores)
    load_weight, load_stacked = start(weight_far, weight), start(stacked_far, stacked)
    load_grad = start(grad_far, grad)
    frames, bins, triple = stacked.shape
    width = triple // 3
    half = width // 2
    load_weight.wait()
    for i in range(3):
        for j in range(3):
            real, imag = weight[0, i, j], weight[1, i, j]
            at = j * width
            matrix[i, :half, at : at + half] = real
            matrix[i, :half, at + half : at + width] = imag
            matrix[i, half:, at : at + half] = -imag
            matrix[i, half:, at + half : at + width] = real
    load_stacked.wait()
    load_grad.wait()
    inner = (frames - 1) * bins
    flat = stacked[...].reshape(frames * bins, triple)
    total[...] = grad[...].reshape(frames * bins, width).astype(F32) + mm(flat, matrix[1], NT)
    total[:inner] += mm(flat[bins:], matrix[0], NT)
    total[bins:] += mm(flat[:inner], matrix[2], NT)


def conv_data_finish_body(total, even_down, odd_down, matrix, out, up, down):
    sort_halos(even_down, odd_down, up, down)
    frames, bins, width = out.shape

    def stack(edge):
        extra = edge[:, bins:, :].astype(F32)
        rows = edge[:, :bins, :].astype(F32)
        return stack_back(rows, extra[:, 0:1, :], extra[:, 3:4, :])[0]

    out[...] = total[...].reshape(frames, bins, width).astype(BF)
    out[0] = (total[:bins] + mm(stack(up), matrix[2], NT)).astype(BF)
    out[frames - 1] = (total[(frames - 1) * bins :] + mm(stack(down), matrix[0], NT)).astype(BF)


def sum_body(came, out):
    total = came[0].astype(F32)
    for source in range(1, came.shape[0]):
        total = total + came[source].astype(F32)
    out[...] = total


def join_body(early, early_got, mine, got, message):
    cut = early.shape[1]
    message[:, :cut, :] = (early[...].astype(F32) + early_got[...].astype(F32)).astype(BF)
    message[:, cut:, :] = (mine[...].astype(F32) + got[...].astype(F32)).astype(BF)


def regroup_body(came, chunk, total, rows):
    sum_body(came, total)
    rows[...] = jnp.zeros(rows.shape, F32)
    for z in range(chunk.shape[0]):
        rows[z, 0:GROUPS, :] = total[pl.ds(z, GROUPS, stride=8), :]
    chunk[...] = rows[...].astype(BF)


def share_body(came, conv, qkv, out, total):
    sum_body(came, total)
    qkv[...] = total[0:12]
    out[...] = total[12:16]
    conv[...] = total[16:25]


def pair_exchanges(first, second):
    size = lax.axis_size("z") * lax.axis_size("y")
    near = [(i, i ^ 1) for i in range(size)]
    apart = [(i, i + 1 if i % 2 else i - 1) for i in range(1, size - 1)]
    return lax.ppermute(first, ("z", "y"), near), lax.ppermute(second, ("z", "y"), apart)


def exchange(array, axis):
    return lax.all_to_all(array, axis, split_axis=0, concat_axis=0, tiled=True)


def swap_cores(array):
    return lax.ppermute(array, "core", [(0, 1), (1, 0)])


def shards(spectrum, conv_weight, qkv_weight, out_weight, cotangent):
    frames, bins, width = spectrum.shape
    cells = frames * bins
    wide = HEADS * HEAD
    long = bins + EXTRA
    vmem = pltpu.VMEM
    cotangent = cotangent.reshape(cells, width)
    odd = lax.rem(lax.axis_index("y"), 2) == 1
    first, last = spectrum[:1], spectrum[frames - 1 :]
    halo_a, halo_b = pair_exchanges(jnp.where(odd, first, last), jnp.where(odd, last, first))
    tile = vmem((frames, bins, width), BF)
    tile_f = vmem((frames, bins, width), F32)
    pieces = vmem((frames, EXTRA, width), F32)
    square = vmem((cells, width), BF)
    kernels = vmem(conv_weight.shape, BF)
    halo = vmem((1, bins, width), BF)
    own, borders, matrix = kernel_call(
        conv_own_body, "conv_own",
        [
            ((cells, width), F32, "any"), ((2, frames, width), F32, "any"),
            ((3, 3 * width, width), BF, "any"),
        ],
        spectrum, conv_weight, far=(0, 1),
        scratch=[tile, kernels, vmem((frames, bins, 3 * width), BF)], copies=2, mflops=1200,
    )
    payload, conv = kernel_call(
        conv_finish_body, "conv_finish",
        [((frames, long, width), BF, "any"), ((frames, bins, width), F32, "vmem")],
        spectrum, halo_a, halo_b, own, borders, matrix, far=(0,),
        scratch=[tile, pieces, halo, halo], copies=1, mflops=200,
    )
    frame = exchange(payload, ("x", "core"))
    turned_shape = (width, cells + 2 * bins)
    turned, grad_att, slope = kernel_call(
        prepare_body, "prepare",
        [
            (turned_shape, BF, "hbm"), ((cells, wide), BF, "hbm"),
            ((frames, bins, width), F32, "hbm"),
        ],
        conv, spectrum, halo_a, halo_b, cotangent, out_weight, far=(1, 4, 5),
        scratch=[
            tile_f, tile, square, vmem((wide, width), BF), vmem(turned_shape, BF),
            vmem((cells, wide), BF), halo, halo,
        ],
        copies=6, mflops=300,
    )
    attended_v, cells_v = vmem((cells, wide), BF), vmem((cells, 3 * wide), BF)
    back, hidden, attended, grad_cells = kernel_call(
        attend_body, "attend",
        [
            ((frames, long, width), BF, "any"), ((cells, width), BF, "hbm"),
            ((cells, wide), BF, "hbm"), ((cells, 3 * wide), BF, "hbm"),
        ],
        frame, qkv_weight, grad_att, cotangent, far=(1, 2, 3),
        scratch=[
            vmem((width, 3 * wide), BF), attended_v, square, square, cells_v, attended_v, cells_v,
            vmem((HEAD, cells), F32), vmem((HEAD, cells), F32), pieces,
        ],
        copies=6, mflops=15000,
    )
    grads = exchange(back, ("x", "core"))
    ring = lax.axis_size("y") * lax.axis_size("x")
    early_shape = (ring, 8 * EARLY, 128)
    late_shape = (ring, 8 * (GROUPS - EARLY), 128)
    enhanced, theirs, mine, slope, turned = kernel_call(
        attend_rest_body, "attend_rest",
        [
            ((cells, width), BF, "any"), (early_shape, BF, "any"), (early_shape, BF, "hbm"),
            ((frames, bins, width), F32, "vmem"), (turned_shape, BF, "vmem"),
        ],
        hidden, attended, grad_cells, cotangent, out_weight, slope, turned,
        far=(0, 1, 2, 3, 4, 5, 6),
        scratch=[
            square, attended_v, cells_v, square, vmem((wide, width), BF), vmem(early_shape, BF),
            vmem((12, width, HEAD), F32), vmem((2, wide, HEAD), F32), vmem(early_shape, F32),
        ],
        copies=8, mflops=1500, limit=40,
    )
    theirs, grads = lax.optimization_barrier((theirs, grads))
    got = swap_cores(theirs)
    stacked_shape = (frames, bins, 3 * width)
    edges, theirs, late_mine, early, stacked, grad_tile = kernel_call(
        conv_weight_body, "conv_weight_grad",
        [
            ((2, 1, long, width), BF, "any"), (late_shape, BF, "any"), (late_shape, BF, "any"),
            (early_shape, BF, "any"), (stacked_shape, BF, "hbm"),
            ((frames, bins, width), BF, "hbm"),
        ],
        grads, slope, turned, mine, far=(3,),
        scratch=[
            vmem(stacked_shape, BF), tile,
            vmem((18 * (width // 2), width // 2), F32), vmem(late_shape, F32), pieces,
        ],
        copies=3, mflops=1200, limit=40,
    )
    late_got = swap_cores(theirs)
    edges, late_got = lax.optimization_barrier((edges, late_got))
    (message,) = kernel_call(
        join_body, "join", [((ring, 8 * GROUPS, 128), BF, "any")], early, got, late_mine,
        late_got,
    )
    late = exchange(message, ("y", "x"))
    total, matrix_back = kernel_call(
        conv_data_body, "conv_data",
        [((cells, width), F32, "any"), ((3, width, 3 * width), BF, "any")],
        grad_tile, stacked, conv_weight, far=(0, 1, 2),
        scratch=[tile, vmem(stacked_shape, BF), kernels], copies=3, mflops=1200,
    )
    edge_a, edge_b = pair_exchanges(edges[0], edges[1])
    (grad_spectrum,) = kernel_call(
        conv_data_finish_body, "conv_data_finish", [((frames, bins, width), BF, "any")],
        total, edge_a, edge_b, matrix_back,
        scratch=[vmem((1, long, width), BF), vmem((1, long, width), BF)], mflops=100,
    )
    late, grad_spectrum = lax.optimization_barrier((late, grad_spectrum))
    (chunk,) = kernel_call(
        regroup_body, "regroup", [((lax.axis_size("z"), 32, 128), BF, "any")],
        late,
        scratch=[vmem(late.shape[1:], F32), vmem((lax.axis_size("z"), 32, 128), F32)],
    )
    shares = kernel_call(
        share_body, "share", [((9, 128), F32, "any"), ((12, 128), F32, "any"), ((4, 128), F32, "any")],
        exchange(chunk, "z"),
        scratch=[vmem((32, 128), F32)],
    )
    return (enhanced.reshape(1, cells, width), grad_spectrum, *[s.reshape(-1) for s in shares])


def solution(mesh):
    mesh = Mesh(mesh.devices.reshape(8, 4, 4, 2), ("z", "y", "x", "core"))
    every = P(("z", "y", "x", "core"))
    tiles, rows = P(("z", "y"), ("x", "core"), None), P(("z", "y", "x", "core"), None, None)
    return jax.shard_map(
        shards,
        mesh=mesh,
        in_specs=(tiles, P(), P(), P(), rows),
        out_specs=(rows, tiles, every, every, every),
        check_vma=False,
    )
```
